512 devices in a mesh: lat: 16 (over z_hi, x), lon: 32 (over z_lo, y, core).
Axes of the slice: x: 4, y: 8, z: 8 (z_hi: 4, z_lo: 2; z = z_hi * 2 + z_lo), core: 2. Of those that a mesh axis runs over, the one named last changes fastest.
Arguments:
- feats: bfloat16 [2, 128, 1024, 128], P(None, 'lat', 'lon'), may hold values from -41 to 41
- cond: bfloat16 [2, 128, 1024, 128], P(None, 'lat', 'lon'), may hold values from -6 to 6
- null_field: bfloat16 [128, 1024, 128], P('lat', 'lon'), may hold values from -6 to 6
- drop_flags: int32 [2, 128], replicated, may hold values from 0 to 1, as said below
- emb: float32 [2, 512], replicated, may hold values from -5 to 5
- style_weight: float32 [512, 128], replicated, may hold values from -0.044194173 to 0.044194173
- conv_weight: float32 [3, 3, 128, 128], replicated, may hold values from -0.1875 to 0.1875
- gamma: float32 [128], replicated, may hold values from 0.1 to 1.9
- beta: float32 [128], replicated, may hold values from -3 to 3
- cotangent: bfloat16 [2, 128, 1024, 128], P(None, 'lat', 'lon'), may hold values from -6 to 6
Outputs:
- block_out: bfloat16 [2, 128, 1024, 128], P(None, 'lat', 'lon')
- grad_feats: bfloat16 [2, 128, 1024, 128], P(None, 'lat', 'lon')
- grad_weight: float32 [3, 3, 128, 128], replicated
- grad_style: float32 [512, 128], replicated
- gamma_gradient: float32 [128], replicated
- grad_beta: float32 [128], replicated
The draws below stay inside these ranges and needn't reach their ends.
Inputs may be any that keep to these rules, and one draw needn't show every extreme that they name: `drop_flags`: each sample drops exactly 64 of its channels.
All inputs are finite; a program needn't handle non-finite values.
Results may differ from the reference program's by a relative error of at most 0.0056.
Values may be sent and summed in bfloat16 or wider, within the bound.
No kernel may reach another device: no remote copies, remote signals or barrier semaphores. Data moves between devices by JAX's collectives and lax.ppermute only.
A program may use at most 64 MiB of HBM per device.

```python
import math
import jax
import jax.numpy as jnp
from jax import lax

C = 128
E = 512
GROUPS = 32
B = 2
NH = 128
NW = 1024


def draw_feats(key, part):
    key = jax.random.fold_in(key, 11)
    key_base, key_chan = jax.random.split(key, 2)
    lat_frac = (jnp.arange(NH, dtype=jnp.float32) + 0.5) / NH
    lon_frac = (jnp.arange(NW, dtype=jnp.float32) + 0.5) / NW
    cell_scale = (0.5 + lat_frac)[:, None] * (0.5 + lon_frac)[None, :]
    chan_scale = jnp.exp(jax.random.uniform(key_chan, (C,), jnp.float32, math.log(0.3), math.log(3.0)))
    base = jnp.clip(jax.random.normal(key_base, (B, NH, NW, C), jnp.float32), -6.0, 6.0)
    values = base * cell_scale[None, :, :, None] * chan_scale
    return jnp.clip(values, -41.0, 41.0).astype(jnp.bfloat16)


def one_sample_flags(sample_key):
    order = jax.random.permutation(sample_key, C)
    return (order < C // 2).astype(jnp.int32)


def draw_drop_flags(key, part):
    key = jax.random.fold_in(key, 23)
    sample_keys = jax.random.split(key, B)
    return jax.vmap(one_sample_flags)(sample_keys).astype(jnp.int32)


def steps_of(key, extent, pieces, low, high):
    def one(axis_at, parts):
        heights = jax.random.uniform(jax.random.fold_in(jax.random.fold_in(key, 6), axis_at), (parts,), jnp.float32, low / len(pieces), high / len(pieces))
        return jnp.repeat(jnp.exp(heights), extent[axis_at] // parts).reshape((-1,) + (1,) * (len(extent) - axis_at - 1))

    loudness = one(*pieces[0])
    for cut in pieces[1:]:
        loudness = loudness * one(*cut)
    return loudness


def scatter_about(rng, dims, scale, most, cuts=(), kind=jnp.bfloat16):
    values = scale * jax.random.normal(rng, dims, jnp.float32)
    if cuts:
        values = values * steps_of(rng, dims, cuts, -0.22, 0.18)
    return jnp.clip(values, -most, most).astype(kind)


def setup_inputs(seed: int = 0) -> dict:
    streams_of = jax.random.split(jax.random.key(seed), 11)
    feats = draw_feats(jax.random.fold_in(streams_of[10], 71), 0)
    cond = scatter_about(streams_of[1], (B, NH, NW, C), 1.0, 6.0, ((1, 16), (2, 32)))
    null_field = scatter_about(streams_of[2], (NH, NW, C), 1.0, 6.0, ((0, 16), (1, 32)))
    drop_flags = draw_drop_flags(jax.random.fold_in(streams_of[10], 71), 0)
    emb = scatter_about(streams_of[4], (B, E), 1.0, 5.0, (), jnp.float32)
    style_weight = scatter_about(streams_of[5], (E, C), (0.3 / E ** 0.5), 0.044194173, (), jnp.float32)
    conv_weight = scatter_about(streams_of[6], (3, 3, C, C), (9 * C) ** -0.5, 0.1875, (), jnp.float32)
    gamma = jnp.clip(1.0 + 0.18 * jax.random.normal(streams_of[7], (C,), jnp.float32), 0.1, 1.9)
    beta = scatter_about(streams_of[8], (C,), 0.5, 3.0, (), jnp.float32)
    cotangent = scatter_about(streams_of[9], (B, NH, NW, C), 1.0, 6.0, ((1, 16), (2, 32)))
    return {"feats": feats, "cond": cond, "null_field": null_field, "drop_flags": drop_flags, "emb": emb, "style_weight": style_weight, "conv_weight": conv_weight, "gamma": gamma, "beta": beta, "cotangent": cotangent}


def modulate(conv_weight, style_weight, emb):
    style_scale = 1.0 + jnp.dot(emb, style_weight, precision=lax.Precision.HIGHEST)
    modded = conv_weight[None] * style_scale[:, None, None, :, None]
    demod = lax.rsqrt(lax.optimization_barrier(jnp.sum(modded * modded, axis=(1, 2, 3))) + 1e-08)
    return modded * demod[:, None, None, None, :]

def pad_grid(field):
    wrapped = jnp.concatenate([field[:, -1:], field, field[:, :1]], axis=1)
    border = jnp.zeros((1, wrapped.shape[1], wrapped.shape[2]), field.dtype)
    return jnp.concatenate([border, wrapped, border], axis=0)

def apply_taps(padded, taps):
    height = padded.shape[0] - 2
    width = padded.shape[1] - 2
    total = jnp.zeros((height * width, taps.shape[3]), jnp.float32)
    for row_tap in range(3):
        for col_tap in range(3):
            window = padded[row_tap:row_tap + height, col_tap:col_tap + width].reshape(height * width, -1)
            total = total + jnp.dot(window, taps[row_tap, col_tap], preferred_element_type=jnp.float32)
    return total.reshape(height, width, -1)

def filter_grad(padded, cotan):
    height, width, channels = cotan.shape
    flat_cot = cotan.reshape(height * width, channels)
    rows_out = []
    for row_tap in range(3):
        cols_out = []
        for col_tap in range(3):
            window = padded[row_tap:row_tap + height, col_tap:col_tap + width].reshape(height * width, channels)
            cols_out.append(jnp.dot(window.T, flat_cot, preferred_element_type=jnp.float32))
        rows_out.append(jnp.stack(cols_out))
    return jnp.stack(rows_out)

def reference(feats, cond, null_field, drop_flags, emb, style_weight, conv_weight, gamma, beta, cotangent):
    channels = feats.shape[3]
    group_size = channels // GROUPS
    cells_per_group = NH * NW * group_size
    scale_gradient = 1.0 / math.sqrt(B * NH * NW)
    dropped = drop_flags.astype(jnp.float32)[:, None, None, :]
    mixed = (feats.astype(jnp.float32) + dropped * null_field.astype(jnp.float32)[None] + (1.0 - dropped) * cond.astype(jnp.float32)).astype(jnp.bfloat16)
    mixed32 = mixed.astype(jnp.float32)

    def group_count_total(values):
        return lax.optimization_barrier(jnp.sum(values, axis=(1, 2))).reshape(B, GROUPS, group_size).sum(-1)

    def expand_groups(stat):
        return jnp.repeat(stat, group_size, axis=1)[:, None, None, :]
    group_mean = group_count_total(mixed32) / cells_per_group
    centered_input = mixed32 - expand_groups(group_mean)
    group_var = group_count_total(centered_input * centered_input) / cells_per_group
    inverse_deviation = expand_groups(lax.rsqrt(group_var + 1e-05))
    normalized_input = centered_input * inverse_deviation
    preactivation = normalized_input * gamma + beta
    act = jax.nn.silu(preactivation).astype(jnp.bfloat16)
    w_eff = modulate(conv_weight, style_weight, emb).astype(jnp.bfloat16)
    outputs = []
    grad_acts = []
    grad_effs = []
    for sample in range(B):
        act_pad = pad_grid(act[sample])
        cot_pad = pad_grid(cotangent[sample])
        conv_out = apply_taps(act_pad, w_eff[sample])
        outputs.append((mixed32[sample] + conv_out).astype(jnp.bfloat16))
        back_taps = jnp.swapaxes(w_eff[sample, ::-1, ::-1], 2, 3)
        grad_acts.append(apply_taps(cot_pad, back_taps))
        grad_effs.append(filter_grad(act_pad, cotangent[sample]))
    block_out = jnp.stack(outputs)
    grad_act = jnp.stack(grad_acts)
    grad_eff = jnp.stack(grad_effs)
    sig = jax.nn.sigmoid(preactivation)
    preactivation_gradient = grad_act * sig * (1.0 + preactivation * (1.0 - sig))
    gamma_gradient = scale_gradient * lax.optimization_barrier(jnp.sum(preactivation_gradient * normalized_input, axis=(0, 1, 2)))
    grad_beta = scale_gradient * lax.optimization_barrier(jnp.sum(preactivation_gradient, axis=(0, 1, 2)))
    normalized_gradient = preactivation_gradient * gamma
    product_mean = group_count_total(normalized_gradient) / cells_per_group
    squared_mean = group_count_total(normalized_gradient * normalized_input) / cells_per_group
    mixed_gradient = inverse_deviation * (normalized_gradient - expand_groups(product_mean) - normalized_input * expand_groups(squared_mean))
    grad_feats = (cotangent.astype(jnp.float32) + mixed_gradient).astype(jnp.bfloat16)
    _, pullback = jax.vjp(lambda weight, style: modulate(weight, style, emb), conv_weight, style_weight)
    weight_part, style_part = pullback(grad_eff)
    return (block_out, grad_feats, scale_gradient * weight_part, scale_gradient * style_part, gamma_gradient, grad_beta)
```

```python
import math

import jax
import jax.numpy as jnp
from jax import lax
from jax.sharding import Mesh, PartitionSpec as P

GROUPS = 32
LAT = ("zh", "x")
LON = ("zl", "y", "c")
PLANE = ("x", "y")
COLUMN = ("zh", "zl")
F32 = jnp.float32
BF16 = jnp.bfloat16


def shift(block, axes, step, periodic):
    count = lax.axis_size(axes)
    pairs = [(i, i + step) for i in range(count)]
    if periodic:
        pairs = [(source, target % count) for source, target in pairs]
    else:
        pairs = [(source, target) for source, target in pairs if 0 <= target < count]
    return lax.ppermute(block, axes, pairs)


def extend(block, axes, dim, periodic):
    last = block.shape[dim] - 1
    low = shift(lax.slice_in_dim(block, last, last + 1, axis=dim), axes, 1, periodic)
    high = shift(lax.slice_in_dim(block, 0, 1, axis=dim), axes, -1, periodic)
    return jnp.concatenate([low, block, high], axis=dim)


def everyone(row, axes):
    count = lax.axis_size(axes)
    return lax.all_to_all(jnp.broadcast_to(row[None], (count,) + row.shape), axes, 0, 0)


def merge_moments(rows, count):
    mean = jnp.mean(rows[:, :1], axis=0)
    away = rows[:, :1] - mean
    spread = jnp.sum(rows[:, 1:] + count * away * away, axis=0)
    return jnp.concatenate([mean, spread], axis=0)


def two_terms(values):
    high = values.astype(BF16)
    return high, (values - high.astype(F32)).astype(BF16)


def apply_taps(padded, taps, tile_rows, tile_cols):
    total = jnp.zeros(padded.shape[:1] + (tile_rows, tile_cols, taps.shape[4]), F32)
    for row_tap in range(3):
        for col_tap in range(3):
            window = padded[:, row_tap : row_tap + tile_rows, col_tap : col_tap + tile_cols]
            total = total + jnp.einsum(
                "bhwi,bio->bhwo", window, taps[:, row_tap, col_tap], preferred_element_type=F32
            )
    return total


def on_device(
    feats, cond, null_field, drop_flags, emb, style_weight, conv_weight, gamma, beta, cotangent
):
    samples, tile_rows, tile_cols, channels = feats.shape
    group_size = channels // GROUPS
    lat_count, lon_count = lax.axis_size(LAT), lax.axis_size(LON)
    devices_all = lat_count * lon_count
    cells_local = tile_rows * tile_cols * group_size
    cells_per_group = cells_local * devices_all
    scale_gradient = 1.0 / math.sqrt(samples * tile_rows * tile_cols * devices_all)

    def group_total(values):
        return jnp.sum(values, axis=(1, 2)).reshape(samples, GROUPS, group_size).sum(-1)

    def expand(stat):
        return jnp.repeat(stat, group_size, axis=1)[:, None, None, :]

    dropped = drop_flags.astype(F32)[:, None, None, :]
    mixed = (
        feats.astype(F32)
        + dropped * null_field.astype(F32)[None]
        + (1.0 - dropped) * cond.astype(F32)
    ).astype(BF16)
    mixed32 = mixed.astype(F32)
    local_mean = group_total(mixed32) / cells_local
    away = mixed32 - expand(local_mean)
    local_spread = group_total(away * away)
    moments = jnp.stack([local_mean.reshape(-1), local_spread.reshape(-1)])
    moments = merge_moments(everyone(moments, LON), cells_local)
    moments = merge_moments(everyone(moments, LAT), cells_local * lon_count)
    group_mean = moments[0].reshape(samples, GROUPS)
    group_var = moments[1].reshape(samples, GROUPS) / cells_per_group

    both = jnp.stack([mixed, cotangent])
    both = extend(both, LON, 3, True)
    both = extend(both, LAT, 2, False)
    mixed_pad, cot_pad = both[0], both[1]

    style = 1.0 + jnp.dot(emb, style_weight, precision=lax.Precision.HIGHEST)
    power = jnp.sum(conv_weight * conv_weight, axis=(0, 1))
    demod = lax.rsqrt(jnp.dot(style * style, power, precision=lax.Precision.HIGHEST) + 1e-08)
    modded = conv_weight[None] * style[:, None, None, :, None]
    w_eff = (modded * demod[:, None, None, None, :]).astype(BF16)
    back_taps = jnp.swapaxes(w_eff[:, ::-1, ::-1], 3, 4)
    grad_act = apply_taps(cot_pad, back_taps, tile_rows, tile_cols)

    inverse_deviation = expand(lax.rsqrt(group_var + 1e-05))
    mean_all = expand(group_mean)

    def normalize(values):
        return (values.astype(F32) - mean_all) * inverse_deviation

    lat_at = lax.axis_index(LAT)
    row_at = jnp.arange(tile_rows + 2) + lat_at * tile_rows - 1
    inside = ((row_at >= 0) & (row_at < lat_count * tile_rows))[None, :, None, None]
    act_pad = jax.nn.silu(normalize(mixed_pad) * gamma + beta)
    act_pad = jnp.where(inside, act_pad, 0.0).astype(BF16)
    conv_out = apply_taps(act_pad, w_eff, tile_rows, tile_cols)
    block_out = (mixed32 + conv_out).astype(BF16)

    blocks = []
    for row_tap in range(3):
        for col_tap in range(3):
            window = act_pad[:, row_tap : row_tap + tile_rows, col_tap : col_tap + tile_cols]
            blocks.append(jnp.einsum("bhwi,bhwo->bio", window, cotangent, preferred_element_type=F32))
    local_eff = jnp.stack(blocks, axis=1)
    flat_weight = conv_weight.reshape((9, channels, channels))
    scaled = local_eff * demod[:, None, None, :]
    local_weight = jnp.sum(scaled * style[:, None, :, None], axis=0)
    local_style = jnp.sum(scaled * flat_weight[None], axis=(1, 3))
    local_demod = jnp.sum(local_eff * (flat_weight[None] * style[:, None, :, None]), axis=(1, 2))

    normalized = normalize(mixed)
    preactivation = normalized * gamma + beta
    sig = jax.nn.sigmoid(preactivation)
    grad_pre = grad_act * sig * (1.0 + preactivation * (1.0 - sig))
    local_gamma = jnp.sum(grad_pre * normalized, axis=(0, 1, 2))
    local_beta = jnp.sum(grad_pre, axis=(0, 1, 2))
    normalized_gradient = grad_pre * gamma
    local_p = group_total(normalized_gradient)
    local_q = group_total(normalized_gradient * normalized)

    small = jnp.concatenate(
        [
            local_demod.reshape(-1),
            local_style.reshape(-1),
            local_gamma,
            local_beta,
            local_p.reshape(-1),
            local_q.reshape(-1),
        ]
    )
    core_count, plane_count = lax.axis_size("c"), lax.axis_size(PLANE)
    parts = core_count * plane_count
    each = -(-small.shape[0] // parts)
    rows = 9 * channels // parts

    def pack(weight_rows, values):
        room = [(0, 0)] * (values.ndim - 1) + [(0, channels // 2 - each)]
        high, low = two_terms(values)
        extra = jnp.concatenate([jnp.pad(high, room), jnp.pad(low, room)], axis=-1)
        return jnp.concatenate([weight_rows.astype(BF16), extra[..., None, :]], axis=-2)

    def unpack(packed):
        wide = packed.astype(F32)
        half = channels // 2
        return wide[..., :rows, :], wide[..., rows, :each] + wide[..., rows, half : half + each]

    small_parts = jnp.pad(small, (0, each * parts - small.shape[0]))
    payload = pack(
        local_weight.reshape(core_count, plane_count, rows, channels),
        small_parts.reshape(core_count, plane_count, each),
    )
    for axes in ("c", PLANE, COLUMN):
        if axes == COLUMN:
            arrived = everyone(payload, axes)
        else:
            arrived = lax.all_to_all(payload, axes, 0, 0)
        weight_sum, small_sum = unpack(arrived)
        payload = pack(weight_sum.sum(0), small_sum.sum(0))
    payload = lax.all_gather(everyone(payload, PLANE), "c")
    weight_sum, small_sum = unpack(payload)
    weight_sum = weight_sum.reshape(3, 3, channels, channels)
    small_sum = small_sum.reshape(-1)
    cuts = [samples * channels, samples * channels, channels, channels, samples * GROUPS, samples * GROUPS]
    pieces, start = [], 0
    for cut in cuts:
        pieces.append(small_sum[start : start + cut])
        start += cut
    demod_sum = pieces[0].reshape(samples, channels) * demod * demod * demod
    style_sum = pieces[1].reshape(samples, channels)
    shrink = jnp.einsum("bi,bo->io", style * style, demod_sum, precision=lax.Precision.HIGHEST)
    grad_weight = scale_gradient * (weight_sum - shrink * conv_weight)
    grad_style_rows = style_sum - style * jnp.dot(
        demod_sum, power.T, precision=lax.Precision.HIGHEST
    )
    grad_style = scale_gradient * jnp.dot(emb.T, grad_style_rows, precision=lax.Precision.HIGHEST)
    product_mean = pieces[4].reshape(samples, GROUPS) / cells_per_group
    squared_mean = pieces[5].reshape(samples, GROUPS) / cells_per_group
    mixed_gradient = inverse_deviation * (
        normalized_gradient - expand(product_mean) - normalized * expand(squared_mean)
    )
    grad_feats = (cotangent.astype(F32) + mixed_gradient).astype(BF16)
    return (
        block_out,
        grad_feats,
        grad_weight,
        grad_style,
        scale_gradient * pieces[2],
        scale_gradient * pieces[3],
    )


def solution(mesh):
    parts = Mesh(mesh.devices.reshape(4, 4, 2, 8, 2), LAT + LON)
    tile = P(None, LAT, LON, None)
    placed = (tile, tile, P(LAT, LON, None), P(), P(), P(), P(), P(), P(), tile)
    return jax.shard_map(
        on_device,
        mesh=parts,
        in_specs=placed,
        out_specs=(tile, tile, P(), P(), P(), P()),
        check_vma=False,
    )
```

```python
import functools
import math

import jax
import jax.numpy as jnp
from jax import lax
from jax.experimental import pallas as pl
from jax.experimental.pallas import tpu as pltpu
from jax.sharding import Mesh, PartitionSpec as P

GROUPS = 32
LAT = ("zh", "x")
LON = ("zl", "y", "c")
NEAR = ("zl", "y")
F32 = jnp.float32
BF16 = jnp.bfloat16
TILE = 8
SHARDS = 32
SLOT = 40
LANES = 128


def shift(block, axes, step, periodic):
    count = lax.axis_size(axes)
    pairs = [(i, i + step) for i in range(count)]
    if periodic:
        pairs = [(source, target % count) for source, target in pairs]
    else:
        pairs = [(source, target) for source, target in pairs if 0 <= target < count]
    return lax.ppermute(block, axes, pairs)


def extend(block, axes, dim, periodic):
    last = block.shape[dim] - 1
    low = shift(lax.slice_in_dim(block, last, last + 1, axis=dim), axes, 1, periodic)
    high = shift(lax.slice_in_dim(block, 0, 1, axis=dim), axes, -1, periodic)
    return jnp.concatenate([low, block, high], axis=dim)


def exchange(block, axes):
    return lax.all_to_all(block, axes, 0, 0)


def everyone(block, axes):
    return exchange(jnp.broadcast_to(block[None], (lax.axis_size(axes),) + block.shape), axes)


def call(body, outputs, scratch=()):
    return pl.pallas_call(
        body,
        out_shape=outputs,
        scratch_shapes=list(scratch),
        compiler_params=pltpu.CompilerParams(vmem_limit_bytes=48 * 1024 * 1024),
    )


def array(shape, dtype=F32):
    return jax.ShapeDtypeStruct(shape, dtype)


def lanes_of(rows=1):
    return lax.broadcasted_iota(jnp.int32, (rows, LANES), 1)


def group_total(row):
    lane = lanes_of()
    for step in (1, 2):
        after, before = pltpu.roll(row, LANES - step, 1), pltpu.roll(row, step, 1)
        row = row + jnp.where((lane & step) == 0, after, before)
    return row


def weave(first, second):
    return jnp.where((lanes_of() & 1) == 0, first, second)


def unweave(row, sample):
    if sample == 0:
        return weave(row, pltpu.roll(row, 1, 1))
    return weave(pltpu.roll(row, LANES - 1, 1), row)


def mix_body(feats, cond, null, flags, mixed_out, moments_out):
    samples, tile_rows, tile_cols, channels = feats.shape
    cells = tile_rows * tile_cols
    null32 = null[...].astype(F32)
    means, spreads = [], []
    for sample in range(samples):
        dropped = flags[sample : sample + 1, :].astype(F32).reshape(1, 1, channels)
        mixed = (
            feats[sample].astype(F32) + dropped * null32 + (1.0 - dropped) * cond[sample].astype(F32)
        ).astype(BF16)
        mixed_out[sample] = mixed
        wide = mixed.astype(F32).reshape(cells, channels)
        size = cells * (channels // GROUPS)
        mean = group_total(jnp.sum(wide, axis=0, keepdims=True)) * (1.0 / size)
        away = wide - mean
        means.append(mean)
        spreads.append(group_total(jnp.sum(away * away, axis=0, keepdims=True)))
    row = jnp.concatenate([weave(*means), weave(*spreads)], axis=0)
    moments_out[...] = jnp.broadcast_to(row[None], moments_out.shape)


def merged(rows, count):
    mean = jnp.mean(rows[:, 0:1, :], axis=0)
    away = rows[:, 0:1, :] - mean[None]
    spread = jnp.sum(rows[:, 1:2, :] + count * away * away, axis=0)
    return mean, spread


def merge_body(count, rows, moments_out):
    row = jnp.concatenate(merged(rows[...], count), axis=0)
    moments_out[...] = jnp.broadcast_to(row[None], moments_out.shape)


def sums_body(
    count, cells, rows, padded, mixed, cotangent, grad_act, affine, keep, style_col, demod, weight,
    stats_out, payload_out, act, shifted, total,
):
    samples, tile_rows, tile_cols, channels = cotangent.shape
    size = tile_rows * tile_cols
    mean_all, spread_all = merged(rows[...], count)
    inverse_all = lax.rsqrt(spread_all * (1.0 / cells) + 1e-05)
    gamma, beta = affine[0:1, :], affine[1:2, :]
    sums = [[], [], [], []]
    for sample in range(samples):
        mean, inverse = unweave(mean_all, sample), unweave(inverse_all, sample)
        stats_out[sample : sample + 1, :] = mean
        stats_out[samples + sample : samples + sample + 1, :] = inverse
        around = (padded[sample].astype(F32) - mean[None]) * inverse[None]
        around = around * gamma[None] + beta[None]
        act[...] = around / (1.0 + jnp.exp(-around))
        for side, at in ((0, 0), (1, tile_rows + 1)):
            act[at] = jnp.where(keep[side : side + 1, :] > 0.0, act[at], 0.0)
        for tap in range(3):
            moved = act[:, tap : tap + tile_cols, :].reshape(-1, channels)
            shifted[:, tap * channels : (tap + 1) * channels] = moved.astype(BF16)
        flat_cot = cotangent[sample].reshape(size, channels)
        style_full = jnp.broadcast_to(style_col[:, sample : sample + 1], (channels, channels))
        demod_row = demod[sample : sample + 1, :]
        both = style_full * demod_row
        product = jnp.zeros((channels, channels), F32)
        for row_tap in range(3):
            window = shifted[row_tap * tile_cols : row_tap * tile_cols + size, :]
            grad = lax.dot_general(
                window, flat_cot, (((0,), (0,)), ((), ())), preferred_element_type=F32
            )
            for col_tap in range(3):
                tap = row_tap * 3 + col_tap
                block = grad[col_tap * channels : (col_tap + 1) * channels, :]
                product = product + block * weight[tap]
                here = slice(tap * channels, (tap + 1) * channels)
                part = block * both
                total[here, :] = part if sample == 0 else total[here, :] + part
        sums[0].append(jnp.sum(product * style_full, axis=0, keepdims=True))
        sums[1].append(jnp.sum((product * demod_row).T, axis=0, keepdims=True))
        normalized = (mixed[sample].reshape(size, channels).astype(F32) - mean) * inverse
        pre = normalized * gamma + beta
        sig = 1.0 / (1.0 + jnp.exp(-pre))
        grad_pre = grad_act[sample].reshape(size, channels) * (sig * (1.0 + pre * (1.0 - sig)))
        sums[2].append(jnp.sum(grad_pre * normalized, axis=0, keepdims=True))
        sums[3].append(jnp.sum(grad_pre, axis=0, keepdims=True))
    small = jnp.concatenate(sum(sums, []), axis=0)
    lane = lanes_of(TILE)
    sub = lax.broadcasted_iota(jnp.int32, (TILE, channels), 0)
    quarters = []
    for quarter in range(4):
        turned = pltpu.roll(small, LANES - 32 * quarter, 1) if quarter else small
        piece = jnp.where(lane < 64, turned, pltpu.roll(turned, 64, 1))
        piece = jnp.where((lane & 32) == 0, piece, 0.0)
        quarters.append(split_terms(piece, lane))
    for shard in range(SHARDS):
        main = total[32 * shard : 32 * shard + 32, :]
        start = 8 * channels + 8 * (shard // 2)
        last = total[start : start + 8, :]
        if shard % 2:
            last = pltpu.roll(last, 4, 0)
        extra = quarters[shard % 4][shard // 4 : shard // 4 + 1, :]
        tail = jnp.where(sub < 4, last, jnp.where(sub == 4, extra, 0.0))
        payload_out[shard] = jnp.concatenate([main, tail], axis=0).astype(BF16)


def split_terms(values, lane):
    high = values.astype(BF16).astype(F32)
    return jnp.where(lane < 64, high, values - high)


def resplit(slots):
    row = lax.broadcasted_iota(jnp.int32, slots.shape, slots.ndim - 2)
    lane = lax.broadcasted_iota(jnp.int32, slots.shape, slots.ndim - 1)
    joined = slots + jnp.roll(slots, 64, slots.ndim - 1)
    high = lax.reduce_precision(joined, 8, 7)
    terms = jnp.where(lane < 64, high, joined - high)
    return jnp.where(row == 36, terms, slots).astype(BF16)


def last_body(
    scale, cells, gathered, stats, mixed, cotangent, grad_act, affine, style, style_col, demod,
    power, weight, emb_col, feats_out, weight_out, style_out, affine_out,
):
    samples, tile_rows, tile_cols, channels = cotangent.shape
    size = tile_rows * tile_cols
    lane = lanes_of()
    sub = lax.broadcasted_iota(jnp.int32, (TILE, channels), 0)
    main, tails, small = [], [], []
    for shard in range(SHARDS):
        slot = gathered[shard].astype(F32)
        main.append(slot[0:32, :])
        tails.append(slot[32:40, :])
    for row in range(TILE):
        whole = jnp.zeros((1, channels), F32)
        for quarter in range(4):
            piece = tails[4 * row + quarter][4:5, :]
            piece = piece + pltpu.roll(piece, 64, 1)
            if quarter:
                piece = pltpu.roll(piece, 32 * quarter, 1)
            whole = jnp.where((lane >> 5) == quarter, piece, whole)
        small.append(whole)
    demod_sums, style_sums, gamma_sums, beta_sums = small[0:2], small[2:4], small[4:6], small[6:8]
    gamma, beta = affine[0:1, :], affine[1:2, :]
    affine_out[0:1, :] = scale * (gamma_sums[0] + gamma_sums[1])
    affine_out[1:2, :] = scale * (beta_sums[0] + beta_sums[1])
    shrink = jnp.zeros((channels, channels), F32)
    rows = []
    for sample in range(samples):
        demod_row = demod[sample : sample + 1, :]
        pulled = demod_sums[sample] * (demod_row * demod_row * demod_row)
        style_full = jnp.broadcast_to(style_col[:, sample : sample + 1], (channels, channels))
        shrink = shrink + style_full * style_full * pulled
        spent = jnp.sum((power[...] * pulled).T, axis=0, keepdims=True)
        rows.append(style_sums[sample] - style[sample : sample + 1, :] * spent)
    for tap in range(8):
        for part in range(4):
            here = slice(32 * part, 32 * part + 32)
            weight_out[tap, here, :] = scale * (
                main[4 * tap + part] - shrink[here, :] * weight[tap, here, :]
            )
    for pair in range(16):
        here = slice(8 * pair, 8 * pair + 8)
        block = jnp.where(sub < 4, tails[2 * pair], pltpu.roll(tails[2 * pair + 1], 4, 0))
        weight_out[8, here, :] = scale * (block - shrink[here, :] * weight[8, here, :])
    style_out[...] = scale * (emb_col[:, 0:1] * rows[0] + emb_col[:, 1:2] * rows[1])
    for sample in range(samples):
        mean = stats[sample : sample + 1, :]
        inverse = stats[samples + sample : samples + sample + 1, :]
        product_mean = group_total(gamma * beta_sums[sample]) * (1.0 / cells)
        squared_mean = group_total(gamma * gamma_sums[sample]) * (1.0 / cells)
        normalized = (mixed[sample].reshape(size, channels).astype(F32) - mean) * inverse
        pre = normalized * gamma + beta
        sig = 1.0 / (1.0 + jnp.exp(-pre))
        grad_pre = grad_act[sample].reshape(size, channels) * (sig * (1.0 + pre * (1.0 - sig)))
        change = inverse * (gamma * grad_pre - product_mean - normalized * squared_mean)
        out = cotangent[sample].reshape(size, channels).astype(F32) + change
        feats_out[sample] = out.astype(BF16).reshape(tile_rows, tile_cols, channels)


def apply_taps(padded, taps, tile_rows, tile_cols):
    total = jnp.zeros(padded.shape[:1] + (tile_rows, tile_cols, taps.shape[4]), F32)
    for row_tap in range(3):
        for col_tap in range(3):
            window = padded[:, row_tap : row_tap + tile_rows, col_tap : col_tap + tile_cols]
            total = total + jnp.einsum(
                "bhwi,bio->bhwo", window, taps[:, row_tap, col_tap], preferred_element_type=F32
            )
    return total


def on_device(
    feats, cond, null_field, drop_flags, emb, style_weight, conv_weight, gamma, beta, cotangent
):
    samples, tile_rows, tile_cols, channels = feats.shape
    group_size = channels // GROUPS
    lat_count, lon_count = lax.axis_size(LAT), lax.axis_size(LON)
    devices_all = lat_count * lon_count
    cells_local = tile_rows * tile_cols * group_size
    cells_per_group = cells_local * devices_all
    scale_gradient = 1.0 / math.sqrt(samples * tile_rows * tile_cols * devices_all)
    taps = conv_weight.reshape(9, channels, channels)

    mixed, moments = call(
        mix_body, (array(feats.shape, BF16), array((lon_count, 2, LANES)))
    )(feats, cond, null_field, drop_flags)
    moments = exchange(moments, LON)
    both = extend(jnp.stack([mixed, cotangent]), LON, 3, True)
    moments = call(
        functools.partial(merge_body, cells_local), array((lat_count, 2, LANES))
    )(moments)
    both, moments = lax.optimization_barrier((both, moments))
    moments = exchange(moments, LAT)
    both = extend(both, LAT, 2, False)
    mixed_pad, cot_pad = both[0], both[1]

    style = 1.0 + jnp.dot(emb, style_weight, precision=lax.Precision.HIGHEST)
    power = jnp.sum(conv_weight * conv_weight, axis=(0, 1))
    demod = lax.rsqrt(jnp.dot(style * style, power, precision=lax.Precision.HIGHEST) + 1e-08)
    modded = conv_weight[None] * style[:, None, None, :, None]
    w_eff = (modded * demod[:, None, None, None, :]).astype(BF16)
    back_taps = jnp.swapaxes(w_eff[:, ::-1, ::-1], 3, 4)
    grad_act = apply_taps(cot_pad, back_taps, tile_rows, tile_cols)

    lat_at = lax.axis_index(LAT)
    inside = jnp.stack([lat_at > 0, lat_at < lat_count - 1])
    keep = jnp.broadcast_to(inside.astype(F32)[:, None], (2, LANES))
    affine = jnp.stack([gamma, beta])
    style_col = style.T
    stats, payload = call(
        functools.partial(sums_body, cells_local * lon_count, cells_per_group),
        (array((2 * samples, LANES)), array((SHARDS, SLOT, LANES), BF16)),
        (
            pltpu.VMEM((tile_rows + 2, tile_cols + 2, channels), F32),
            pltpu.VMEM(((tile_rows + 2) * tile_cols, 3 * channels), BF16),
            pltpu.VMEM((9 * channels, channels), F32),
        ),
    )(moments, mixed_pad, mixed, cotangent, grad_act, affine, keep, style_col, demod, taps)

    core_count, near_count = lax.axis_size("c"), lax.axis_size(NEAR)
    payload = payload.reshape(core_count, near_count, SLOT, LANES)
    payload = resplit(jnp.sum(exchange(payload, "c").astype(F32), axis=0))
    payload = resplit(jnp.sum(exchange(payload, NEAR).astype(F32), axis=0))
    payload = resplit(jnp.sum(everyone(payload, LAT).astype(F32), axis=0))
    payload = lax.all_gather(everyone(payload, NEAR), "c")

    mean = stats[:samples][:, None, None, :]
    inverse = stats[samples:][:, None, None, :]
    row_at = jnp.arange(tile_rows + 2)
    inside_rows = ((row_at > 0) | inside[0]) & ((row_at <= tile_rows) | inside[1])
    pre_pad = (mixed_pad.astype(F32) - mean) * inverse * gamma + beta
    act_pad = jnp.where(inside_rows[None, :, None, None], jax.nn.silu(pre_pad), 0.0).astype(BF16)
    conv_out = apply_taps(act_pad, w_eff, tile_rows, tile_cols)
    block_out = (mixed.astype(F32) + conv_out).astype(BF16)

    grad_feats, grad_weight, grad_style, grad_affine = call(
        functools.partial(last_body, scale_gradient, cells_per_group),
        (
            array(feats.shape, BF16),
            array(taps.shape),
            array(style_weight.shape),
            array((2, LANES)),
        ),
    )(
        payload.reshape(SHARDS, SLOT, LANES), stats, mixed, cotangent, grad_act, affine, style,
        style_col, demod, power, taps, emb.T,
    )
    return (
        block_out,
        grad_feats,
        grad_weight.reshape(conv_weight.shape),
        grad_style,
        grad_affine[0],
        grad_affine[1],
    )


def solution(mesh):
    parts = Mesh(mesh.devices.reshape(4, 4, 2, 8, 2), LAT + LON)
    tile = P(None, LAT, LON, None)
    placed = (tile, tile, P(LAT, LON, None), P(), P(), P(), P(), P(), P(), tile)
    return jax.shard_map(
        on_device,
        mesh=parts,
        in_specs=placed,
        out_specs=(tile, tile, P(), P(), P(), P()),
        check_vma=False,
    )
```

```python
import functools
import math

import jax
import jax.numpy as jnp
from jax import lax
from jax.experimental import pallas as pl
from jax.experimental.pallas import tpu as pltpu
from jax.sharding import Mesh, PartitionSpec as P

GROUPS = 32
LAT = ("zh", "x")
LON = ("zl", "y", "c")
NEAR = ("zl", "y")
F32 = jnp.float32
BF16 = jnp.bfloat16
TILE = 8
SHARDS = 32
SLOT = 40
LANES = 128


def shift(block, axes, step, periodic):
    count = lax.axis_size(axes)
    pairs = [(i, i + step) for i in range(count)]
    if periodic:
        pairs = [(source, target % count) for source, target in pairs]
    else:
        pairs = [(source, target) for source, target in pairs if 0 <= target < count]
    return lax.ppermute(block, axes, pairs)


def extend(block, axes, dim, periodic):
    last = block.shape[dim] - 1
    low = shift(lax.slice_in_dim(block, last, last + 1, axis=dim), axes, 1, periodic)
    high = shift(lax.slice_in_dim(block, 0, 1, axis=dim), axes, -1, periodic)
    return jnp.concatenate([low, block, high], axis=dim)


def exchange(block, axes):
    return lax.all_to_all(block, axes, 0, 0)


def everyone(block, axes):
    return exchange(jnp.broadcast_to(block[None], (lax.axis_size(axes),) + block.shape), axes)


def call(body, outputs, scratch=(), room=48, **more):
    return pl.pallas_call(
        body,
        out_shape=outputs,
        scratch_shapes=list(scratch),
        **more,
        compiler_params=pltpu.CompilerParams(vmem_limit_bytes=room * 1024 * 1024),
    )


def array(shape, dtype=F32):
    return jax.ShapeDtypeStruct(shape, dtype)


def lanes_of(rows=1):
    return lax.broadcasted_iota(jnp.int32, (rows, LANES), 1)


def group_total(row):
    lane = lanes_of()
    for step in (1, 2):
        after, before = pltpu.roll(row, LANES - step, 1), pltpu.roll(row, step, 1)
        row = row + jnp.where((lane & step) == 0, after, before)
    return row


def weave(first, second):
    return jnp.where((lanes_of() & 1) == 0, first, second)


def unweave(row, sample):
    if sample == 0:
        return weave(row, pltpu.roll(row, 1, 1))
    return weave(pltpu.roll(row, LANES - 1, 1), row)


def mix_body(
    feats_in, cond_in, null_in, cot_in, flags, mixed_out, moments_out, first_out, last_out,
    feats, cond, null, cot, arrivals,
):
    copies = []
    for at, (source, target) in enumerate(
        ((null_in, null), (feats_in, feats), (cond_in, cond), (cot_in, cot))
    ):
        copies.append(pltpu.make_async_copy(source, target, arrivals.at[at]))
        copies[-1].start()
    for copy in copies[:3]:
        copy.wait()
    samples, tile_rows, tile_cols, channels = feats.shape
    cells = tile_rows * tile_cols
    size = cells * (channels // GROUPS)
    null32 = null[...].astype(F32)
    means, spreads = [], []
    for sample in range(samples):
        dropped = flags[sample : sample + 1, :].astype(F32).reshape(1, 1, channels)
        mixed = (
            feats[sample].astype(F32) + dropped * null32 + (1.0 - dropped) * cond[sample].astype(F32)
        ).astype(BF16)
        mixed_out[sample] = mixed
        wide = mixed.astype(F32)
        first_out[0, sample] = wide[:, 0, :].astype(BF16)
        last_out[0, sample] = wide[:, tile_cols - 1, :].astype(BF16)
        wide = wide.reshape(cells, channels)
        mean = group_total(jnp.sum(wide, axis=0, keepdims=True)) * (1.0 / size)
        away = wide - mean
        means.append(mean)
        spreads.append(group_total(jnp.sum(away * away, axis=0, keepdims=True)))
    row = jnp.concatenate([weave(*means), weave(*spreads)], axis=0)
    moments_out[...] = jnp.broadcast_to(row[None], moments_out.shape)
    copies[3].wait()
    for sample in range(samples):
        wide = cot[sample].astype(F32)
        first_out[1, sample] = wide[:, 0, :].astype(BF16)
        last_out[1, sample] = wide[:, tile_cols - 1, :].astype(BF16)


def merged(rows, count):
    mean = jnp.mean(rows[:, 0:1, :], axis=0)
    away = rows[:, 0:1, :] - mean[None]
    spread = jnp.sum(rows[:, 1:2, :] + count * away * away, axis=0)
    return mean, spread


def merge_body(count, rows, moments_out):
    row = jnp.concatenate(merged(rows[...], count), axis=0)
    moments_out[...] = jnp.broadcast_to(row[None], moments_out.shape)


def windows(padded, spread, shifted, rows, cols):
    spread[...] = padded
    channels = padded.shape[-1]
    for tap in range(3):
        moved = spread[:, tap : tap + cols, :].reshape((rows + 2) * cols, channels)
        shifted[:, tap * channels : (tap + 1) * channels] = moved.astype(BF16)


def back_body(padded, taps, shifted_out, grad_out, spread):
    samples, rows, cols = padded.shape[0], padded.shape[1] - 2, padded.shape[2] - 2
    size = rows * cols
    for sample in range(samples):
        shifted = shifted_out.at[sample]
        windows(padded[sample].astype(F32), spread, shifted, rows, cols)
        total = jnp.zeros((size, taps.shape[3]), F32)
        for row_tap in range(3):
            window = shifted[row_tap * cols : row_tap * cols + size, :]
            total = total + jnp.dot(window, taps[sample, row_tap], preferred_element_type=F32)
        grad_out[sample] = total


def forward_body(padded, taps, stats, affine, keep, block_out, spread, shifted):
    samples, rows, cols = padded.shape[0], padded.shape[1] - 2, padded.shape[2] - 2
    size = rows * cols
    gamma, beta = affine[0:1, :][None], affine[1:2, :][None]
    row = lax.broadcasted_iota(jnp.int32, spread.shape, 0)
    inside = ((row > 0) | (keep[0:1, :] > 0.0)[None]) & ((row <= rows) | (keep[1:2, :] > 0.0)[None])
    for sample in range(samples):
        mixed = padded[sample].astype(F32)
        mean = stats[sample : sample + 1, :][None]
        inverse = stats[samples + sample : samples + sample + 1, :][None]
        pre = (mixed - mean) * inverse * gamma + beta
        act = jnp.where(inside, pre / (1.0 + jnp.exp(-pre)), 0.0)
        windows(act, spread, shifted, rows, cols)
        total = mixed[1 : 1 + rows, 1 : 1 + cols, :].reshape(size, -1)
        for row_tap in range(3):
            window = shifted[row_tap * cols : row_tap * cols + size, :]
            total = total + jnp.dot(window, taps[sample, row_tap], preferred_element_type=F32)
        block_out[sample] = total.astype(BF16).reshape(rows, cols, -1)


def sums_body(
    count, cells, rows, mixed, shifted, grad_act, affine, style_col, demod, weight,
    stats_out, payload_out, total,
):
    samples, tile_rows, tile_cols, channels = mixed.shape
    size = tile_rows * tile_cols
    mean_all, spread_all = merged(rows[...], count)
    inverse_all = lax.rsqrt(spread_all * (1.0 / cells) + 1e-05)
    gamma, beta = affine[0:1, :], affine[1:2, :]
    sums = [[], [], [], []]
    for sample in range(samples):
        mean, inverse = unweave(mean_all, sample), unweave(inverse_all, sample)
        stats_out[sample : sample + 1, :] = mean
        stats_out[samples + sample : samples + sample + 1, :] = inverse
        normalized = (mixed[sample].reshape(size, channels).astype(F32) - mean) * inverse
        pre = normalized * gamma + beta
        sig = 1.0 / (1.0 + jnp.exp(-pre))
        act = (pre * sig).astype(BF16)
        grad_pre = grad_act[sample] * (sig * (1.0 + pre * (1.0 - sig)))
        sums[2].append(jnp.sum(grad_pre * normalized, axis=0, keepdims=True))
        sums[3].append(jnp.sum(grad_pre, axis=0, keepdims=True))
        style_full = jnp.broadcast_to(style_col[:, sample : sample + 1], (channels, channels))
        demod_row = demod[sample : sample + 1, :]
        both = style_full * demod_row
        product = jnp.zeros((channels, channels), F32)
        for row_tap in range(3):
            window = shifted[sample, row_tap * tile_cols : row_tap * tile_cols + size, :]
            grad = lax.dot_general(
                act, window, (((0,), (0,)), ((), ())), preferred_element_type=F32
            )
            for col_tap in range(3):
                tap = (2 - row_tap) * 3 + 2 - col_tap
                block = grad[:, col_tap * channels : (col_tap + 1) * channels]
                product = product + block * weight[tap]
                here = slice(tap * channels, (tap + 1) * channels)
                part = block * both
                total[here, :] = part if sample == 0 else total[here, :] + part
        sums[0].append(jnp.sum(product * style_full, axis=0, keepdims=True))
        sums[1].append(jnp.sum((product * demod_row).T, axis=0, keepdims=True))
    small = jnp.concatenate(sum(sums, []), axis=0)
    lane = lanes_of(TILE)
    sub = lax.broadcasted_iota(jnp.int32, (TILE, channels), 0)
    quarters = []
    for quarter in range(4):
        turned = pltpu.roll(small, LANES - 32 * quarter, 1) if quarter else small
        piece = jnp.where(lane < 64, turned, pltpu.roll(turned, 64, 1))
        piece = jnp.where((lane & 32) == 0, piece, 0.0)
        quarters.append(split_terms(piece, lane))
    for shard in range(SHARDS):
        main = total[32 * shard : 32 * shard + 32, :]
        start = 8 * channels + 8 * (shard // 2)
        last = total[start : start + 8, :]
        if shard % 2:
            last = pltpu.roll(last, 4, 0)
        extra = quarters[shard % 4][shard // 4 : shard // 4 + 1, :]
        tail = jnp.where(sub < 4, last, jnp.where(sub == 4, extra, 0.0))
        payload_out[shard] = jnp.concatenate([main, tail], axis=0).astype(BF16)


def split_terms(values, lane):
    high = values.astype(BF16).astype(F32)
    return jnp.where(lane < 64, high, values - high)


def resplit(slots):
    row = lax.broadcasted_iota(jnp.int32, slots.shape, slots.ndim - 2)
    lane = lax.broadcasted_iota(jnp.int32, slots.shape, slots.ndim - 1)
    joined = slots + jnp.roll(slots, 64, slots.ndim - 1)
    high = lax.reduce_precision(joined, 8, 7)
    terms = jnp.where(lane < 64, high, joined - high)
    return jnp.where(row == 36, terms, slots).astype(BF16)


def last_body(
    scale, cells, gathered, stats, mixed, cotangent, grad_act, affine, style, style_col, demod,
    power, weight, emb_col, feats_out, weight_out, style_out, affine_out,
):
    samples, tile_rows, tile_cols, channels = cotangent.shape
    size = tile_rows * tile_cols
    lane = lanes_of()
    sub = lax.broadcasted_iota(jnp.int32, (TILE, channels), 0)
    main, tails, small = [], [], []
    for shard in range(SHARDS):
        slot = gathered[shard].astype(F32)
        main.append(slot[0:32, :])
        tails.append(slot[32:40, :])
    for row in range(TILE):
        whole = jnp.zeros((1, channels), F32)
        for quarter in range(4):
            piece = tails[4 * row + quarter][4:5, :]
            piece = piece + pltpu.roll(piece, 64, 1)
            if quarter:
                piece = pltpu.roll(piece, 32 * quarter, 1)
            whole = jnp.where((lane >> 5) == quarter, piece, whole)
        small.append(whole)
    demod_sums, style_sums, gamma_sums, beta_sums = small[0:2], small[2:4], small[4:6], small[6:8]
    gamma, beta = affine[0:1, :], affine[1:2, :]
    affine_out[0:1, :] = scale * (gamma_sums[0] + gamma_sums[1])
    affine_out[1:2, :] = scale * (beta_sums[0] + beta_sums[1])
    shrink = jnp.zeros((channels, channels), F32)
    rows = []
    for sample in range(samples):
        demod_row = demod[sample : sample + 1, :]
        pulled = demod_sums[sample] * (demod_row * demod_row * demod_row)
        style_full = jnp.broadcast_to(style_col[:, sample : sample + 1], (channels, channels))
        shrink = shrink + style_full * style_full * pulled
        spent = jnp.sum((power[...] * pulled).T, axis=0, keepdims=True)
        rows.append(style_sums[sample] - style[sample : sample + 1, :] * spent)
    for tap in range(8):
        for part in range(4):
            here = slice(32 * part, 32 * part + 32)
            weight_out[tap, here, :] = scale * (
                main[4 * tap + part] - shrink[here, :] * weight[tap, here, :]
            )
    for pair in range(16):
        here = slice(8 * pair, 8 * pair + 8)
        block = jnp.where(sub < 4, tails[2 * pair], pltpu.roll(tails[2 * pair + 1], 4, 0))
        weight_out[8, here, :] = scale * (block - shrink[here, :] * weight[8, here, :])
    style_out[...] = scale * (emb_col[:, 0:1] * rows[0] + emb_col[:, 1:2] * rows[1])
    for sample in range(samples):
        mean = stats[sample : sample + 1, :]
        inverse = stats[samples + sample : samples + sample + 1, :]
        product_mean = group_total(gamma * beta_sums[sample]) * (1.0 / cells)
        squared_mean = group_total(gamma * gamma_sums[sample]) * (1.0 / cells)
        normalized = (mixed[sample].reshape(size, channels).astype(F32) - mean) * inverse
        pre = normalized * gamma + beta
        sig = 1.0 / (1.0 + jnp.exp(-pre))
        grad_pre = grad_act[sample] * (sig * (1.0 + pre * (1.0 - sig)))
        change = inverse * (gamma * grad_pre - product_mean - normalized * squared_mean)
        out = cotangent[sample].reshape(size, channels).astype(F32) + change
        feats_out[sample] = out.astype(BF16).reshape(tile_rows, tile_cols, channels)


def on_device(
    feats, cond, null_field, drop_flags, emb, style_weight, conv_weight, gamma, beta, cotangent
):
    samples, tile_rows, tile_cols, channels = feats.shape
    group_size = channels // GROUPS
    lat_count, lon_count = lax.axis_size(LAT), lax.axis_size(LON)
    devices_all = lat_count * lon_count
    cells_local = tile_rows * tile_cols * group_size
    cells_per_group = cells_local * devices_all
    scale_gradient = 1.0 / math.sqrt(samples * tile_rows * tile_cols * devices_all)
    taps = conv_weight.reshape(9, channels, channels)

    anywhere, whole = pl.BlockSpec(memory_space=pl.ANY), pl.BlockSpec(memory_space=pltpu.VMEM)
    edge = array((2, samples, tile_rows, channels), BF16)
    mixed, moments, first, last = call(
        mix_body,
        (array(feats.shape, BF16), array((lon_count, 2, LANES)), edge, edge),
        (
            pltpu.VMEM(feats.shape, BF16),
            pltpu.VMEM(feats.shape, BF16),
            pltpu.VMEM(null_field.shape, BF16),
            pltpu.VMEM(feats.shape, BF16),
            pltpu.SemaphoreType.DMA((4,)),
        ),
        room=60,
        in_specs=[anywhere] * 4 + [whole],
    )(feats, cond, null_field, cotangent, drop_flags)
    rows = exchange(moments, LON)
    low, high = shift(last, LON, 1, True), shift(first, LON, -1, True)
    moments = call(
        functools.partial(merge_body, cells_local),
        array((lat_count, 2, LANES)),
        cost_estimate=pl.CostEstimate(flops=50_000_000_000, bytes_accessed=150_000_000, transcendentals=0),
    )(rows)
    both = jnp.concatenate(
        [low[:, :, :, None], jnp.stack([mixed, cotangent]), high[:, :, :, None]], axis=3
    )
    rows = exchange(moments, LAT)
    low, high = shift(both[:, :, -1:], LAT, 1, False), shift(both[:, :, :1], LAT, -1, False)
    both = jnp.concatenate([low, both, high], axis=2)
    mixed_pad, cot_pad = both[0], both[1]

    style = 1.0 + jnp.dot(emb, style_weight, precision=lax.Precision.HIGHEST)
    power = jnp.sum(conv_weight * conv_weight, axis=(0, 1))
    demod = lax.rsqrt(jnp.dot(style * style, power, precision=lax.Precision.HIGHEST) + 1e-08)
    modded = conv_weight[None] * style[:, None, None, :, None]
    w_eff = (modded * demod[:, None, None, None, :]).astype(BF16)
    wide = (samples, 3, 3 * channels, channels)
    back_taps = jnp.swapaxes(w_eff[:, ::-1, ::-1], 3, 4).reshape(wide)
    spread = pltpu.VMEM((tile_rows + 2, tile_cols + 2, channels), F32)
    stretch = ((tile_rows + 2) * tile_cols, 3 * channels)
    shifted, grad_act = call(
        back_body,
        (
            array((samples,) + stretch, BF16),
            array((samples, tile_rows * tile_cols, channels)),
        ),
        (spread,),
    )(cot_pad, back_taps)

    lat_at = lax.axis_index(LAT)
    inside = jnp.stack([lat_at > 0, lat_at < lat_count - 1])
    keep = jnp.broadcast_to(inside.astype(F32)[:, None], (2, LANES))
    affine = jnp.stack([gamma, beta])
    style_col = style.T
    stats, payload = call(
        functools.partial(sums_body, cells_local * lon_count, cells_per_group),
        (array((2 * samples, LANES)), array((SHARDS, SLOT, LANES), BF16)),
        (pltpu.VMEM((9 * channels, channels), F32),),
    )(rows, mixed, shifted, grad_act, affine, style_col, demod, taps)

    core_count, near_count = lax.axis_size("c"), lax.axis_size(NEAR)
    payload = lax.all_gather(payload, "c")
    payload = payload.reshape(core_count, core_count, near_count, SLOT, LANES)
    payload = lax.dynamic_index_in_dim(payload, lax.axis_index("c"), 1, False)
    payload = resplit(jnp.sum(payload.astype(F32), axis=0))
    payload = resplit(jnp.sum(exchange(payload, NEAR).astype(F32), axis=0))
    payload = resplit(jnp.sum(everyone(payload, LAT).astype(F32), axis=0))
    payload = lax.all_gather(everyone(payload, NEAR), "c")

    block_out = call(
        forward_body, array(feats.shape, BF16), (spread, pltpu.VMEM(stretch, BF16))
    )(mixed_pad, w_eff.reshape(wide), stats, affine, keep)

    grad_feats, grad_weight, grad_style, grad_affine = call(
        functools.partial(last_body, scale_gradient, cells_per_group),
        (
            array(feats.shape, BF16),
            array(taps.shape),
            array(style_weight.shape),
            array((2, LANES)),
        ),
    )(
        payload.reshape(SHARDS, SLOT, LANES), stats, mixed, cotangent, grad_act, affine, style,
        style_col, demod, power, taps, emb.T,
    )
    return (
        block_out,
        grad_feats,
        grad_weight.reshape(conv_weight.shape),
        grad_style,
        grad_affine[0],
        grad_affine[1],
    )


def solution(mesh):
    parts = Mesh(mesh.devices.reshape(4, 4, 2, 8, 2), LAT + LON)
    tile = P(None, LAT, LON, None)
    placed = (tile, tile, P(LAT, LON, None), P(), P(), P(), P(), P(), P(), tile)
    return jax.shard_map(
        on_device,
        mesh=parts,
        in_specs=placed,
        out_specs=(tile, tile, P(), P(), P(), P()),
        check_vma=False,
    )
```

```python
import functools
import math

import jax
import jax.numpy as jnp
from jax import lax
from jax.experimental import pallas as pl
from jax.experimental.pallas import tpu as pltpu
from jax.sharding import Mesh, PartitionSpec as P

GROUPS = 32
LAT = ("zh", "x")
LON = ("zl", "y", "c")
NEAR = ("zl", "y")
F32 = jnp.float32
BF16 = jnp.bfloat16
TILE = 8
SHARDS = 32
SLOT = 40
LANES = 128


def shift(block, axes, step, periodic):
    count = lax.axis_size(axes)
    pairs = [(i, i + step) for i in range(count)]
    if periodic:
        pairs = [(source, target % count) for source, target in pairs]
    else:
        pairs = [(source, target) for source, target in pairs if 0 <= target < count]
    return lax.ppermute(block, axes, pairs)


def extend(block, axes, dim, periodic):
    last = block.shape[dim] - 1
    low = shift(lax.slice_in_dim(block, last, last + 1, axis=dim), axes, 1, periodic)
    high = shift(lax.slice_in_dim(block, 0, 1, axis=dim), axes, -1, periodic)
    return jnp.concatenate([low, block, high], axis=dim)


def exchange(block, axes):
    return lax.all_to_all(block, axes, 0, 0)


def everyone(block, axes):
    return exchange(jnp.broadcast_to(block[None], (lax.axis_size(axes),) + block.shape), axes)


def call(body, outputs, scratch=(), room=48, **more):
    return pl.pallas_call(
        body,
        out_shape=outputs,
        scratch_shapes=list(scratch),
        **more,
        compiler_params=pltpu.CompilerParams(vmem_limit_bytes=room * 1024 * 1024),
    )


def array(shape, dtype=F32):
    return jax.ShapeDtypeStruct(shape, dtype)


def lanes_of(rows=1):
    return lax.broadcasted_iota(jnp.int32, (rows, LANES), 1)


def group_total(row):
    lane = lanes_of()
    for step in (1, 2):
        after, before = pltpu.roll(row, LANES - step, 1), pltpu.roll(row, step, 1)
        row = row + jnp.where((lane & step) == 0, after, before)
    return row


def weave(first, second):
    return jnp.where((lanes_of() & 1) == 0, first, second)


def unweave(row, sample):
    if sample == 0:
        return weave(row, pltpu.roll(row, 1, 1))
    return weave(pltpu.roll(row, LANES - 1, 1), row)


def mix_body(
    feats_in, cond_in, null_in, cot_in, flags, mixed_out, moments_out, first_out, last_out,
    feats, cond, null, cot, arrivals,
):
    copies = []
    for at, (source, target) in enumerate(
        ((null_in, null), (feats_in, feats), (cond_in, cond), (cot_in, cot))
    ):
        copies.append(pltpu.make_async_copy(source, target, arrivals.at[at]))
        copies[-1].start()
    for copy in copies[:3]:
        copy.wait()
    samples, tile_rows, tile_cols, channels = feats.shape
    cells = tile_rows * tile_cols
    size = cells * (channels // GROUPS)
    null32 = null[...].astype(F32)
    means, spreads = [], []
    for sample in range(samples):
        dropped = flags[sample : sample + 1, :].astype(F32).reshape(1, 1, channels)
        mixed = (
            feats[sample].astype(F32) + dropped * null32 + (1.0 - dropped) * cond[sample].astype(F32)
        ).astype(BF16)
        mixed_out[sample] = mixed
        wide = mixed.astype(F32)
        first_out[0, sample] = wide[:, 0, :].astype(BF16)
        last_out[0, sample] = wide[:, tile_cols - 1, :].astype(BF16)
        wide = wide.reshape(cells, channels)
        mean = group_total(jnp.sum(wide, axis=0, keepdims=True)) * (1.0 / size)
        away = wide - mean
        means.append(mean)
        spreads.append(group_total(jnp.sum(away * away, axis=0, keepdims=True)))
    row = jnp.concatenate([weave(*means), weave(*spreads)], axis=0)
    moments_out[...] = jnp.broadcast_to(row[None], moments_out.shape)
    copies[3].wait()
    for sample in range(samples):
        wide = cot[sample].astype(F32)
        first_out[1, sample] = wide[:, 0, :].astype(BF16)
        last_out[1, sample] = wide[:, tile_cols - 1, :].astype(BF16)


def merged(rows, count):
    mean = jnp.mean(rows[:, 0:1, :], axis=0)
    away = rows[:, 0:1, :] - mean[None]
    spread = jnp.sum(rows[:, 1:2, :] + count * away * away, axis=0)
    return mean, spread


def merge_body(count, rows, moments_out):
    row = jnp.concatenate(merged(rows[...], count), axis=0)
    moments_out[...] = jnp.broadcast_to(row[None], moments_out.shape)


def windows(padded, spread, shifted, rows, cols):
    spread[...] = padded
    channels = padded.shape[-1]
    for tap in range(3):
        moved = spread[:, tap : tap + cols, :].reshape((rows + 2) * cols, channels)
        shifted[:, tap * channels : (tap + 1) * channels] = moved.astype(BF16)


def normalize_body(count, cells, rows, mixed, affine, stats_out, act_out, slope_out, norm_out):
    samples, tile_rows, tile_cols, channels = mixed.shape
    mean_all, spread_all = merged(rows[...], count)
    inverse_all = lax.rsqrt(spread_all * (1.0 / cells) + 1e-05)
    for sample in range(samples):
        mean, inverse = unweave(mean_all, sample), unweave(inverse_all, sample)
        stats_out[sample : sample + 1, :] = mean
        stats_out[samples + sample : samples + sample + 1, :] = inverse
        flat = mixed[sample].reshape(tile_rows * tile_cols, channels).astype(F32)
        normalized = (flat - mean) * inverse
        pre = normalized * affine[0:1, :] + affine[1:2, :]
        sig = 1.0 / (1.0 + jnp.exp(-pre))
        norm_out[sample] = normalized
        act_out[sample] = (pre * sig).astype(BF16)
        slope_out[sample] = sig * (1.0 + pre * (1.0 - sig))


def forward_body(padded, taps, stats, affine, keep, block_out, spread, shifted):
    samples, rows, cols = padded.shape[0], padded.shape[1] - 2, padded.shape[2] - 2
    size = rows * cols
    gamma, beta = affine[0:1, :][None], affine[1:2, :][None]
    row = lax.broadcasted_iota(jnp.int32, spread.shape, 0)
    inside = ((row > 0) | (keep[0:1, :] > 0.0)[None]) & ((row <= rows) | (keep[1:2, :] > 0.0)[None])
    for sample in range(samples):
        mixed = padded[sample].astype(F32)
        mean = stats[sample : sample + 1, :][None]
        inverse = stats[samples + sample : samples + sample + 1, :][None]
        pre = (mixed - mean) * inverse * gamma + beta
        act = jnp.where(inside, pre / (1.0 + jnp.exp(-pre)), 0.0)
        windows(act, spread, shifted, rows, cols)
        total = mixed[1 : 1 + rows, 1 : 1 + cols, :].reshape(size, -1)
        for row_tap in range(3):
            window = shifted[row_tap * cols : row_tap * cols + size, :]
            total = total + jnp.dot(window, taps[sample, row_tap], preferred_element_type=F32)
        block_out[sample] = total.astype(BF16).reshape(rows, cols, -1)


def sums_body(
    padded, act, slope, norm, back_taps, style_col, demod, weight,
    grad_out, payload_out, spread, shifted, total,
):
    samples, rows, cols = padded.shape[0], padded.shape[1] - 2, padded.shape[2] - 2
    size, channels = rows * cols, padded.shape[3]
    sums = [[], [], [], []]
    for sample in range(samples):
        windows(padded[sample].astype(F32), spread, shifted, rows, cols)
        style_full = jnp.broadcast_to(style_col[:, sample : sample + 1], (channels, channels))
        demod_row = demod[sample : sample + 1, :]
        both = style_full * demod_row
        product = jnp.zeros((channels, channels), F32)
        grad_act = jnp.zeros((size, channels), F32)
        for row_tap in range(3):
            window = shifted[row_tap * cols : row_tap * cols + size, :]
            grad_act = grad_act + jnp.dot(
                window, back_taps[sample, row_tap], preferred_element_type=F32
            )
            grad = lax.dot_general(
                act[sample], window, (((0,), (0,)), ((), ())), preferred_element_type=F32
            )
            for col_tap in range(3):
                tap = (2 - row_tap) * 3 + 2 - col_tap
                block = grad[:, col_tap * channels : (col_tap + 1) * channels]
                product = product + block * weight[tap]
                here = slice(tap * channels, (tap + 1) * channels)
                part = block * both
                total[here, :] = part if sample == 0 else total[here, :] + part
        grad_pre = grad_act * slope[sample]
        grad_out[sample] = grad_pre
        sums[0].append(jnp.sum(product * style_full, axis=0, keepdims=True))
        sums[1].append(jnp.sum((product * demod_row).T, axis=0, keepdims=True))
        sums[2].append(jnp.sum(grad_pre * norm[sample], axis=0, keepdims=True))
        sums[3].append(jnp.sum(grad_pre, axis=0, keepdims=True))
    small = jnp.concatenate(sum(sums, []), axis=0)
    lane = lanes_of(TILE)
    sub = lax.broadcasted_iota(jnp.int32, (TILE, channels), 0)
    quarters = []
    for quarter in range(4):
        turned = pltpu.roll(small, LANES - 32 * quarter, 1) if quarter else small
        piece = jnp.where(lane < 64, turned, pltpu.roll(turned, 64, 1))
        piece = jnp.where((lane & 32) == 0, piece, 0.0)
        quarters.append(split_terms(piece, lane))
    for shard in range(SHARDS):
        main = total[32 * shard : 32 * shard + 32, :]
        start = 8 * channels + 8 * (shard // 2)
        last = total[start : start + 8, :]
        if shard % 2:
            last = pltpu.roll(last, 4, 0)
        extra = quarters[shard % 4][shard // 4 : shard // 4 + 1, :]
        tail = jnp.where(sub < 4, last, jnp.where(sub == 4, extra, 0.0))
        payload_out[shard] = jnp.concatenate([main, tail], axis=0).astype(BF16)


def split_terms(values, lane):
    high = values.astype(BF16).astype(F32)
    return jnp.where(lane < 64, high, values - high)


def resplit(slots):
    row = lax.broadcasted_iota(jnp.int32, slots.shape, slots.ndim - 2)
    lane = lax.broadcasted_iota(jnp.int32, slots.shape, slots.ndim - 1)
    joined = slots + jnp.roll(slots, 64, slots.ndim - 1)
    high = lax.reduce_precision(joined, 8, 7)
    terms = jnp.where(lane < 64, high, joined - high)
    return jnp.where(row == 36, terms, slots).astype(BF16)


def last_body(
    scale, cells, gathered, stats, norm, cotangent, grad_pre, affine, style, style_col, demod,
    power, weight, emb_col, feats_out, weight_out, style_out, affine_out,
):
    samples, tile_rows, tile_cols, channels = cotangent.shape
    size = tile_rows * tile_cols
    lane = lanes_of()
    sub = lax.broadcasted_iota(jnp.int32, (TILE, channels), 0)
    main, tails, small = [], [], []
    for shard in range(SHARDS):
        slot = gathered[shard].astype(F32)
        main.append(slot[0:32, :])
        tails.append(slot[32:40, :])
    for row in range(TILE):
        whole = jnp.zeros((1, channels), F32)
        for quarter in range(4):
            piece = tails[4 * row + quarter][4:5, :]
            piece = piece + pltpu.roll(piece, 64, 1)
            if quarter:
                piece = pltpu.roll(piece, 32 * quarter, 1)
            whole = jnp.where((lane >> 5) == quarter, piece, whole)
        small.append(whole)
    demod_sums, style_sums, gamma_sums, beta_sums = small[0:2], small[2:4], small[4:6], small[6:8]
    gamma = affine[0:1, :]
    affine_out[0:1, :] = scale * (gamma_sums[0] + gamma_sums[1])
    affine_out[1:2, :] = scale * (beta_sums[0] + beta_sums[1])
    shrink = jnp.zeros((channels, channels), F32)
    rows = []
    for sample in range(samples):
        demod_row = demod[sample : sample + 1, :]
        pulled = demod_sums[sample] * (demod_row * demod_row * demod_row)
        style_full = jnp.broadcast_to(style_col[:, sample : sample + 1], (channels, channels))
        shrink = shrink + style_full * style_full * pulled
        spent = jnp.sum((power[...] * pulled).T, axis=0, keepdims=True)
        rows.append(style_sums[sample] - style[sample : sample + 1, :] * spent)
    for tap in range(8):
        for part in range(4):
            here = slice(32 * part, 32 * part + 32)
            weight_out[tap, here, :] = scale * (
                main[4 * tap + part] - shrink[here, :] * weight[tap, here, :]
            )
    for pair in range(16):
        here = slice(8 * pair, 8 * pair + 8)
        block = jnp.where(sub < 4, tails[2 * pair], pltpu.roll(tails[2 * pair + 1], 4, 0))
        weight_out[8, here, :] = scale * (block - shrink[here, :] * weight[8, here, :])
    style_out[...] = scale * (emb_col[:, 0:1] * rows[0] + emb_col[:, 1:2] * rows[1])
    for sample in range(samples):
        inverse = stats[samples + sample : samples + sample + 1, :]
        product_mean = group_total(gamma * beta_sums[sample]) * (1.0 / cells)
        squared_mean = group_total(gamma * gamma_sums[sample]) * (1.0 / cells)
        change = inverse * (gamma * grad_pre[sample] - product_mean - norm[sample] * squared_mean)
        out = cotangent[sample].reshape(size, channels).astype(F32) + change
        feats_out[sample] = out.astype(BF16).reshape(tile_rows, tile_cols, channels)


def on_device(
    feats, cond, null_field, drop_flags, emb, style_weight, conv_weight, gamma, beta, cotangent
):
    samples, tile_rows, tile_cols, channels = feats.shape
    group_size = channels // GROUPS
    lat_count, lon_count = lax.axis_size(LAT), lax.axis_size(LON)
    devices_all = lat_count * lon_count
    cells_local = tile_rows * tile_cols * group_size
    cells_per_group = cells_local * devices_all
    scale_gradient = 1.0 / math.sqrt(samples * tile_rows * tile_cols * devices_all)
    taps = conv_weight.reshape(9, channels, channels)

    anywhere, whole = pl.BlockSpec(memory_space=pl.ANY), pl.BlockSpec(memory_space=pltpu.VMEM)
    edge = array((2, samples, tile_rows, channels), BF16)
    mixed, moments, first, last = call(
        mix_body,
        (array(feats.shape, BF16), array((lon_count, 2, LANES)), edge, edge),
        (
            pltpu.VMEM(feats.shape, BF16),
            pltpu.VMEM(feats.shape, BF16),
            pltpu.VMEM(null_field.shape, BF16),
            pltpu.VMEM(feats.shape, BF16),
            pltpu.SemaphoreType.DMA((4,)),
        ),
        room=60,
        in_specs=[anywhere] * 4 + [whole],
    )(feats, cond, null_field, cotangent, drop_flags)
    rows = exchange(moments, LON)
    low, high = shift(last, LON, 1, True), shift(first, LON, -1, True)
    moments = call(functools.partial(merge_body, cells_local), array((lat_count, 2, LANES)))(rows)
    moments, low, high = lax.optimization_barrier((moments, low, high))
    both = jnp.concatenate(
        [low[:, :, :, None], jnp.stack([mixed, cotangent]), high[:, :, :, None]], axis=3
    )
    rows = exchange(moments, LAT)
    low, high = shift(both[:, :, -1:], LAT, 1, False), shift(both[:, :, :1], LAT, -1, False)
    affine = jnp.stack([gamma, beta])
    flat = (samples, tile_rows * tile_cols, channels)
    stats, act, slope, norm = call(
        functools.partial(normalize_body, cells_local * lon_count, cells_per_group),
        (array((2 * samples, LANES)), array(flat, BF16), array(flat), array(flat)),
    )(rows, mixed, affine)
    act, low, high = lax.optimization_barrier((act, low, high))
    both = jnp.concatenate([low, both, high], axis=2)
    mixed_pad, cot_pad = both[0], both[1]

    style = 1.0 + jnp.dot(emb, style_weight, precision=lax.Precision.HIGHEST)
    power = jnp.sum(conv_weight * conv_weight, axis=(0, 1))
    demod = lax.rsqrt(jnp.dot(style * style, power, precision=lax.Precision.HIGHEST) + 1e-08)
    modded = conv_weight[None] * style[:, None, None, :, None]
    w_eff = (modded * demod[:, None, None, None, :]).astype(BF16)
    wide = (samples, 3, 3 * channels, channels)
    back_taps = jnp.swapaxes(w_eff[:, ::-1, ::-1], 3, 4).reshape(wide)
    spread = pltpu.VMEM((tile_rows + 2, tile_cols + 2, channels), F32)
    stretch = ((tile_rows + 2) * tile_cols, 3 * channels)
    lat_at = lax.axis_index(LAT)
    inside = jnp.stack([lat_at > 0, lat_at < lat_count - 1])
    keep = jnp.broadcast_to(inside.astype(F32)[:, None], (2, LANES))
    style_col = style.T
    grad_pre, payload = call(
        sums_body,
        (array(flat), array((SHARDS, SLOT, LANES), BF16)),
        (spread, pltpu.VMEM(stretch, BF16), pltpu.VMEM((9 * channels, channels), F32)),
    )(cot_pad, act, slope, norm, back_taps, style_col, demod, taps)

    core_count, near_count = lax.axis_size("c"), lax.axis_size(NEAR)
    payload = lax.all_gather(payload, "c")
    payload = payload.reshape(core_count, core_count, near_count, SLOT, LANES)
    payload = lax.dynamic_index_in_dim(payload, lax.axis_index("c"), 1, False)
    payload = resplit(jnp.sum(payload.astype(F32), axis=0))
    payload = resplit(jnp.sum(exchange(payload, NEAR).astype(F32), axis=0))
    payload = resplit(jnp.sum(everyone(payload, LAT).astype(F32), axis=0))
    payload = lax.all_gather(everyone(payload, NEAR), "c")

    block_out = call(
        forward_body, array(feats.shape, BF16), (spread, pltpu.VMEM(stretch, BF16))
    )(mixed_pad, w_eff.reshape(wide), stats, affine, keep)

    grad_feats, grad_weight, grad_style, grad_affine = call(
        functools.partial(last_body, scale_gradient, cells_per_group),
        (
            array(feats.shape, BF16),
            array(taps.shape),
            array(style_weight.shape),
            array((2, LANES)),
        ),
    )(
        payload.reshape(SHARDS, SLOT, LANES), stats, norm, cotangent, grad_pre, affine, style,
        style_col, demod, power, taps, emb.T,
    )
    return (
        block_out,
        grad_feats,
        grad_weight.reshape(conv_weight.shape),
        grad_style,
        grad_affine[0],
        grad_affine[1],
    )


def solution(mesh):
    parts = Mesh(mesh.devices.reshape(4, 4, 2, 8, 2), LAT + LON)
    tile = P(None, LAT, LON, None)
    placed = (tile, tile, P(LAT, LON, None), P(), P(), P(), P(), P(), P(), tile)
    return jax.shard_map(
        on_device,
        mesh=parts,
        in_specs=placed,
        out_specs=(tile, tile, P(), P(), P(), P()),
        check_vma=False,
    )
```

```python
import functools
import math

import jax
import jax.numpy as jnp
from jax import lax
from jax.experimental import pallas as pl
from jax.experimental.pallas import tpu as pltpu
from jax.sharding import Mesh, PartitionSpec as P

GROUPS = 32
LAT = ("zh", "x")
LON = ("zl", "y", "c")
NEAR = ("zl", "y")
F32 = jnp.float32
BF16 = jnp.bfloat16
TILE = 8
SHARDS = 32
SLOT = 40
LANES = 128


def shift(block, axes, step, periodic):
    count = lax.axis_size(axes)
    pairs = [(i, i + step) for i in range(count)]
    if periodic:
        pairs = [(source, target % count) for source, target in pairs]
    else:
        pairs = [(source, target) for source, target in pairs if 0 <= target < count]
    return lax.ppermute(block, axes, pairs)


def extend(block, axes, dim, periodic):
    last = block.shape[dim] - 1
    low = shift(lax.slice_in_dim(block, last, last + 1, axis=dim), axes, 1, periodic)
    high = shift(lax.slice_in_dim(block, 0, 1, axis=dim), axes, -1, periodic)
    return jnp.concatenate([low, block, high], axis=dim)


def exchange(block, axes):
    return lax.all_to_all(block, axes, 0, 0)


def everyone(block, axes):
    return exchange(jnp.broadcast_to(block[None], (lax.axis_size(axes),) + block.shape), axes)


def call(body, outputs, scratch=(), room=48, **more):
    return pl.pallas_call(
        body,
        out_shape=outputs,
        scratch_shapes=list(scratch),
        **more,
        compiler_params=pltpu.CompilerParams(vmem_limit_bytes=room * 1024 * 1024),
    )


def array(shape, dtype=F32):
    return jax.ShapeDtypeStruct(shape, dtype)


def lanes_of(rows=1):
    return lax.broadcasted_iota(jnp.int32, (rows, LANES), 1)


def group_total(row):
    lane = lanes_of()
    for step in (1, 2):
        after, before = pltpu.roll(row, LANES - step, 1), pltpu.roll(row, step, 1)
        row = row + jnp.where((lane & step) == 0, after, before)
    return row


def weave(first, second):
    return jnp.where((lanes_of() & 1) == 0, first, second)


def unweave(row, sample):
    if sample == 0:
        return weave(row, pltpu.roll(row, 1, 1))
    return weave(pltpu.roll(row, LANES - 1, 1), row)


def place(axes):
    index = 0
    for axis in axes:
        index = index * lax.axis_size(axis) + lax.axis_index(axis)
    return index


def three_terms(value):
    terms = []
    for _ in range(3):
        terms.append(value.astype(BF16).astype(F32))
        value = value - terms[-1]
    return terms


def merged(slots, count):
    rows = slots[:, 0:8, :].astype(F32)
    means = rows[:, 0:1, :] + rows[:, 1:2, :] + rows[:, 2:3, :]
    spreads = rows[:, 3:4, :] + rows[:, 4:5, :] + rows[:, 5:6, :]
    mean = jnp.mean(means, axis=0)
    away = means - mean[None]
    return mean, jnp.sum(spreads + count * away * away, axis=0)


def header(mean, spread):
    return three_terms(mean) + three_terms(spread) + [jnp.zeros((2, LANES), F32)]


def mix_body(
    feats_in, cond_in, null_in, cot_in, flags, mixed_out, slots_out,
    feats, cond, null, cot, arrivals,
):
    copies = []
    for at, (source, target) in enumerate(
        ((null_in, null), (feats_in, feats), (cond_in, cond), (cot_in, cot))
    ):
        copies.append(pltpu.make_async_copy(source, target, arrivals.at[at]))
        copies[-1].start()
    for copy in copies[:3]:
        copy.wait()
    samples, tile_rows, tile_cols, channels = feats.shape
    cells = tile_rows * tile_cols
    size = cells * (channels // GROUPS)
    null32 = null[...].astype(F32)
    means, spreads = [], []
    for sample in range(samples):
        dropped = flags[sample : sample + 1, :].astype(F32).reshape(1, 1, channels)
        mixed = (
            feats[sample].astype(F32) + dropped * null32 + (1.0 - dropped) * cond[sample].astype(F32)
        ).astype(BF16)
        mixed_out[sample] = mixed
        wide = mixed.astype(F32).reshape(cells, channels)
        mean = group_total(jnp.sum(wide, axis=0, keepdims=True)) * (1.0 / size)
        away = wide - mean
        means.append(mean)
        spreads.append(group_total(jnp.sum(away * away, axis=0, keepdims=True)))
    rows = header(weave(*means), weave(*spreads))
    copies[3].wait()
    firsts, lasts = [], []
    for sample in range(samples):
        wide = cot[sample].astype(F32)
        firsts.append(wide[:, 0, :])
        lasts.append(wide[:, tile_cols - 1, :])
    slots_out[...] = jnp.broadcast_to(
        jnp.concatenate(rows + firsts, axis=0).astype(BF16)[None], slots_out.shape
    )
    after = lax.rem(place(LON) + 1, slots_out.shape[0])
    slots_out[after] = jnp.concatenate(rows + lasts, axis=0).astype(BF16)


def merge_body(count, slots, cot, wide_out, slots_out, edge):
    samples, tile_rows, tile_cols, channels = cot.shape
    lon_count, lat_count = slots.shape[0], slots_out.shape[0]
    mean, spread = merged(slots, count)
    me = place(LON)
    before = slots[lax.rem(me + lon_count - 1, lon_count)].astype(F32)
    after = slots[lax.rem(me + 1, lon_count)].astype(F32)
    for sample in range(samples):
        here = slice(8 + sample * tile_rows, 8 + (sample + 1) * tile_rows)
        wide_out[sample, :, 0, :] = before[here, :]
        wide_out[sample, :, 1 : 1 + tile_cols, :] = cot[sample].astype(F32)
        wide_out[sample, :, 1 + tile_cols, :] = after[here, :]
    edge[...] = jnp.zeros(edge.shape, F32)
    edge[0:8, :] = jnp.concatenate(header(mean, spread), axis=0)
    span = tile_cols + 2
    for sample in range(samples):
        edge[8 + sample * span : 8 + (sample + 1) * span, :] = wide_out[sample, 0]
    slots_out[...] = jnp.broadcast_to(edge[...].astype(BF16)[None], slots_out.shape)
    for sample in range(samples):
        edge[8 + sample * span : 8 + (sample + 1) * span, :] = wide_out[sample, tile_rows - 1]
    row = place(LAT)

    @pl.when(row < lat_count - 1)
    def _():
        slots_out[row + 1] = edge[...].astype(BF16)


def windows(spread, shifted, rows, cols):
    channels = spread.shape[-1]
    for tap in range(3):
        moved = spread[:, tap : tap + cols, :].reshape((rows + 2) * cols, channels)
        shifted[:, tap * channels : (tap + 1) * channels] = moved.astype(BF16)


def forward_body(padded, taps, stats, affine, keep, block_out, spread, shifted):
    samples, rows, cols = padded.shape[0], padded.shape[1] - 2, padded.shape[2] - 2
    size = rows * cols
    gamma, beta = affine[0:1, :][None], affine[1:2, :][None]
    row = lax.broadcasted_iota(jnp.int32, spread.shape, 0)
    inside = ((row > 0) | (keep[0:1, :] > 0.0)[None]) & ((row <= rows) | (keep[1:2, :] > 0.0)[None])
    for sample in range(samples):
        mixed = padded[sample].astype(F32)
        mean = stats[sample : sample + 1, :][None]
        inverse = stats[samples + sample : samples + sample + 1, :][None]
        pre = (mixed - mean) * inverse * gamma + beta
        act = jnp.where(inside, pre / (1.0 + jnp.exp(-pre)), 0.0)
        spread[...] = act
        windows(spread, shifted, rows, cols)
        total = mixed[1 : 1 + rows, 1 : 1 + cols, :].reshape(size, -1)
        for row_tap in range(3):
            window = shifted[row_tap * cols : row_tap * cols + size, :]
            total = total + jnp.dot(window, taps[sample, row_tap], preferred_element_type=F32)
        block_out[sample] = total.astype(BF16).reshape(rows, cols, -1)


def sums_body(
    count, cells, slots, mixed, wide, affine, back_taps, style_col, demod, weight,
    stats_out, norm_out, grad_out, payload_out, edge, spread, shifted, total,
):
    samples, rows, cols, channels = mixed.shape
    size, span = rows * cols, cols + 2
    mean_all, spread_all = merged(slots, count)
    inverse_all = lax.rsqrt(spread_all * (1.0 / cells) + 1e-05)
    lat_count, row = slots.shape[0], place(LAT)
    below = slots[lax.max(row - 1, 0)].astype(F32)
    above = slots[lax.min(row + 1, lat_count - 1)].astype(F32)
    edge[0] = jnp.where(row > 0, below, 0.0)
    edge[1] = jnp.where(row < lat_count - 1, above, 0.0)
    sums = [[], [], [], []]
    for sample in range(samples):
        mean, inverse = unweave(mean_all, sample), unweave(inverse_all, sample)
        stats_out[sample : sample + 1, :] = mean
        stats_out[samples + sample : samples + sample + 1, :] = inverse
        flat = mixed[sample].reshape(size, channels).astype(F32)
        norm = (flat - mean) * inverse
        pre = norm * affine[0:1, :] + affine[1:2, :]
        sig = 1.0 / (1.0 + jnp.exp(-pre))
        norm_out[sample] = norm
        act = (pre * sig).astype(BF16)
        slope = sig * (1.0 + pre * (1.0 - sig))
        here = slice(8 + sample * span, 8 + (sample + 1) * span)
        spread[0] = edge[0, here, :]
        spread[1 : 1 + rows] = wide[sample]
        spread[1 + rows] = edge[1, here, :]
        windows(spread, shifted, rows, cols)
        style_full = jnp.broadcast_to(style_col[:, sample : sample + 1], (channels, channels))
        demod_row = demod[sample : sample + 1, :]
        both = style_full * demod_row
        product = jnp.zeros((channels, channels), F32)
        grad_act = jnp.zeros((size, channels), F32)
        for row_tap in range(3):
            window = shifted[row_tap * cols : row_tap * cols + size, :]
            grad_act = grad_act + jnp.dot(
                window, back_taps[sample, row_tap], preferred_element_type=F32
            )
            grad = lax.dot_general(
                act, window, (((0,), (0,)), ((), ())), preferred_element_type=F32
            )
            for col_tap in range(3):
                tap = (2 - row_tap) * 3 + 2 - col_tap
                block = grad[:, col_tap * channels : (col_tap + 1) * channels]
                product = product + block * weight[tap]
                here = slice(tap * channels, (tap + 1) * channels)
                part = block * both
                total[here, :] = part if sample == 0 else total[here, :] + part
        grad_pre = grad_act * slope
        grad_out[sample] = grad_pre
        sums[0].append(jnp.sum(product * style_full, axis=0, keepdims=True))
        sums[1].append(jnp.sum((product * demod_row).T, axis=0, keepdims=True))
        sums[2].append(jnp.sum(grad_pre * norm, axis=0, keepdims=True))
        sums[3].append(jnp.sum(grad_pre, axis=0, keepdims=True))
    small = jnp.concatenate(sum(sums, []), axis=0)
    lane = lanes_of(TILE)
    sub = lax.broadcasted_iota(jnp.int32, (TILE, channels), 0)
    quarters = []
    for quarter in range(4):
        turned = pltpu.roll(small, LANES - 32 * quarter, 1) if quarter else small
        piece = jnp.where(lane < 64, turned, pltpu.roll(turned, 64, 1))
        piece = jnp.where((lane & 32) == 0, piece, 0.0)
        quarters.append(split_terms(piece, lane))
    for shard in range(SHARDS):
        main = total[32 * shard : 32 * shard + 32, :]
        start = 8 * channels + 8 * (shard // 2)
        last = total[start : start + 8, :]
        if shard % 2:
            last = pltpu.roll(last, 4, 0)
        extra = quarters[shard % 4][shard // 4 : shard // 4 + 1, :]
        tail = jnp.where(sub < 4, last, jnp.where(sub == 4, extra, 0.0))
        payload_out[shard] = jnp.concatenate([main, tail], axis=0).astype(BF16)


def split_terms(values, lane):
    high = values.astype(BF16).astype(F32)
    return jnp.where(lane < 64, high, values - high)


def resplit(slots):
    row = lax.broadcasted_iota(jnp.int32, slots.shape, slots.ndim - 2)
    lane = lax.broadcasted_iota(jnp.int32, slots.shape, slots.ndim - 1)
    joined = slots + jnp.roll(slots, 64, slots.ndim - 1)
    high = lax.reduce_precision(joined, 8, 7)
    terms = jnp.where(lane < 64, high, joined - high)
    return jnp.where(row == 36, terms, slots).astype(BF16)


def last_body(
    scale, cells, gathered, stats, norm, cotangent, grad_pre, affine, style, style_col, demod,
    power, weight, emb_col, feats_out, weight_out, style_out, gamma_out, beta_out,
):
    samples, tile_rows, tile_cols, channels = cotangent.shape
    size = tile_rows * tile_cols
    lane = lanes_of()
    sub = lax.broadcasted_iota(jnp.int32, (TILE, channels), 0)
    main, tails, small = [], [], []
    for shard in range(SHARDS):
        slot = gathered[shard].astype(F32)
        main.append(slot[0:32, :])
        tails.append(slot[32:40, :])
    for row in range(TILE):
        whole = jnp.zeros((1, channels), F32)
        for quarter in range(4):
            piece = tails[4 * row + quarter][4:5, :]
            piece = piece + pltpu.roll(piece, 64, 1)
            if quarter:
                piece = pltpu.roll(piece, 32 * quarter, 1)
            whole = jnp.where((lane >> 5) == quarter, piece, whole)
        small.append(whole)
    demod_sums, style_sums, gamma_sums, beta_sums = small[0:2], small[2:4], small[4:6], small[6:8]
    gamma = affine[0:1, :]
    gamma_out[...] = scale * (gamma_sums[0] + gamma_sums[1])
    beta_out[...] = scale * (beta_sums[0] + beta_sums[1])
    shrink = jnp.zeros((channels, channels), F32)
    rows = []
    for sample in range(samples):
        demod_row = demod[sample : sample + 1, :]
        pulled = demod_sums[sample] * (demod_row * demod_row * demod_row)
        style_full = jnp.broadcast_to(style_col[:, sample : sample + 1], (channels, channels))
        shrink = shrink + style_full * style_full * pulled
        spent = jnp.sum((power[...] * pulled).T, axis=0, keepdims=True)
        rows.append(style_sums[sample] - style[sample : sample + 1, :] * spent)
    for tap in range(8):
        for part in range(4):
            here = slice(32 * part, 32 * part + 32)
            weight_out[tap, here, :] = scale * (
                main[4 * tap + part] - shrink[here, :] * weight[tap, here, :]
            )
    for pair in range(16):
        here = slice(8 * pair, 8 * pair + 8)
        block = jnp.where(sub < 4, tails[2 * pair], pltpu.roll(tails[2 * pair + 1], 4, 0))
        weight_out[8, here, :] = scale * (block - shrink[here, :] * weight[8, here, :])
    style_out[...] = scale * (emb_col[:, 0:1] * rows[0] + emb_col[:, 1:2] * rows[1])
    for sample in range(samples):
        inverse = stats[samples + sample : samples + sample + 1, :]
        product_mean = group_total(gamma * beta_sums[sample]) * (1.0 / cells)
        squared_mean = group_total(gamma * gamma_sums[sample]) * (1.0 / cells)
        change = inverse * (gamma * grad_pre[sample] - product_mean - norm[sample] * squared_mean)
        out = cotangent[sample].reshape(size, channels).astype(F32) + change
        feats_out[sample] = out.astype(BF16).reshape(tile_rows, tile_cols, channels)


def on_device(
    feats, cond, null_field, drop_flags, emb, style_weight, conv_weight, gamma, beta, cotangent
):
    samples, tile_rows, tile_cols, channels = feats.shape
    group_size = channels // GROUPS
    lat_count, lon_count = lax.axis_size(LAT), lax.axis_size(LON)
    devices_all = lat_count * lon_count
    cells_local = tile_rows * tile_cols * group_size
    cells_per_group = cells_local * devices_all
    scale_gradient = 1.0 / math.sqrt(samples * tile_rows * tile_cols * devices_all)
    taps = conv_weight.reshape(9, channels, channels)

    anywhere, whole = pl.BlockSpec(memory_space=pl.ANY), pl.BlockSpec(memory_space=pltpu.VMEM)
    head = 8
    lon_slot = head + samples * tile_rows
    lat_slot = -(-(head + samples * (tile_cols + 2)) // 16) * 16
    mixed, slots = call(
        mix_body,
        (array(feats.shape, BF16), array((lon_count, lon_slot, LANES), BF16)),
        (
            pltpu.VMEM(feats.shape, BF16),
            pltpu.VMEM(feats.shape, BF16),
            pltpu.VMEM(null_field.shape, BF16),
            pltpu.VMEM(feats.shape, BF16),
            pltpu.SemaphoreType.DMA((4,)),
        ),
        room=60,
        in_specs=[anywhere] * 4 + [whole],
    )(feats, cond, null_field, cotangent, drop_flags)
    slots = exchange(slots, LON)
    wide_cot, slots = call(
        functools.partial(merge_body, cells_local),
        (
            array((samples, tile_rows, tile_cols + 2, channels)),
            array((lat_count, lat_slot, LANES), BF16),
        ),
        (pltpu.VMEM((lat_slot, LANES), F32),),
    )(slots, cotangent)
    slots = exchange(slots, LAT)
    affine = jnp.stack([gamma, beta])

    style = 1.0 + jnp.dot(emb, style_weight, precision=lax.Precision.HIGHEST)
    power = jnp.sum(conv_weight * conv_weight, axis=(0, 1))
    demod = lax.rsqrt(jnp.dot(style * style, power, precision=lax.Precision.HIGHEST) + 1e-08)
    modded = conv_weight[None] * style[:, None, None, :, None]
    w_eff = (modded * demod[:, None, None, None, :]).astype(BF16)
    taps_shape = (samples, 3, 3 * channels, channels)
    back_taps = jnp.swapaxes(w_eff[:, ::-1, ::-1], 3, 4).reshape(taps_shape)
    spread = pltpu.VMEM((tile_rows + 2, tile_cols + 2, channels), F32)
    shifted = pltpu.VMEM(((tile_rows + 2) * tile_cols, 3 * channels), BF16)
    flat = (samples, tile_rows * tile_cols, channels)
    style_col = style.T
    stats, norm, grad_pre, payload = call(
        functools.partial(sums_body, cells_local * lon_count, cells_per_group),
        (
            array((2 * samples, LANES)),
            array(flat),
            array(flat),
            array((SHARDS, SLOT, LANES), BF16),
        ),
        (
            pltpu.VMEM((2, lat_slot, LANES), F32),
            spread,
            shifted,
            pltpu.VMEM((9 * channels, channels), F32),
        ),
    )(slots, mixed, wide_cot, affine, back_taps, style_col, demod, taps)

    core_count, near_count = lax.axis_size("c"), lax.axis_size(NEAR)
    payload = lax.all_gather(payload, "c")
    payload = payload.reshape(core_count, core_count, near_count, SLOT, LANES)
    payload = lax.dynamic_index_in_dim(payload, lax.axis_index("c"), 1, False)
    payload = resplit(jnp.sum(payload.astype(F32), axis=0))
    payload, mixed = lax.optimization_barrier((payload, mixed))
    low, high = shift(mixed[:, :, -1:], LON, 1, True), shift(mixed[:, :, :1], LON, -1, True)
    payload = resplit(jnp.sum(exchange(payload, NEAR).astype(F32), axis=0))
    payload, low, high = lax.optimization_barrier((payload, low, high))
    padded = jnp.concatenate([low, mixed, high], axis=2)
    low, high = shift(padded[:, -1:], LAT, 1, False), shift(padded[:, :1], LAT, -1, False)
    payload = resplit(jnp.sum(everyone(payload, LAT).astype(F32), axis=0))
    payload, low, high = lax.optimization_barrier((payload, low, high))
    padded = jnp.concatenate([low, padded, high], axis=1)
    payload = lax.all_gather(everyone(payload, NEAR), "c")

    lat_at = lax.axis_index(LAT)
    inside = jnp.stack([lat_at > 0, lat_at < lat_count - 1])
    keep = jnp.broadcast_to(inside.astype(F32)[:, None], (2, LANES))
    block_out = call(forward_body, array(feats.shape, BF16), (spread, shifted))(
        padded, w_eff.reshape(taps_shape), stats, affine, keep
    )

    grad_feats, grad_weight, grad_style, grad_gamma, grad_beta = call(
        functools.partial(last_body, scale_gradient, cells_per_group),
        (
            array(feats.shape, BF16),
            array(taps.shape),
            array(style_weight.shape),
            array((1, LANES)),
            array((1, LANES)),
        ),
    )(
        payload.reshape(SHARDS, SLOT, LANES), stats, norm, cotangent, grad_pre, affine, style,
        style_col, demod, power, taps, emb.T,
    )
    return (
        block_out,
        grad_feats,
        grad_weight.reshape(conv_weight.shape),
        grad_style,
        grad_gamma[0],
        grad_beta[0],
    )


def solution(mesh):
    parts = Mesh(mesh.devices.reshape(4, 4, 2, 8, 2), LAT + LON)
    tile = P(None, LAT, LON, None)
    placed = (tile, tile, P(LAT, LON, None), P(), P(), P(), P(), P(), P(), tile)
    return jax.shard_map(
        on_device,
        mesh=parts,
        in_specs=placed,
        out_specs=(tile, tile, P(), P(), P(), P()),
        check_vma=False,
    )
```

```python
import functools
import math

import jax
import jax.numpy as jnp
from jax import lax
from jax.experimental import pallas as pl
from jax.experimental.pallas import tpu as pltpu
from jax.sharding import Mesh, PartitionSpec as P

GROUPS = 32
LAT = ("zh", "x")
LON = ("zl", "y", "c")
NEAR = ("zl", "y")
F32 = jnp.float32
BF16 = jnp.bfloat16
TILE = 8
SHARDS = 32
SLOT = 40
LANES = 128


def shift(block, axes, step, periodic):
    count = lax.axis_size(axes)
    pairs = [(i, i + step) for i in range(count)]
    if periodic:
        pairs = [(source, target % count) for source, target in pairs]
    else:
        pairs = [(source, target) for source, target in pairs if 0 <= target < count]
    return lax.ppermute(block, axes, pairs)


def extend(block, axes, dim, periodic):
    last = block.shape[dim] - 1
    low = shift(lax.slice_in_dim(block, last, last + 1, axis=dim), axes, 1, periodic)
    high = shift(lax.slice_in_dim(block, 0, 1, axis=dim), axes, -1, periodic)
    return jnp.concatenate([low, block, high], axis=dim)


def exchange(block, axes):
    return lax.all_to_all(block, axes, 0, 0)


def everyone(block, axes):
    return exchange(jnp.broadcast_to(block[None], (lax.axis_size(axes),) + block.shape), axes)


def call(body, outputs, scratch=(), room=48, **more):
    return pl.pallas_call(
        body,
        out_shape=outputs,
        scratch_shapes=list(scratch),
        **more,
        compiler_params=pltpu.CompilerParams(vmem_limit_bytes=room * 1024 * 1024),
    )


def array(shape, dtype=F32):
    return jax.ShapeDtypeStruct(shape, dtype)


def lanes_of(rows=1):
    return lax.broadcasted_iota(jnp.int32, (rows, LANES), 1)


def group_total(row):
    lane = lanes_of()
    for step in (1, 2):
        after, before = pltpu.roll(row, LANES - step, 1), pltpu.roll(row, step, 1)
        row = row + jnp.where((lane & step) == 0, after, before)
    return row


def weave(first, second):
    return jnp.where((lanes_of() & 1) == 0, first, second)


def unweave(row, sample):
    if sample == 0:
        return weave(row, pltpu.roll(row, 1, 1))
    return weave(pltpu.roll(row, LANES - 1, 1), row)


def place(axes):
    index = 0
    for axis in axes:
        index = index * lax.axis_size(axis) + lax.axis_index(axis)
    return index


def three_terms(value):
    terms = []
    for _ in range(3):
        terms.append(value.astype(BF16).astype(F32))
        value = value - terms[-1]
    return terms


def merged(slots, count):
    rows = slots[:, 0:8, :].astype(F32)
    means = rows[:, 0:1, :] + rows[:, 1:2, :] + rows[:, 2:3, :]
    spreads = rows[:, 3:4, :] + rows[:, 4:5, :] + rows[:, 5:6, :]
    mean = jnp.mean(means, axis=0)
    away = means - mean[None]
    return mean, jnp.sum(spreads + count * away * away, axis=0)


def header(mean, spread):
    return three_terms(mean) + three_terms(spread) + [jnp.zeros((2, LANES), F32)]


def mix_body(
    feats_in, cond_in, null_in, cot_in, flags, mixed_out, slots_out,
    feats, cond, null, cot, arrivals,
):
    copies = []
    for at, (source, target) in enumerate(
        ((null_in, null), (feats_in, feats), (cond_in, cond), (cot_in, cot))
    ):
        copies.append(pltpu.make_async_copy(source, target, arrivals.at[at]))
        copies[-1].start()
    for copy in copies[:3]:
        copy.wait()
    samples, tile_rows, tile_cols, channels = feats.shape
    cells = tile_rows * tile_cols
    size = cells * (channels // GROUPS)
    null32 = null[...].astype(F32)
    means, spreads = [], []
    for sample in range(samples):
        dropped = flags[sample : sample + 1, :].astype(F32).reshape(1, 1, channels)
        mixed = (
            feats[sample].astype(F32) + dropped * null32 + (1.0 - dropped) * cond[sample].astype(F32)
        ).astype(BF16)
        mixed_out[sample] = mixed
        wide = mixed.astype(F32).reshape(cells, channels)
        mean = group_total(jnp.sum(wide, axis=0, keepdims=True)) * (1.0 / size)
        away = wide - mean
        means.append(mean)
        spreads.append(group_total(jnp.sum(away * away, axis=0, keepdims=True)))
    rows = header(weave(*means), weave(*spreads))
    copies[3].wait()
    firsts, lasts = [], []
    for sample in range(samples):
        wide = cot[sample].astype(F32)
        firsts.append(wide[:, 0, :])
        lasts.append(wide[:, tile_cols - 1, :])
    slots_out[...] = jnp.broadcast_to(
        jnp.concatenate(rows + firsts, axis=0).astype(BF16)[None], slots_out.shape
    )
    after = lax.rem(place(LON) + 1, slots_out.shape[0])
    slots_out[after] = jnp.concatenate(rows + lasts, axis=0).astype(BF16)


def merge_body(count, slots, cot, wide_out, slots_out, edge):
    samples, tile_rows, tile_cols, channels = cot.shape
    lon_count, lat_count = slots.shape[0], slots_out.shape[0]
    mean, spread = merged(slots, count)
    me = place(LON)
    before = slots[lax.rem(me + lon_count - 1, lon_count)].astype(F32)
    after = slots[lax.rem(me + 1, lon_count)].astype(F32)
    for sample in range(samples):
        here = slice(8 + sample * tile_rows, 8 + (sample + 1) * tile_rows)
        wide_out[sample, :, 0, :] = before[here, :]
        wide_out[sample, :, 1 : 1 + tile_cols, :] = cot[sample].astype(F32)
        wide_out[sample, :, 1 + tile_cols, :] = after[here, :]
    edge[...] = jnp.zeros(edge.shape, F32)
    edge[0:8, :] = jnp.concatenate(header(mean, spread), axis=0)
    span = tile_cols + 2
    for sample in range(samples):
        edge[8 + sample * span : 8 + (sample + 1) * span, :] = wide_out[sample, 0]
    slots_out[...] = jnp.broadcast_to(edge[...].astype(BF16)[None], slots_out.shape)
    for sample in range(samples):
        edge[8 + sample * span : 8 + (sample + 1) * span, :] = wide_out[sample, tile_rows - 1]
    row = place(LAT)

    @pl.when(row < lat_count - 1)
    def _():
        slots_out[row + 1] = edge[...].astype(BF16)


def weights_body(
    emb, style_weight, weight, style_out, column_out, demod_out, power_out, emb_out, back_out, taps_out,
):
    samples, channels = emb.shape[0], weight.shape[2]
    exact = lax.Precision.HIGHEST
    style = 1.0 + jnp.dot(
        emb[...], style_weight[...], precision=exact, preferred_element_type=F32
    )
    power = jnp.zeros((channels, channels), F32)
    for tap in range(9):
        power = power + weight[tap] * weight[tap]
    squares = jnp.dot(style * style, power, precision=exact, preferred_element_type=F32)
    demod = lax.rsqrt(squares + 1e-08)
    style_out[...] = style
    demod_out[...] = demod
    power_out[...] = power
    for sample in range(samples):
        here = slice(sample, sample + 1)
        column = jnp.broadcast_to(style[here, :], (channels, channels)).T
        column_out[sample] = column
        emb_out[sample] = jnp.broadcast_to(emb[here, :], (channels, emb.shape[1])).T
        for tap in range(9):
            row, col = tap // 3, tap % 3
            block = weight[tap] * column * demod[here, :]
            taps_out[sample, row, col * channels : (col + 1) * channels, :] = block.astype(BF16)
            row, col = 2 - row, 2 - col
            back_out[sample, row, col * channels : (col + 1) * channels, :] = block.T.astype(BF16)


def windows(spread, shifted, rows, cols):
    channels = spread.shape[-1]
    for tap in range(3):
        moved = spread[:, tap : tap + cols, :].reshape((rows + 2) * cols, channels)
        shifted[:, tap * channels : (tap + 1) * channels] = moved.astype(BF16)


def forward_body(padded, taps, stats, gamma, beta, block_out, spread, shifted):
    samples, rows, cols = padded.shape[0], padded.shape[1] - 2, padded.shape[2] - 2
    size = rows * cols
    row = lax.broadcasted_iota(jnp.int32, spread.shape, 0) + place(LAT) * rows
    inside = (row > 0) & (row <= rows * lax.axis_size(LAT))
    for sample in range(samples):
        mixed = padded[sample].astype(F32)
        mean = stats[sample : sample + 1, :][None]
        inverse = stats[samples + sample : samples + sample + 1, :][None]
        pre = (mixed - mean) * inverse * gamma[...][None] + beta[...][None]
        act = jnp.where(inside, pre / (1.0 + jnp.exp(-pre)), 0.0)
        spread[...] = act
        windows(spread, shifted, rows, cols)
        total = mixed[1 : 1 + rows, 1 : 1 + cols, :].reshape(size, -1)
        for row_tap in range(3):
            window = shifted[row_tap * cols : row_tap * cols + size, :]
            total = total + jnp.dot(window, taps[sample, row_tap], preferred_element_type=F32)
        block_out[sample] = total.astype(BF16).reshape(rows, cols, -1)


def sums_body(
    count, cells, slots, mixed, wide, gamma, beta, back_taps, column, demod, weight,
    stats_out, norm_out, grad_out, payload_out, edge, spread, shifted, total,
):
    samples, rows, cols, channels = mixed.shape
    size, span = rows * cols, cols + 2
    mean_all, spread_all = merged(slots, count)
    inverse_all = lax.rsqrt(spread_all * (1.0 / cells) + 1e-05)
    lat_count, row = slots.shape[0], place(LAT)
    below = slots[lax.max(row - 1, 0)].astype(F32)
    above = slots[lax.min(row + 1, lat_count - 1)].astype(F32)
    edge[0] = jnp.where(row > 0, below, 0.0)
    edge[1] = jnp.where(row < lat_count - 1, above, 0.0)
    sums = [[], [], [], []]
    for sample in range(samples):
        mean, inverse = unweave(mean_all, sample), unweave(inverse_all, sample)
        stats_out[sample : sample + 1, :] = mean
        stats_out[samples + sample : samples + sample + 1, :] = inverse
        flat = mixed[sample].reshape(size, channels).astype(F32)
        norm = (flat - mean) * inverse
        pre = norm * gamma[...] + beta[...]
        sig = 1.0 / (1.0 + jnp.exp(-pre))
        norm_out[sample] = norm
        act = (pre * sig).astype(BF16)
        slope = sig * (1.0 + pre * (1.0 - sig))
        here = slice(8 + sample * span, 8 + (sample + 1) * span)
        spread[0] = edge[0, here, :]
        spread[1 : 1 + rows] = wide[sample]
        spread[1 + rows] = edge[1, here, :]
        windows(spread, shifted, rows, cols)
        style_full = column[sample]
        demod_row = demod[sample : sample + 1, :]
        both = style_full * demod_row
        product = jnp.zeros((channels, channels), F32)
        grad_act = jnp.zeros((size, channels), F32)
        for row_tap in range(3):
            window = shifted[row_tap * cols : row_tap * cols + size, :]
            grad_act = grad_act + jnp.dot(
                window, back_taps[sample, row_tap], preferred_element_type=F32
            )
            grad = lax.dot_general(
                act, window, (((0,), (0,)), ((), ())), preferred_element_type=F32
            )
            for col_tap in range(3):
                tap = (2 - row_tap) * 3 + 2 - col_tap
                block = grad[:, col_tap * channels : (col_tap + 1) * channels]
                product = product + block * weight[tap]
                here = slice(tap * channels, (tap + 1) * channels)
                part = block * both
                total[here, :] = part if sample == 0 else total[here, :] + part
        grad_pre = grad_act * slope
        grad_out[sample] = grad_pre
        sums[0].append(jnp.sum(product * style_full, axis=0, keepdims=True))
        sums[1].append(jnp.sum((product * demod_row).T, axis=0, keepdims=True))
        sums[2].append(jnp.sum(grad_pre * norm, axis=0, keepdims=True))
        sums[3].append(jnp.sum(grad_pre, axis=0, keepdims=True))
    small = jnp.concatenate(sum(sums, []), axis=0)
    lane = lanes_of(TILE)
    sub = lax.broadcasted_iota(jnp.int32, (TILE, channels), 0)
    quarters = []
    for quarter in range(4):
        turned = pltpu.roll(small, LANES - 32 * quarter, 1) if quarter else small
        piece = jnp.where(lane < 64, turned, pltpu.roll(turned, 64, 1))
        piece = jnp.where((lane & 32) == 0, piece, 0.0)
        quarters.append(split_terms(piece, lane))
    for shard in range(SHARDS):
        main = total[32 * shard : 32 * shard + 32, :]
        start = 8 * channels + 8 * (shard // 2)
        last = total[start : start + 8, :]
        if shard % 2:
            last = pltpu.roll(last, 4, 0)
        extra = quarters[shard % 4][shard // 4 : shard // 4 + 1, :]
        tail = jnp.where(sub < 4, last, jnp.where(sub == 4, extra, 0.0))
        payload_out[shard] = jnp.concatenate([main, tail], axis=0).astype(BF16)


def split_terms(values, lane):
    high = values.astype(BF16).astype(F32)
    return jnp.where(lane < 64, high, values - high)


def resplit(slots):
    row = lax.broadcasted_iota(jnp.int32, slots.shape, slots.ndim - 2)
    lane = lax.broadcasted_iota(jnp.int32, slots.shape, slots.ndim - 1)
    joined = slots + jnp.roll(slots, 64, slots.ndim - 1)
    high = lax.reduce_precision(joined, 8, 7)
    terms = jnp.where(lane < 64, high, joined - high)
    return jnp.where(row == 36, terms, slots).astype(BF16)


def last_body(
    scale, cells, gathered, stats, norm, cotangent, grad_pre, gamma, style, column, demod,
    power, weight, emb_full, feats_out, weight_out, style_out, gamma_out, beta_out,
):
    samples, tile_rows, tile_cols, channels = cotangent.shape
    size = tile_rows * tile_cols
    lane = lanes_of()
    sub = lax.broadcasted_iota(jnp.int32, (TILE, channels), 0)
    main, tails, small = [], [], []
    for shard in range(SHARDS):
        slot = gathered[shard].astype(F32)
        main.append(slot[0:32, :])
        tails.append(slot[32:40, :])
    for row in range(TILE):
        whole = jnp.zeros((1, channels), F32)
        for quarter in range(4):
            piece = tails[4 * row + quarter][4:5, :]
            piece = piece + pltpu.roll(piece, 64, 1)
            if quarter:
                piece = pltpu.roll(piece, 32 * quarter, 1)
            whole = jnp.where((lane >> 5) == quarter, piece, whole)
        small.append(whole)
    demod_sums, style_sums, gamma_sums, beta_sums = small[0:2], small[2:4], small[4:6], small[6:8]
    gain = gamma[...]
    gamma_out[...] = scale * (gamma_sums[0] + gamma_sums[1])
    beta_out[...] = scale * (beta_sums[0] + beta_sums[1])
    shrink = jnp.zeros((channels, channels), F32)
    rows = []
    for sample in range(samples):
        demod_row = demod[sample : sample + 1, :]
        pulled = demod_sums[sample] * (demod_row * demod_row * demod_row)
        style_full = column[sample]
        shrink = shrink + style_full * style_full * pulled
        spent = jnp.sum((power[...] * pulled).T, axis=0, keepdims=True)
        rows.append(style_sums[sample] - style[sample : sample + 1, :] * spent)
    for tap in range(8):
        for part in range(4):
            here = slice(32 * part, 32 * part + 32)
            weight_out[tap, here, :] = scale * (
                main[4 * tap + part] - shrink[here, :] * weight[tap, here, :]
            )
    for pair in range(16):
        here = slice(8 * pair, 8 * pair + 8)
        block = jnp.where(sub < 4, tails[2 * pair], pltpu.roll(tails[2 * pair + 1], 4, 0))
        weight_out[8, here, :] = scale * (block - shrink[here, :] * weight[8, here, :])
    style_out[...] = scale * (emb_full[0] * rows[0] + emb_full[1] * rows[1])
    for sample in range(samples):
        inverse = stats[samples + sample : samples + sample + 1, :]
        product_mean = group_total(gain * beta_sums[sample]) * (1.0 / cells)
        squared_mean = group_total(gain * gamma_sums[sample]) * (1.0 / cells)
        change = inverse * (gain * grad_pre[sample] - product_mean - norm[sample] * squared_mean)
        out = cotangent[sample].reshape(size, channels).astype(F32) + change
        feats_out[sample] = out.astype(BF16).reshape(tile_rows, tile_cols, channels)


def on_device(
    feats, cond, null_field, drop_flags, emb, style_weight, conv_weight, gamma, beta, cotangent
):
    samples, tile_rows, tile_cols, channels = feats.shape
    group_size = channels // GROUPS
    lat_count, lon_count = lax.axis_size(LAT), lax.axis_size(LON)
    devices_all = lat_count * lon_count
    cells_local = tile_rows * tile_cols * group_size
    cells_per_group = cells_local * devices_all
    scale_gradient = 1.0 / math.sqrt(samples * tile_rows * tile_cols * devices_all)
    taps = conv_weight.reshape(9, channels, channels)

    anywhere, whole = pl.BlockSpec(memory_space=pl.ANY), pl.BlockSpec(memory_space=pltpu.VMEM)
    head = 8
    lon_slot = head + samples * tile_rows
    lat_slot = -(-(head + samples * (tile_cols + 2)) // 16) * 16
    mixed, slots = call(
        mix_body,
        (array(feats.shape, BF16), array((lon_count, lon_slot, LANES), BF16)),
        (
            pltpu.VMEM(feats.shape, BF16),
            pltpu.VMEM(feats.shape, BF16),
            pltpu.VMEM(null_field.shape, BF16),
            pltpu.VMEM(feats.shape, BF16),
            pltpu.SemaphoreType.DMA((4,)),
        ),
        room=60,
        in_specs=[anywhere] * 4 + [whole],
    )(feats, cond, null_field, cotangent, drop_flags)
    slots = exchange(slots, LON)
    low, high = shift(mixed[:, :, -1:], LON, 1, True), shift(mixed[:, :, :1], LON, -1, True)
    wide_cot, slots = call(
        functools.partial(merge_body, cells_local),
        (
            array((samples, tile_rows, tile_cols + 2, channels)),
            array((lat_count, lat_slot, LANES), BF16),
        ),
        (pltpu.VMEM((lat_slot, LANES), F32),),
    )(slots, cotangent)
    slots, low, high = lax.optimization_barrier((slots, low, high))
    slots = exchange(slots, LAT)
    padded = jnp.concatenate([low, mixed, high], axis=2)
    low, high = shift(padded[:, -1:], LAT, 1, False), shift(padded[:, :1], LAT, -1, False)
    gamma, beta = gamma[None], beta[None]

    taps_shape = (samples, 3, 3 * channels, channels)
    style, column, demod, power, emb_full, back_taps, fore_taps = call(
        weights_body,
        (
            array((samples, channels)),
            array((samples, channels, channels)),
            array((samples, channels)),
            array((channels, channels)),
            array((samples,) + style_weight.shape),
            array(taps_shape, BF16),
            array(taps_shape, BF16),
        ),
    )(emb, style_weight, taps)
    spread = pltpu.VMEM((tile_rows + 2, tile_cols + 2, channels), F32)
    shifted = pltpu.VMEM(((tile_rows + 2) * tile_cols, 3 * channels), BF16)
    flat = (samples, tile_rows * tile_cols, channels)
    stats, norm, grad_pre, payload = call(
        functools.partial(sums_body, cells_local * lon_count, cells_per_group),
        (
            array((2 * samples, LANES)),
            array(flat),
            array(flat),
            array((SHARDS, SLOT, LANES), BF16),
        ),
        (
            pltpu.VMEM((2, lat_slot, LANES), F32),
            spread,
            shifted,
            pltpu.VMEM((9 * channels, channels), F32),
        ),
    )(slots, mixed, wide_cot, gamma, beta, back_taps, column, demod, taps)

    payload, low, high = lax.optimization_barrier((payload, low, high))
    padded = jnp.concatenate([low, padded, high], axis=1)
    core_count, near_count = lax.axis_size("c"), lax.axis_size(NEAR)
    payload = lax.all_gather(payload, "c")
    payload = payload.reshape(core_count, core_count, near_count, SLOT, LANES)
    payload = lax.dynamic_index_in_dim(payload, lax.axis_index("c"), 1, False)
    payload = resplit(jnp.sum(payload.astype(F32), axis=0))
    payload = resplit(jnp.sum(exchange(payload, NEAR).astype(F32), axis=0))
    payload = resplit(jnp.sum(everyone(payload, LAT).astype(F32), axis=0))
    payload = lax.all_gather(everyone(payload, NEAR), "c")

    block_out = call(forward_body, array(feats.shape, BF16), (spread, shifted))(
        padded, fore_taps, stats, gamma, beta
    )

    grad_feats, grad_weight, grad_style, grad_gamma, grad_beta = call(
        functools.partial(last_body, scale_gradient, cells_per_group),
        (
            array(feats.shape, BF16),
            array(taps.shape),
            array(style_weight.shape),
            array((1, LANES)),
            array((1, LANES)),
        ),
    )(
        payload.reshape(SHARDS, SLOT, LANES), stats, norm, cotangent, grad_pre, gamma, style,
        column, demod, power, taps, emb_full,
    )
    return (
        block_out,
        grad_feats,
        grad_weight.reshape(conv_weight.shape),
        grad_style,
        grad_gamma[0],
        grad_beta[0],
    )


def solution(mesh):
    parts = Mesh(mesh.devices.reshape(4, 4, 2, 8, 2), LAT + LON)
    tile = P(None, LAT, LON, None)
    placed = (tile, tile, P(LAT, LON, None), P(), P(), P(), P(), P(), P(), tile)
    return jax.shard_map(
        on_device,
        mesh=parts,
        in_specs=placed,
        out_specs=(tile, tile, P(), P(), P(), P()),
        check_vma=False,
    )
```

```python
import functools
import math

import jax
import jax.numpy as jnp
from jax import lax
from jax.experimental import pallas as pl
from jax.experimental.pallas import tpu as pltpu
from jax.sharding import Mesh, PartitionSpec as P

GROUPS = 32
LAT = ("zh", "x")
LON = ("zl", "y", "c")
NEAR = ("zl", "y")
F32 = jnp.float32
BF16 = jnp.bfloat16
TILE = 8
SHARDS = 32
SLOT = 40
LANES = 128


def shift(block, axes, step, periodic):
    count = lax.axis_size(axes)
    pairs = [(i, i + step) for i in range(count)]
    if periodic:
        pairs = [(source, target % count) for source, target in pairs]
    else:
        pairs = [(source, target) for source, target in pairs if 0 <= target < count]
    return lax.ppermute(block, axes, pairs)


def extend(block, axes, dim, periodic):
    last = block.shape[dim] - 1
    low = shift(lax.slice_in_dim(block, last, last + 1, axis=dim), axes, 1, periodic)
    high = shift(lax.slice_in_dim(block, 0, 1, axis=dim), axes, -1, periodic)
    return jnp.concatenate([low, block, high], axis=dim)


def exchange(block, axes):
    return lax.all_to_all(block, axes, 0, 0)


def everyone(block, axes):
    return exchange(jnp.broadcast_to(block[None], (lax.axis_size(axes),) + block.shape), axes)


def call(body, outputs, scratch=(), room=48, **more):
    return pl.pallas_call(
        body,
        out_shape=outputs,
        scratch_shapes=list(scratch),
        **more,
        compiler_params=pltpu.CompilerParams(vmem_limit_bytes=room * 1024 * 1024),
    )


def array(shape, dtype=F32):
    return jax.ShapeDtypeStruct(shape, dtype)


def lanes_of(rows=1):
    return lax.broadcasted_iota(jnp.int32, (rows, LANES), 1)


def group_total(row):
    lane = lanes_of()
    for step in (1, 2):
        after, before = pltpu.roll(row, LANES - step, 1), pltpu.roll(row, step, 1)
        row = row + jnp.where((lane & step) == 0, after, before)
    return row


def weave(first, second):
    return jnp.where((lanes_of() & 1) == 0, first, second)


def unweave(row, sample):
    if sample == 0:
        return weave(row, pltpu.roll(row, 1, 1))
    return weave(pltpu.roll(row, LANES - 1, 1), row)


def place(axes):
    index = 0
    for axis in axes:
        index = index * lax.axis_size(axis) + lax.axis_index(axis)
    return index


def three_terms(value):
    terms = []
    for _ in range(3):
        terms.append(value.astype(BF16).astype(F32))
        value = value - terms[-1]
    return terms


def merged(slots, count):
    rows = slots[:, 0:8, :].astype(F32)
    means = rows[:, 0:1, :] + rows[:, 1:2, :] + rows[:, 2:3, :]
    spreads = rows[:, 3:4, :] + rows[:, 4:5, :] + rows[:, 5:6, :]
    mean = jnp.mean(means, axis=0)
    away = means - mean[None]
    return mean, jnp.sum(spreads + count * away * away, axis=0)


def header(mean, spread):
    return three_terms(mean) + three_terms(spread) + [jnp.zeros((2, LANES), F32)]


def fetcher(arrivals):
    used = iter(range(arrivals.shape[0]))

    def fetch(source, target):
        copy = pltpu.make_async_copy(source, target, arrivals.at[next(used)])
        copy.start()
        return copy

    return fetch


def mix_body(
    feats_in, cond_in, null_in, cot_in, flags_in, mixed_out, moments_out, first_out, last_out,
    feats, cond, null, cot, flags, arrivals,
):
    fetch = fetcher(arrivals)
    flags_copy, null_copy = fetch(flags_in, flags), fetch(null_in, null)
    field_copies = [
        (fetch(feats_in.at[sample], feats.at[sample]), fetch(cond_in.at[sample], cond.at[sample]))
        for sample in range(feats.shape[0])
    ]
    cot_copy = fetch(cot_in, cot)
    flags_copy.wait()
    null_copy.wait()
    samples, tile_rows, tile_cols, channels = feats.shape
    cells = tile_rows * tile_cols
    size = cells * (channels // GROUPS)
    null32 = null[...].astype(F32)
    means, spreads = [], []
    for sample in range(samples):
        for copy in field_copies[sample]:
            copy.wait()
        dropped = flags[sample : sample + 1, :].astype(F32).reshape(1, 1, channels)
        mixed = (
            feats[sample].astype(F32) + dropped * null32 + (1.0 - dropped) * cond[sample].astype(F32)
        ).astype(BF16)
        mixed_out[sample] = mixed
        wide = mixed.astype(F32)
        first_out[0, sample] = wide[:, 0, :].astype(BF16)
        last_out[0, sample] = wide[:, tile_cols - 1, :].astype(BF16)
        wide = wide.reshape(cells, channels)
        mean = group_total(jnp.sum(wide, axis=0, keepdims=True)) * (1.0 / size)
        away = wide - mean
        means.append(mean)
        spreads.append(group_total(jnp.sum(away * away, axis=0, keepdims=True)))
    moments = jnp.concatenate([weave(*means), weave(*spreads)], axis=0)
    moments_out[...] = jnp.broadcast_to(moments[None], moments_out.shape)
    cot_copy.wait()
    for sample in range(samples):
        wide = cot[sample].astype(F32)
        first_out[1, sample] = wide[:, 0, :].astype(BF16)
        last_out[1, sample] = wide[:, tile_cols - 1, :].astype(BF16)


def build_body(moments, low, high, cot, wide_out, slots_out, edge):
    samples, tile_rows, tile_cols, channels = cot.shape
    lat_count = slots_out.shape[0]
    for sample in range(samples):
        wide_out[sample, :, 0, :] = low[1, sample].astype(F32)
        wide_out[sample, :, 1 : 1 + tile_cols, :] = cot[sample].astype(F32)
        wide_out[sample, :, 1 + tile_cols, :] = high[1, sample].astype(F32)
    edge[...] = jnp.zeros(edge.shape, F32)
    edge[0:8, :] = jnp.concatenate(header(moments[0:1, :], moments[1:2, :]), axis=0)
    span = tile_cols + 2
    for sample in range(samples):
        edge[8 + sample * span : 8 + (sample + 1) * span, :] = wide_out[sample, 0]
    slots_out[...] = jnp.broadcast_to(edge[...].astype(BF16)[None], slots_out.shape)
    for sample in range(samples):
        edge[8 + sample * span : 8 + (sample + 1) * span, :] = wide_out[sample, tile_rows - 1]
    row = place(LAT)

    @pl.when(row < lat_count - 1)
    def _():
        slots_out[row + 1] = edge[...].astype(BF16)


def weights_body(
    emb, style_weight, gamma, beta, weight,
    gamma_out, beta_out, style_out, column_out, demod_out, power_out, emb_out, back_out, taps_out,
):
    gamma_out[...] = gamma[...]
    beta_out[...] = beta[...]
    power = jnp.zeros(weight.shape[1:], F32)
    for tap in range(9):
        power = power + weight[tap] * weight[tap]
    samples, channels = emb.shape[0], weight.shape[2]
    exact = lax.Precision.HIGHEST
    style = 1.0 + jnp.dot(
        emb[...], style_weight[...], precision=exact, preferred_element_type=F32
    )
    squares = jnp.dot(style * style, power, precision=exact, preferred_element_type=F32)
    demod = lax.rsqrt(squares + 1e-08)
    style_out[...] = style
    demod_out[...] = demod
    power_out[...] = power
    for sample in range(samples):
        here = slice(sample, sample + 1)
        column = jnp.broadcast_to(style[here, :], (channels, channels)).T
        column_out[sample] = column
        emb_out[sample] = jnp.broadcast_to(emb[here, :], (channels, emb.shape[1])).T
        for tap in range(9):
            row, col = tap // 3, tap % 3
            block = weight[tap] * column * demod[here, :]
            taps_out[sample, row, col * channels : (col + 1) * channels, :] = block.astype(BF16)
            row, col = 2 - row, 2 - col
            back_out[sample, row, col * channels : (col + 1) * channels, :] = block.T.astype(BF16)


def windows(spread, shifted, rows, cols):
    channels = spread.shape[-1]
    for tap in range(3):
        moved = spread[:, tap : tap + cols, :].reshape((rows + 2) * cols, channels)
        shifted[:, tap * channels : (tap + 1) * channels] = moved.astype(BF16)


def forward_body(padded, taps, stats, gamma, beta, block_out, spread, shifted):
    samples, rows, cols = padded.shape[0], padded.shape[1] - 2, padded.shape[2] - 2
    size = rows * cols
    row = lax.broadcasted_iota(jnp.int32, spread.shape, 0) + place(LAT) * rows
    inside = (row > 0) & (row <= rows * lax.axis_size(LAT))
    for sample in range(samples):
        mixed = padded[sample].astype(F32)
        mean = stats[sample : sample + 1, :][None]
        inverse = stats[samples + sample : samples + sample + 1, :][None]
        pre = (mixed - mean) * inverse * gamma[...][None] + beta[...][None]
        act = jnp.where(inside, pre / (1.0 + jnp.exp(-pre)), 0.0)
        spread[...] = act
        windows(spread, shifted, rows, cols)
        total = mixed[1 : 1 + rows, 1 : 1 + cols, :].reshape(size, -1)
        for row_tap in range(3):
            window = shifted[row_tap * cols : row_tap * cols + size, :]
            total = total + jnp.dot(window, taps[sample, row_tap], preferred_element_type=F32)
        block_out[sample] = total.astype(BF16).reshape(rows, cols, -1)


def sums_body(
    count, cells, slots, mixed, wide, gamma, beta, back_taps, column, demod, weight,
    stats_out, norm_out, grad_out, payload_out, edge, spread, shifted, total,
):
    samples, rows, cols, channels = mixed.shape
    size, span = rows * cols, cols + 2
    mean_all, spread_all = merged(slots, count)
    inverse_all = lax.rsqrt(spread_all * (1.0 / cells) + 1e-05)
    lat_count, row = slots.shape[0], place(LAT)
    below = slots[lax.max(row - 1, 0)].astype(F32)
    above = slots[lax.min(row + 1, lat_count - 1)].astype(F32)
    edge[0] = jnp.where(row > 0, below, 0.0)
    edge[1] = jnp.where(row < lat_count - 1, above, 0.0)
    sums = [[], [], [], []]
    for sample in range(samples):
        mean, inverse = unweave(mean_all, sample), unweave(inverse_all, sample)
        stats_out[sample : sample + 1, :] = mean
        stats_out[samples + sample : samples + sample + 1, :] = inverse
        flat = mixed[sample].reshape(size, channels).astype(F32)
        norm = (flat - mean) * inverse
        pre = norm * gamma[...] + beta[...]
        sig = 1.0 / (1.0 + jnp.exp(-pre))
        norm_out[sample] = norm
        act = (pre * sig).astype(BF16)
        slope = sig * (1.0 + pre * (1.0 - sig))
        here = slice(8 + sample * span, 8 + (sample + 1) * span)
        spread[0] = edge[0, here, :]
        spread[1 : 1 + rows] = wide[sample]
        spread[1 + rows] = edge[1, here, :]
        windows(spread, shifted, rows, cols)
        style_full = column[sample]
        demod_row = demod[sample : sample + 1, :]
        both = style_full * demod_row
        product = jnp.zeros((channels, channels), F32)
        grad_act = jnp.zeros((size, channels), F32)
        for row_tap in range(3):
            window = shifted[row_tap * cols : row_tap * cols + size, :]
            grad_act = grad_act + jnp.dot(
                window, back_taps[sample, row_tap], preferred_element_type=F32
            )
            grad = lax.dot_general(
                act, window, (((0,), (0,)), ((), ())), preferred_element_type=F32
            )
            for col_tap in range(3):
                tap = (2 - row_tap) * 3 + 2 - col_tap
                block = grad[:, col_tap * channels : (col_tap + 1) * channels]
                product = product + block * weight[tap]
                here = slice(tap * channels, (tap + 1) * channels)
                part = block * both
                total[here, :] = part if sample == 0 else total[here, :] + part
        grad_pre = grad_act * slope
        grad_out[sample] = grad_pre
        sums[0].append(jnp.sum(product * style_full, axis=0, keepdims=True))
        sums[1].append(jnp.sum((product * demod_row).T, axis=0, keepdims=True))
        sums[2].append(jnp.sum(grad_pre * norm, axis=0, keepdims=True))
        sums[3].append(jnp.sum(grad_pre, axis=0, keepdims=True))
    small = jnp.concatenate(sum(sums, []), axis=0)
    lane = lanes_of(TILE)
    sub = lax.broadcasted_iota(jnp.int32, (TILE, channels), 0)
    quarters = []
    for quarter in range(4):
        turned = pltpu.roll(small, LANES - 32 * quarter, 1) if quarter else small
        piece = jnp.where(lane < 64, turned, pltpu.roll(turned, 64, 1))
        piece = jnp.where((lane & 32) == 0, piece, 0.0)
        quarters.append(split_terms(piece, lane))
    for shard in range(SHARDS):
        main = total[32 * shard : 32 * shard + 32, :]
        start = 8 * channels + 8 * (shard // 2)
        last = total[start : start + 8, :]
        if shard % 2:
            last = pltpu.roll(last, 4, 0)
        extra = quarters[shard % 4][shard // 4 : shard // 4 + 1, :]
        tail = jnp.where(sub < 4, last, jnp.where(sub == 4, extra, 0.0))
        payload_out[shard] = jnp.concatenate([main, tail], axis=0).astype(BF16)


def split_terms(values, lane):
    high = values.astype(BF16).astype(F32)
    return jnp.where(lane < 64, high, values - high)


def resplit(slots):
    row = lax.broadcasted_iota(jnp.int32, slots.shape, slots.ndim - 2)
    lane = lax.broadcasted_iota(jnp.int32, slots.shape, slots.ndim - 1)
    joined = slots + jnp.roll(slots, 64, slots.ndim - 1)
    high = lax.reduce_precision(joined, 8, 7)
    terms = jnp.where(lane < 64, high, joined - high)
    return jnp.where(row == 36, terms, slots).astype(BF16)


def last_body(
    scale, cells, gathered, stats, norm, cotangent, grad_pre, gamma, style, column, demod,
    power, weight, emb_full, feats_out, weight_out, style_out, gamma_out, beta_out,
):
    samples, tile_rows, tile_cols, channels = cotangent.shape
    size = tile_rows * tile_cols
    lane = lanes_of()
    sub = lax.broadcasted_iota(jnp.int32, (TILE, channels), 0)
    main, tails, small = [], [], []
    for shard in range(SHARDS):
        slot = gathered[shard].astype(F32)
        main.append(slot[0:32, :])
        tails.append(slot[32:40, :])
    for row in range(TILE):
        whole = jnp.zeros((1, channels), F32)
        for quarter in range(4):
            piece = tails[4 * row + quarter][4:5, :]
            piece = piece + pltpu.roll(piece, 64, 1)
            if quarter:
                piece = pltpu.roll(piece, 32 * quarter, 1)
            whole = jnp.where((lane >> 5) == quarter, piece, whole)
        small.append(whole)
    demod_sums, style_sums, gamma_sums, beta_sums = small[0:2], small[2:4], small[4:6], small[6:8]
    gain = gamma[...]
    gamma_out[...] = scale * (gamma_sums[0] + gamma_sums[1])
    beta_out[...] = scale * (beta_sums[0] + beta_sums[1])
    shrink = jnp.zeros((channels, channels), F32)
    rows = []
    for sample in range(samples):
        demod_row = demod[sample : sample + 1, :]
        pulled = demod_sums[sample] * (demod_row * demod_row * demod_row)
        style_full = column[sample]
        shrink = shrink + style_full * style_full * pulled
        spent = jnp.sum((power[...] * pulled).T, axis=0, keepdims=True)
        rows.append(style_sums[sample] - style[sample : sample + 1, :] * spent)
    for tap in range(8):
        for part in range(4):
            here = slice(32 * part, 32 * part + 32)
            weight_out[tap, here, :] = scale * (
                main[4 * tap + part] - shrink[here, :] * weight[tap, here, :]
            )
    for pair in range(16):
        here = slice(8 * pair, 8 * pair + 8)
        block = jnp.where(sub < 4, tails[2 * pair], pltpu.roll(tails[2 * pair + 1], 4, 0))
        weight_out[8, here, :] = scale * (block - shrink[here, :] * weight[8, here, :])
    style_out[...] = scale * (emb_full[0] * rows[0] + emb_full[1] * rows[1])
    for sample in range(samples):
        inverse = stats[samples + sample : samples + sample + 1, :]
        product_mean = group_total(gain * beta_sums[sample]) * (1.0 / cells)
        squared_mean = group_total(gain * gamma_sums[sample]) * (1.0 / cells)
        change = inverse * (gain * grad_pre[sample] - product_mean - norm[sample] * squared_mean)
        out = cotangent[sample].reshape(size, channels).astype(F32) + change
        feats_out[sample] = out.astype(BF16).reshape(tile_rows, tile_cols, channels)


def on_device(
    feats, cond, null_field, drop_flags, emb, style_weight, conv_weight, gamma, beta, cotangent
):
    samples, tile_rows, tile_cols, channels = feats.shape
    group_size = channels // GROUPS
    lat_count, lon_count = lax.axis_size(LAT), lax.axis_size(LON)
    devices_all = lat_count * lon_count
    cells_local = tile_rows * tile_cols * group_size
    cells_per_group = cells_local * devices_all
    scale_gradient = 1.0 / math.sqrt(samples * tile_rows * tile_cols * devices_all)
    taps = conv_weight.reshape(9, channels, channels)

    lat_slot = -(-(8 + samples * (tile_cols + 2)) // 16) * 16
    edges = array((2, samples, tile_rows, channels), BF16)
    mixed, moments, first, last = call(
        mix_body,
        (array(feats.shape, BF16), array((lon_count, 2, LANES)), edges, edges),
        (
            pltpu.VMEM(feats.shape, BF16),
            pltpu.VMEM(feats.shape, BF16),
            pltpu.VMEM(null_field.shape, BF16),
            pltpu.VMEM(feats.shape, BF16),
            pltpu.VMEM(drop_flags.shape, jnp.int32),
            pltpu.SemaphoreType.DMA((2 * samples + 3,)),
        ),
        room=60,
        in_specs=[pl.BlockSpec(memory_space=pl.ANY)] * 5,
    )(feats, cond, null_field, cotangent, drop_flags)
    rows = exchange(moments, LON)
    low, high = shift(last, LON, 1, True), shift(first, LON, -1, True)
    mean = jnp.mean(rows[:, :1], axis=0)
    away = rows[:, :1] - mean
    moments = jnp.concatenate(
        [mean, jnp.sum(rows[:, 1:] + cells_local * (away * away), axis=0)], axis=0
    )
    moments, low, high = lax.optimization_barrier((moments, low, high))
    wide_cot, slots = call(
        build_body,
        (
            array((samples, tile_rows, tile_cols + 2, channels)),
            array((lat_count, lat_slot, LANES), BF16),
        ),
        (pltpu.VMEM((lat_slot, LANES), F32),),
    )(moments, low, high, cotangent)
    slots = exchange(slots, LAT)
    padded = jnp.concatenate([low[0][:, :, None], mixed, high[0][:, :, None]], axis=2)
    low, high = shift(padded[:, -1:], LAT, 1, False), shift(padded[:, :1], LAT, -1, False)

    taps_shape = (samples, 3, 3 * channels, channels)
    gamma, beta, style, column, demod, power, emb_full, back_taps, fore_taps = call(
        weights_body,
        (
            array((1, channels)),
            array((1, channels)),
            array((samples, channels)),
            array((samples, channels, channels)),
            array((samples, channels)),
            array((channels, channels)),
            array((samples,) + style_weight.shape),
            array(taps_shape, BF16),
            array(taps_shape, BF16),
        ),
    )(emb, style_weight, gamma[None], beta[None], taps)
    spread = pltpu.VMEM((tile_rows + 2, tile_cols + 2, channels), F32)
    shifted = pltpu.VMEM(((tile_rows + 2) * tile_cols, 3 * channels), BF16)
    flat = (samples, tile_rows * tile_cols, channels)
    stats, norm, grad_pre, payload = call(
        functools.partial(sums_body, cells_local * lon_count, cells_per_group),
        (
            array((2 * samples, LANES)),
            array(flat),
            array(flat),
            array((SHARDS, SLOT, LANES), BF16),
        ),
        (
            pltpu.VMEM((2, lat_slot, LANES), F32),
            spread,
            shifted,
            pltpu.VMEM((9 * channels, channels), F32),
        ),
    )(slots, mixed, wide_cot, gamma, beta, back_taps, column, demod, taps)

    payload, low, high = lax.optimization_barrier((payload, low, high))
    padded = jnp.concatenate([low, padded, high], axis=1)
    core_count, near_count = lax.axis_size("c"), lax.axis_size(NEAR)
    payload = lax.all_gather(payload, "c")
    payload = payload.reshape(core_count, core_count, near_count, SLOT, LANES)
    payload = lax.dynamic_index_in_dim(payload, lax.axis_index("c"), 1, False)
    payload = resplit(jnp.sum(payload.astype(F32), axis=0))
    payload = resplit(jnp.sum(exchange(payload, NEAR).astype(F32), axis=0))
    payload = resplit(jnp.sum(everyone(payload, LAT).astype(F32), axis=0))
    payload = lax.all_gather(everyone(payload, NEAR), "c")

    block_out = call(forward_body, array(feats.shape, BF16), (spread, shifted))(
        padded, fore_taps, stats, gamma, beta
    )

    grad_feats, grad_weight, grad_style, grad_gamma, grad_beta = call(
        functools.partial(last_body, scale_gradient, cells_per_group),
        (
            array(feats.shape, BF16),
            array(taps.shape),
            array(style_weight.shape),
            array((1, LANES)),
            array((1, LANES)),
        ),
    )(
        payload.reshape(SHARDS, SLOT, LANES), stats, norm, cotangent, grad_pre, gamma, style,
        column, demod, power, taps, emb_full,
    )
    return (
        block_out,
        grad_feats,
        grad_weight.reshape(conv_weight.shape),
        grad_style,
        grad_gamma[0],
        grad_beta[0],
    )


def solution(mesh):
    parts = Mesh(mesh.devices.reshape(4, 4, 2, 8, 2), LAT + LON)
    tile = P(None, LAT, LON, None)
    placed = (tile, tile, P(LAT, LON, None), P(), P(), P(), P(), P(), P(), tile)
    return jax.shard_map(
        on_device,
        mesh=parts,
        in_specs=placed,
        out_specs=(tile, tile, P(), P(), P(), P()),
        check_vma=False,
    )
```

```python
import functools
import math

import jax
import jax.numpy as jnp
from jax import lax
from jax.experimental import pallas as pl
from jax.experimental.pallas import tpu as pltpu
from jax.sharding import Mesh, PartitionSpec as P

GROUPS = 32
LAT = ("zh", "x")
LON = ("zl", "y", "c")
NEAR = ("zl", "y")
F32 = jnp.float32
BF16 = jnp.bfloat16
TILE = 8
SHARDS = 32
SLOT = 40
LANES = 128


def shift(block, axes, step, periodic):
    count = lax.axis_size(axes)
    pairs = [(i, i + step) for i in range(count)]
    if periodic:
        pairs = [(source, target % count) for source, target in pairs]
    else:
        pairs = [(source, target) for source, target in pairs if 0 <= target < count]
    return lax.ppermute(block, axes, pairs)


def extend(block, axes, dim, periodic):
    last = block.shape[dim] - 1
    low = shift(lax.slice_in_dim(block, last, last + 1, axis=dim), axes, 1, periodic)
    high = shift(lax.slice_in_dim(block, 0, 1, axis=dim), axes, -1, periodic)
    return jnp.concatenate([low, block, high], axis=dim)


def exchange(block, axes):
    return lax.all_to_all(block, axes, 0, 0)


def everyone(block, axes):
    return exchange(jnp.broadcast_to(block[None], (lax.axis_size(axes),) + block.shape), axes)


def call(body, outputs, scratch=(), room=48, **more):
    return pl.pallas_call(
        body,
        out_shape=outputs,
        scratch_shapes=list(scratch),
        **more,
        compiler_params=pltpu.CompilerParams(vmem_limit_bytes=room * 1024 * 1024),
    )


def array(shape, dtype=F32):
    return jax.ShapeDtypeStruct(shape, dtype)


def lanes_of(rows=1):
    return lax.broadcasted_iota(jnp.int32, (rows, LANES), 1)


def group_total(row):
    lane = lanes_of()
    for step in (1, 2):
        after, before = pltpu.roll(row, LANES - step, 1), pltpu.roll(row, step, 1)
        row = row + jnp.where((lane & step) == 0, after, before)
    return row


def weave(first, second):
    return jnp.where((lanes_of() & 1) == 0, first, second)


def unweave(row, sample):
    if sample == 0:
        return weave(row, pltpu.roll(row, 1, 1))
    return weave(pltpu.roll(row, LANES - 1, 1), row)


def place(axes):
    index = 0
    for axis in axes:
        index = index * lax.axis_size(axis) + lax.axis_index(axis)
    return index


def three_terms(value):
    terms = []
    for _ in range(3):
        terms.append(value.astype(BF16).astype(F32))
        value = value - terms[-1]
    return terms


def merged(slots, count):
    rows = slots[:, 0:8, :].astype(F32)
    means = rows[:, 0:1, :] + rows[:, 1:2, :] + rows[:, 2:3, :]
    spreads = rows[:, 3:4, :] + rows[:, 4:5, :] + rows[:, 5:6, :]
    mean = jnp.mean(means, axis=0)
    away = means - mean[None]
    return mean, jnp.sum(spreads + count * away * away, axis=0)


def header(mean, spread):
    return three_terms(mean) + three_terms(spread) + [jnp.zeros((2, LANES), F32)]


def fetcher(arrivals):
    used = iter(range(arrivals.shape[0]))

    def fetch(source, target):
        copy = pltpu.make_async_copy(source, target, arrivals.at[next(used)])
        copy.start()
        return copy

    return fetch


def mix_body(
    feats_in, cond_in, null_in, cot_in, flags_in, mixed_out, moments_out, first_out, last_out,
    feats, cond, null, cot, flags, arrivals,
):
    fetch = fetcher(arrivals)
    flags_copy, null_copy = fetch(flags_in, flags), fetch(null_in, null)
    field_copies = [
        (fetch(feats_in.at[sample], feats.at[sample]), fetch(cond_in.at[sample], cond.at[sample]))
        for sample in range(feats.shape[0])
    ]
    cot_copy = fetch(cot_in, cot)
    flags_copy.wait()
    null_copy.wait()
    samples, tile_rows, tile_cols, channels = feats.shape
    cells = tile_rows * tile_cols
    size = cells * (channels // GROUPS)
    null32 = null[...].astype(F32)
    means, spreads = [], []
    for sample in range(samples):
        for copy in field_copies[sample]:
            copy.wait()
        dropped = flags[sample : sample + 1, :].astype(F32).reshape(1, 1, channels)
        mixed = (
            feats[sample].astype(F32) + dropped * null32 + (1.0 - dropped) * cond[sample].astype(F32)
        ).astype(BF16)
        mixed_out[sample] = mixed
        wide = mixed.astype(F32)
        first_out[0, sample] = wide[:, 0, :].astype(BF16)
        last_out[0, sample] = wide[:, tile_cols - 1, :].astype(BF16)
        wide = wide.reshape(cells, channels)
        mean = group_total(jnp.sum(wide, axis=0, keepdims=True)) * (1.0 / size)
        away = wide - mean
        means.append(mean)
        spreads.append(group_total(jnp.sum(away * away, axis=0, keepdims=True)))
    moments = jnp.concatenate([weave(*means), weave(*spreads)], axis=0)
    moments_out[...] = jnp.broadcast_to(moments[None], moments_out.shape)
    cot_copy.wait()
    for sample in range(samples):
        wide = cot[sample].astype(F32)
        first_out[1, sample] = wide[:, 0, :].astype(BF16)
        last_out[1, sample] = wide[:, tile_cols - 1, :].astype(BF16)


def build_body(moments, low, high, cot, wide_out, slots_out, edge):
    samples, tile_rows, tile_cols, channels = cot.shape
    lat_count = slots_out.shape[0]
    for sample in range(samples):
        wide_out[sample, :, 0, :] = low[1, sample].astype(F32)
        wide_out[sample, :, 1 : 1 + tile_cols, :] = cot[sample].astype(F32)
        wide_out[sample, :, 1 + tile_cols, :] = high[1, sample].astype(F32)
    edge[...] = jnp.zeros(edge.shape, F32)
    edge[0:8, :] = jnp.concatenate(header(moments[0:1, :], moments[1:2, :]), axis=0)
    span = tile_cols + 2
    for sample in range(samples):
        edge[8 + sample * span : 8 + (sample + 1) * span, :] = wide_out[sample, 0]
    slots_out[...] = jnp.broadcast_to(edge[...].astype(BF16)[None], slots_out.shape)
    for sample in range(samples):
        edge[8 + sample * span : 8 + (sample + 1) * span, :] = wide_out[sample, tile_rows - 1]
    row = place(LAT)

    @pl.when(row < lat_count - 1)
    def _():
        slots_out[row + 1] = edge[...].astype(BF16)


def weights_body(
    emb, style_weight, gamma, beta, weight,
    gamma_out, beta_out, style_out, column_out, demod_out, power_out, emb_out, back_out, taps_out,
):
    gamma_out[...] = gamma[...]
    beta_out[...] = beta[...]
    power = jnp.zeros(weight.shape[1:], F32)
    for tap in range(9):
        power = power + weight[tap] * weight[tap]
    samples, channels = emb.shape[0], weight.shape[2]
    exact = lax.Precision.HIGHEST
    style = 1.0 + jnp.dot(
        emb[...], style_weight[...], precision=exact, preferred_element_type=F32
    )
    squares = jnp.dot(style * style, power, precision=exact, preferred_element_type=F32)
    demod = lax.rsqrt(squares + 1e-08)
    style_out[...] = style
    demod_out[...] = demod
    power_out[...] = power
    for sample in range(samples):
        here = slice(sample, sample + 1)
        column = jnp.broadcast_to(style[here, :], (channels, channels)).T
        column_out[sample] = column
        emb_out[sample] = jnp.broadcast_to(emb[here, :], (channels, emb.shape[1])).T
        for tap in range(9):
            row, col = tap // 3, tap % 3
            block = weight[tap] * column * demod[here, :]
            taps_out[sample, row, col * channels : (col + 1) * channels, :] = block.astype(BF16)
            row, col = 2 - row, 2 - col
            back_out[sample, row, col * channels : (col + 1) * channels, :] = block.T.astype(BF16)


def windows(spread, shifted, rows, cols):
    channels = spread.shape[-1]
    for tap in range(3):
        moved = spread[:, tap : tap + cols, :].reshape((rows + 2) * cols, channels)
        shifted[:, tap * channels : (tap + 1) * channels] = moved.astype(BF16)


def forward_body(padded, taps, stats, gamma, beta, block_out, spread, shifted):
    samples, rows, cols = padded.shape[0], padded.shape[1] - 2, padded.shape[2] - 2
    size = rows * cols
    row = lax.broadcasted_iota(jnp.int32, spread.shape, 0) + place(LAT) * rows
    inside = (row > 0) & (row <= rows * lax.axis_size(LAT))
    for sample in range(samples):
        mixed = padded[sample].astype(F32)
        mean = stats[sample : sample + 1, :][None]
        inverse = stats[samples + sample : samples + sample + 1, :][None]
        pre = (mixed - mean) * inverse * gamma[...][None] + beta[...][None]
        act = jnp.where(inside, pre / (1.0 + jnp.exp(-pre)), 0.0)
        spread[...] = act
        windows(spread, shifted, rows, cols)
        total = mixed[1 : 1 + rows, 1 : 1 + cols, :].reshape(size, -1)
        for row_tap in range(3):
            window = shifted[row_tap * cols : row_tap * cols + size, :]
            total = total + jnp.dot(window, taps[sample, row_tap], preferred_element_type=F32)
        block_out[sample] = total.astype(BF16).reshape(rows, cols, -1)


def sums_body(
    count, cells, slots, mixed, wide, gamma, beta, back_taps, column, demod, weight,
    stats_out, norm_out, grad_out, payload_out, edge, spread, shifted, total,
):
    samples, rows, cols, channels = mixed.shape
    size, span = rows * cols, cols + 2
    mean_all, spread_all = merged(slots, count)
    inverse_all = lax.rsqrt(spread_all * (1.0 / cells) + 1e-05)
    lat_count, row = slots.shape[0], place(LAT)
    below = slots[lax.max(row - 1, 0)].astype(F32)
    above = slots[lax.min(row + 1, lat_count - 1)].astype(F32)
    edge[0] = jnp.where(row > 0, below, 0.0)
    edge[1] = jnp.where(row < lat_count - 1, above, 0.0)
    sums = [[], [], [], []]
    for sample in range(samples):
        mean, inverse = unweave(mean_all, sample), unweave(inverse_all, sample)
        stats_out[sample : sample + 1, :] = mean
        stats_out[samples + sample : samples + sample + 1, :] = inverse
        flat = mixed[sample].reshape(size, channels).astype(F32)
        norm = (flat - mean) * inverse
        pre = norm * gamma[...] + beta[...]
        sig = 1.0 / (1.0 + jnp.exp(-pre))
        norm_out[sample] = norm
        act = (pre * sig).astype(BF16)
        slope = sig * (1.0 + pre * (1.0 - sig))
        here = slice(8 + sample * span, 8 + (sample + 1) * span)
        spread[0] = edge[0, here, :]
        spread[1 : 1 + rows] = wide[sample]
        spread[1 + rows] = edge[1, here, :]
        windows(spread, shifted, rows, cols)
        style_full = column[sample]
        demod_row = demod[sample : sample + 1, :]
        both = style_full * demod_row
        product = jnp.zeros((channels, channels), F32)
        grad_act = jnp.zeros((size, channels), F32)
        for row_tap in range(3):
            window = shifted[row_tap * cols : row_tap * cols + size, :]
            grad_act = grad_act + jnp.dot(
                window, back_taps[sample, row_tap], preferred_element_type=F32
            )
            grad = lax.dot_general(
                act, window, (((0,), (0,)), ((), ())), preferred_element_type=F32
            )
            for col_tap in range(3):
                tap = (2 - row_tap) * 3 + 2 - col_tap
                block = grad[:, col_tap * channels : (col_tap + 1) * channels]
                product = product + block * weight[tap]
                here = slice(tap * channels, (tap + 1) * channels)
                part = block * both
                total[here, :] = part if sample == 0 else total[here, :] + part
        grad_pre = grad_act * slope
        grad_out[sample] = grad_pre
        sums[0].append(jnp.sum(product * style_full, axis=0, keepdims=True))
        sums[1].append(jnp.sum((product * demod_row).T, axis=0, keepdims=True))
        sums[2].append(jnp.sum(grad_pre * norm, axis=0, keepdims=True))
        sums[3].append(jnp.sum(grad_pre, axis=0, keepdims=True))
    small = jnp.concatenate(sum(sums, []), axis=0)
    lane = lanes_of(TILE)
    sub = lax.broadcasted_iota(jnp.int32, (TILE, channels), 0)
    quarters = []
    for quarter in range(4):
        turned = pltpu.roll(small, LANES - 32 * quarter, 1) if quarter else small
        piece = jnp.where(lane < 64, turned, pltpu.roll(turned, 64, 1))
        piece = jnp.where((lane & 32) == 0, piece, 0.0)
        quarters.append(split_terms(piece, lane))
    for shard in range(SHARDS):
        main = total[32 * shard : 32 * shard + 32, :]
        start = 8 * channels + 8 * (shard // 2)
        last = total[start : start + 8, :]
        if shard % 2:
            last = pltpu.roll(last, 4, 0)
        extra = quarters[shard % 4][shard // 4 : shard // 4 + 1, :]
        tail = jnp.where(sub < 4, last, jnp.where(sub == 4, extra, 0.0))
        payload_out[shard] = jnp.concatenate([main, tail], axis=0).astype(BF16)


def split_terms(values, lane):
    high = values.astype(BF16).astype(F32)
    return jnp.where(lane < 64, high, values - high)


def resplit(slots):
    row = lax.broadcasted_iota(jnp.int32, slots.shape, slots.ndim - 2)
    lane = lax.broadcasted_iota(jnp.int32, slots.shape, slots.ndim - 1)
    joined = slots + jnp.roll(slots, 64, slots.ndim - 1)
    high = lax.reduce_precision(joined, 8, 7)
    terms = jnp.where(lane < 64, high, joined - high)
    return jnp.where(row == 36, terms, slots).astype(BF16)


def last_body(
    scale, cells, gathered, stats, norm, cotangent, grad_pre, gamma, style, column, demod,
    power, weight, emb_full, feats_out, weight_out, style_out, gamma_out, beta_out,
):
    samples, tile_rows, tile_cols, channels = cotangent.shape
    size = tile_rows * tile_cols
    lane = lanes_of()
    sub = lax.broadcasted_iota(jnp.int32, (TILE, channels), 0)
    main, tails, small = [], [], []
    for shard in range(SHARDS):
        slot = gathered[shard].astype(F32)
        main.append(slot[0:32, :])
        tails.append(slot[32:40, :])
    for row in range(TILE):
        whole = jnp.zeros((1, channels), F32)
        for quarter in range(4):
            piece = tails[4 * row + quarter][4:5, :]
            piece = piece + pltpu.roll(piece, 64, 1)
            if quarter:
                piece = pltpu.roll(piece, 32 * quarter, 1)
            whole = jnp.where((lane >> 5) == quarter, piece, whole)
        small.append(whole)
    demod_sums, style_sums, gamma_sums, beta_sums = small[0:2], small[2:4], small[4:6], small[6:8]
    gain = gamma[...]
    gamma_out[...] = scale * (gamma_sums[0] + gamma_sums[1])
    beta_out[...] = scale * (beta_sums[0] + beta_sums[1])
    shrink = jnp.zeros((channels, channels), F32)
    rows = []
    for sample in range(samples):
        demod_row = demod[sample : sample + 1, :]
        pulled = demod_sums[sample] * (demod_row * demod_row * demod_row)
        style_full = column[sample]
        shrink = shrink + style_full * style_full * pulled
        spent = jnp.sum((power[...] * pulled).T, axis=0, keepdims=True)
        rows.append(style_sums[sample] - style[sample : sample + 1, :] * spent)
    for tap in range(8):
        for part in range(4):
            here = slice(32 * part, 32 * part + 32)
            weight_out[tap, here, :] = scale * (
                main[4 * tap + part] - shrink[here, :] * weight[tap, here, :]
            )
    for pair in range(16):
        here = slice(8 * pair, 8 * pair + 8)
        block = jnp.where(sub < 4, tails[2 * pair], pltpu.roll(tails[2 * pair + 1], 4, 0))
        weight_out[8, here, :] = scale * (block - shrink[here, :] * weight[8, here, :])
    style_out[...] = scale * (emb_full[0] * rows[0] + emb_full[1] * rows[1])
    for sample in range(samples):
        inverse = stats[samples + sample : samples + sample + 1, :]
        product_mean = group_total(gain * beta_sums[sample]) * (1.0 / cells)
        squared_mean = group_total(gain * gamma_sums[sample]) * (1.0 / cells)
        change = inverse * (gain * grad_pre[sample] - product_mean - norm[sample] * squared_mean)
        out = cotangent[sample].reshape(size, channels).astype(F32) + change
        feats_out[sample] = out.astype(BF16).reshape(tile_rows, tile_cols, channels)


def on_device(
    feats, cond, null_field, drop_flags, emb, style_weight, conv_weight, gamma, beta, cotangent
):
    samples, tile_rows, tile_cols, channels = feats.shape
    group_size = channels // GROUPS
    lat_count, lon_count = lax.axis_size(LAT), lax.axis_size(LON)
    devices_all = lat_count * lon_count
    cells_local = tile_rows * tile_cols * group_size
    cells_per_group = cells_local * devices_all
    scale_gradient = 1.0 / math.sqrt(samples * tile_rows * tile_cols * devices_all)
    taps = conv_weight.reshape(9, channels, channels)

    lat_slot = -(-(8 + samples * (tile_cols + 2)) // 16) * 16
    edges = array((2, samples, tile_rows, channels), BF16)
    mixed, moments, first, last = call(
        mix_body,
        (array(feats.shape, BF16), array((lon_count, 2, LANES)), edges, edges),
        (
            pltpu.VMEM(feats.shape, BF16),
            pltpu.VMEM(feats.shape, BF16),
            pltpu.VMEM(null_field.shape, BF16),
            pltpu.VMEM(feats.shape, BF16),
            pltpu.VMEM(drop_flags.shape, jnp.int32),
            pltpu.SemaphoreType.DMA((2 * samples + 3,)),
        ),
        room=60,
        in_specs=[pl.BlockSpec(memory_space=pl.ANY)] * 5,
    )(feats, cond, null_field, cotangent, drop_flags)
    rows = exchange(moments, LON)
    low, high = shift(last, LON, 1, True), shift(first, LON, -1, True)
    mean = jnp.mean(rows[:, :1], axis=0)
    away = rows[:, :1] - mean
    moments = jnp.concatenate(
        [mean, jnp.sum(rows[:, 1:] + cells_local * (away * away), axis=0)], axis=0
    )
    moments, low, high = lax.optimization_barrier((moments, low, high))
    wide_cot, slots = call(
        build_body,
        (
            array((samples, tile_rows, tile_cols + 2, channels)),
            array((lat_count, lat_slot, LANES), BF16),
        ),
        (pltpu.VMEM((lat_slot, LANES), F32),),
    )(moments, low, high, cotangent)
    slots = exchange(slots, LAT)
    padded = jnp.concatenate([low[0][:, :, None], mixed, high[0][:, :, None]], axis=2)
    low, high = shift(padded[:, -1:], LAT, 1, False), shift(padded[:, :1], LAT, -1, False)

    taps_shape = (samples, 3, 3 * channels, channels)
    gamma, beta, style, column, demod, power, emb_full, back_taps, fore_taps = call(
        weights_body,
        (
            array((1, channels)),
            array((1, channels)),
            array((samples, channels)),
            array((samples, channels, channels)),
            array((samples, channels)),
            array((channels, channels)),
            array((samples,) + style_weight.shape),
            array(taps_shape, BF16),
            array(taps_shape, BF16),
        ),
    )(emb, style_weight, gamma[None], beta[None], taps)
    spread = pltpu.VMEM((tile_rows + 2, tile_cols + 2, channels), F32)
    shifted = pltpu.VMEM(((tile_rows + 2) * tile_cols, 3 * channels), BF16)
    flat = (samples, tile_rows * tile_cols, channels)
    stats, norm, grad_pre, payload = call(
        functools.partial(sums_body, cells_local * lon_count, cells_per_group),
        (
            array((2 * samples, LANES)),
            array(flat),
            array(flat),
            array((SHARDS, SLOT, LANES), BF16),
        ),
        (
            pltpu.VMEM((2, lat_slot, LANES), F32),
            spread,
            shifted,
            pltpu.VMEM((9 * channels, channels), F32),
        ),
    )(slots, mixed, wide_cot, gamma, beta, back_taps, column, demod, taps)

    core_count, near_count = lax.axis_size("c"), lax.axis_size(NEAR)
    payload = lax.all_gather(payload, "c")
    payload = payload.reshape(core_count, core_count, near_count, SLOT, LANES)
    payload = lax.dynamic_index_in_dim(payload, lax.axis_index("c"), 1, False)
    payload = resplit(jnp.sum(payload.astype(F32), axis=0))
    payload = resplit(jnp.sum(exchange(payload, NEAR).astype(F32), axis=0))
    payload = resplit(jnp.sum(everyone(payload, LAT).astype(F32), axis=0))
    payload, low, high = lax.optimization_barrier((payload, low, high))
    padded = jnp.concatenate([low, padded, high], axis=1)
    payload = lax.all_gather(everyone(payload, NEAR), "c")

    block_out = call(forward_body, array(feats.shape, BF16), (spread, shifted))(
        padded, fore_taps, stats, gamma, beta
    )

    grad_feats, grad_weight, grad_style, grad_gamma, grad_beta = call(
        functools.partial(last_body, scale_gradient, cells_per_group),
        (
            array(feats.shape, BF16),
            array(taps.shape),
            array(style_weight.shape),
            array((1, LANES)),
            array((1, LANES)),
        ),
    )(
        payload.reshape(SHARDS, SLOT, LANES), stats, norm, cotangent, grad_pre, gamma, style,
        column, demod, power, taps, emb_full,
    )
    return (
        block_out,
        grad_feats,
        grad_weight.reshape(conv_weight.shape),
        grad_style,
        grad_gamma[0],
        grad_beta[0],
    )


def solution(mesh):
    parts = Mesh(mesh.devices.reshape(4, 4, 2, 8, 2), LAT + LON)
    tile = P(None, LAT, LON, None)
    placed = (tile, tile, P(LAT, LON, None), P(), P(), P(), P(), P(), P(), tile)
    return jax.shard_map(
        on_device,
        mesh=parts,
        in_specs=placed,
        out_specs=(tile, tile, P(), P(), P(), P()),
        check_vma=False,
    )
```

```python
import functools
import math

import jax
import jax.numpy as jnp
from jax import lax
from jax.experimental import pallas as pl
from jax.experimental.pallas import tpu as pltpu
from jax.sharding import Mesh, PartitionSpec as P

GROUPS = 32
LAT = ("zh", "x")
LON = ("zl", "y", "c")
NEAR = ("zl", "y")
F32 = jnp.float32
BF16 = jnp.bfloat16
TILE = 8
SHARDS = 32
SLOT = 40
LANES = 128


def shift(block, axes, step, periodic):
    count = lax.axis_size(axes)
    pairs = [(i, i + step) for i in range(count)]
    if periodic:
        pairs = [(source, target % count) for source, target in pairs]
    else:
        pairs = [(source, target) for source, target in pairs if 0 <= target < count]
    return lax.ppermute(block, axes, pairs)


def exchange(block, axes):
    return lax.all_to_all(block, axes, 0, 0)


def call(body, outputs, scratch=(), room=24, **more):
    return pl.pallas_call(
        body,
        out_shape=outputs,
        scratch_shapes=list(scratch),
        **more,
        compiler_params=pltpu.CompilerParams(vmem_limit_bytes=room * 1024 * 1024),
    )


def array(shape, dtype=F32):
    return jax.ShapeDtypeStruct(shape, dtype)


def lanes_of(rows=1):
    return lax.broadcasted_iota(jnp.int32, (rows, LANES), 1)


def group_total(row):
    lane = lanes_of()
    for step in (1, 2):
        after, before = pltpu.roll(row, LANES - step, 1), pltpu.roll(row, step, 1)
        row = row + jnp.where((lane & step) == 0, after, before)
    return row


def weave(first, second):
    return jnp.where((lanes_of() & 1) == 0, first, second)


def unweave(row, sample):
    if sample == 0:
        return weave(row, pltpu.roll(row, 1, 1))
    return weave(pltpu.roll(row, LANES - 1, 1), row)


def place(axes):
    index = 0
    for axis in axes:
        index = index * lax.axis_size(axis) + lax.axis_index(axis)
    return index


def three_terms(value):
    terms = []
    for _ in range(3):
        terms.append(value.astype(BF16).astype(F32))
        value = value - terms[-1]
    return terms


def merged(slots, count):
    rows = slots[:, 0:8, :].astype(F32)
    means = rows[:, 0:1, :] + rows[:, 1:2, :] + rows[:, 2:3, :]
    spreads = rows[:, 3:4, :] + rows[:, 4:5, :] + rows[:, 5:6, :]
    mean = jnp.mean(means, axis=0)
    away = means - mean[None]
    return mean, jnp.sum(spreads + count * away * away, axis=0)


def header(mean, spread):
    return three_terms(mean) + three_terms(spread) + [jnp.zeros((2, LANES), F32)]


def fetcher(arrivals):
    used = iter(range(arrivals.shape[0]))

    def fetch(source, target):
        copy = pltpu.make_async_copy(source, target, arrivals.at[next(used)])
        copy.start()
        return copy

    return fetch


def mix_body(
    feats_in, cond_in, null_in, cot_in, flags_in, mixed_out, slots_out, edges_out,
    feats, cond, null, cot, flags, arrivals,
):
    fetch = fetcher(arrivals)
    flags_copy, null_copy = fetch(flags_in, flags), fetch(null_in, null)
    field_copies = [
        (fetch(feats_in.at[sample], feats.at[sample]), fetch(cond_in.at[sample], cond.at[sample]))
        for sample in range(feats.shape[0])
    ]
    cot_copy = fetch(cot_in, cot)
    flags_copy.wait()
    null_copy.wait()
    samples, tile_rows, tile_cols, channels = feats.shape
    cells = tile_rows * tile_cols
    size = cells * (channels // GROUPS)
    null32 = null[...].astype(F32)
    means, spreads, firsts, lasts = [], [], [], []
    for sample in range(samples):
        for copy in field_copies[sample]:
            copy.wait()
        dropped = flags[sample : sample + 1, :].astype(F32).reshape(1, 1, channels)
        mixed = (
            feats[sample].astype(F32) + dropped * null32 + (1.0 - dropped) * cond[sample].astype(F32)
        ).astype(BF16)
        mixed_out[sample] = mixed
        wide = mixed.astype(F32)
        firsts.append(wide[:, 0, :])
        lasts.append(wide[:, tile_cols - 1, :])
        wide = wide.reshape(cells, channels)
        mean = group_total(jnp.sum(wide, axis=0, keepdims=True)) * (1.0 / size)
        away = wide - mean
        means.append(mean)
        spreads.append(group_total(jnp.sum(away * away, axis=0, keepdims=True)))
    spare = jnp.zeros((SLOT - 2 * samples * tile_rows, channels), F32)
    edges_out[...] = jnp.concatenate(firsts + lasts + [spare], axis=0).astype(BF16)
    rows = header(weave(*means), weave(*spreads))
    cot_copy.wait()
    firsts, lasts = [], []
    for sample in range(samples):
        wide = cot[sample].astype(F32)
        firsts.append(wide[:, 0, :])
        lasts.append(wide[:, tile_cols - 1, :])
    slots_out[...] = jnp.broadcast_to(
        jnp.concatenate(rows + firsts, axis=0).astype(BF16)[None], slots_out.shape
    )
    after = lax.rem(place(LON) + 1, slots_out.shape[0])
    slots_out[after] = jnp.concatenate(rows + lasts, axis=0).astype(BF16)


def merge_body(count, slots, cot, wide_out, slots_out, edge):
    samples, tile_rows, tile_cols, channels = cot.shape
    lon_count, lat_count = slots.shape[0], slots_out.shape[0]
    mean, spread = merged(slots, count)
    me = place(LON)
    before = slots[lax.rem(me + lon_count - 1, lon_count)].astype(F32)
    after = slots[lax.rem(me + 1, lon_count)].astype(F32)
    for sample in range(samples):
        here = slice(8 + sample * tile_rows, 8 + (sample + 1) * tile_rows)
        wide_out[sample, :, 0, :] = before[here, :]
        wide_out[sample, :, 1 : 1 + tile_cols, :] = cot[sample].astype(F32)
        wide_out[sample, :, 1 + tile_cols, :] = after[here, :]
    edge[...] = jnp.zeros(edge.shape, F32)
    edge[0:8, :] = jnp.concatenate(header(mean, spread), axis=0)
    span = tile_cols + 2
    for sample in range(samples):
        edge[8 + sample * span : 8 + (sample + 1) * span, :] = wide_out[sample, 0]
    slots_out[...] = jnp.broadcast_to(edge[...].astype(BF16)[None], slots_out.shape)
    for sample in range(samples):
        edge[8 + sample * span : 8 + (sample + 1) * span, :] = wide_out[sample, tile_rows - 1]
    row = place(LAT)

    @pl.when(row < lat_count - 1)
    def _():
        slots_out[row + 1] = edge[...].astype(BF16)


def weights_body(
    emb, style_weight, gamma, beta, weight,
    gamma_out, beta_out, style_out, column_out, demod_out, power_out, emb_out, back_out, taps_out,
):
    gamma_out[...] = gamma[...]
    beta_out[...] = beta[...]
    power = jnp.zeros(weight.shape[1:], F32)
    for tap in range(9):
        power = power + weight[tap] * weight[tap]
    samples, channels = emb.shape[0], weight.shape[2]
    exact = lax.Precision.HIGHEST
    style = 1.0 + jnp.dot(
        emb[...], style_weight[...], precision=exact, preferred_element_type=F32
    )
    squares = jnp.dot(style * style, power, precision=exact, preferred_element_type=F32)
    demod = lax.rsqrt(squares + 1e-08)
    style_out[...] = style
    demod_out[...] = demod
    power_out[...] = power
    for sample in range(samples):
        here = slice(sample, sample + 1)
        column = jnp.broadcast_to(style[here, :], (channels, channels)).T
        column_out[sample] = column
        emb_out[sample] = jnp.broadcast_to(emb[here, :], (channels, emb.shape[1])).T
        for tap in range(9):
            row, col = tap // 3, tap % 3
            block = weight[tap] * column * demod[here, :]
            taps_out[sample, row, col * channels : (col + 1) * channels, :] = block.astype(BF16)
            row, col = 2 - row, 2 - col
            back_out[sample, row, col * channels : (col + 1) * channels, :] = block.T.astype(BF16)


def windows(spread, shifted, rows, cols):
    channels = spread.shape[-1]
    for tap in range(3):
        moved = spread[:, tap : tap + cols, :].reshape((rows + 2) * cols, channels)
        shifted[:, tap * channels : (tap + 1) * channels] = moved.astype(BF16)


def forward_body(wide, low, high, taps, stats, gamma, beta, block_out, spread, shifted):
    samples, rows, cols = wide.shape[0], wide.shape[1], wide.shape[2] - 2
    size = rows * cols
    row = lax.broadcasted_iota(jnp.int32, spread.shape, 0) + place(LAT) * rows
    inside = (row > 0) & (row <= rows * lax.axis_size(LAT))
    for sample in range(samples):
        spread[0] = low[sample].astype(F32)
        spread[1 : 1 + rows] = wide[sample]
        spread[1 + rows] = high[sample].astype(F32)
        mean = stats[sample : sample + 1, :][None]
        inverse = stats[samples + sample : samples + sample + 1, :][None]
        pre = (spread[...] - mean) * inverse * gamma[...][None] + beta[...][None]
        spread[...] = jnp.where(inside, pre / (1.0 + jnp.exp(-pre)), 0.0)
        windows(spread, shifted, rows, cols)
        total = wide[sample, :, 1 : 1 + cols, :].reshape(size, -1)
        for row_tap in range(3):
            window = shifted[row_tap * cols : row_tap * cols + size, :]
            total = total + jnp.dot(window, taps[sample, row_tap], preferred_element_type=F32)
        block_out[sample] = total.astype(BF16).reshape(rows, cols, -1)


def sums_body(
    count, cells, slots, mixed, edges, wide, gamma, beta, back_taps, column, demod, weight,
    stats_out, norm_out, grad_out, payload_out, edge, spread, shifted, total,
):
    samples, rows, cols, channels = mixed.shape
    size, span = rows * cols, cols + 2
    mean_all, spread_all = merged(slots, count)
    inverse_all = lax.rsqrt(spread_all * (1.0 / cells) + 1e-05)
    lat_count, row = slots.shape[0], place(LAT)
    below = slots[lax.max(row - 1, 0)].astype(F32)
    above = slots[lax.min(row + 1, lat_count - 1)].astype(F32)
    edge[0] = jnp.where(row > 0, below, 0.0)
    edge[1] = jnp.where(row < lat_count - 1, above, 0.0)
    sums = [[], [], [], []]
    for sample in range(samples):
        mean, inverse = unweave(mean_all, sample), unweave(inverse_all, sample)
        stats_out[sample : sample + 1, :] = mean
        stats_out[samples + sample : samples + sample + 1, :] = inverse
        flat = mixed[sample].reshape(size, channels).astype(F32)
        norm = (flat - mean) * inverse
        pre = norm * gamma[...] + beta[...]
        sig = 1.0 / (1.0 + jnp.exp(-pre))
        norm_out[sample] = norm
        act = (pre * sig).astype(BF16)
        slope = sig * (1.0 + pre * (1.0 - sig))
        here = slice(8 + sample * span, 8 + (sample + 1) * span)
        spread[0] = edge[0, here, :]
        spread[1 : 1 + rows] = wide[sample]
        spread[1 + rows] = edge[1, here, :]
        windows(spread, shifted, rows, cols)
        style_full = column[sample]
        demod_row = demod[sample : sample + 1, :]
        both = style_full * demod_row
        product = jnp.zeros((channels, channels), F32)
        grad_act = jnp.zeros((size, channels), F32)
        for row_tap in range(3):
            window = shifted[row_tap * cols : row_tap * cols + size, :]
            grad_act = grad_act + jnp.dot(
                window, back_taps[sample, row_tap], preferred_element_type=F32
            )
            grad = lax.dot_general(
                act, window, (((0,), (0,)), ((), ())), preferred_element_type=F32
            )
            for col_tap in range(3):
                tap = (2 - row_tap) * 3 + 2 - col_tap
                block = grad[:, col_tap * channels : (col_tap + 1) * channels]
                product = product + block * weight[tap]
                here = slice(tap * channels, (tap + 1) * channels)
                part = block * both
                total[here, :] = part if sample == 0 else total[here, :] + part
        grad_pre = grad_act * slope
        grad_out[sample] = grad_pre
        sums[0].append(jnp.sum(product * style_full, axis=0, keepdims=True))
        sums[1].append(jnp.sum((product * demod_row).T, axis=0, keepdims=True))
        sums[2].append(jnp.sum(grad_pre * norm, axis=0, keepdims=True))
        sums[3].append(jnp.sum(grad_pre, axis=0, keepdims=True))
    payload_out[SHARDS] = edges[...]
    small = jnp.concatenate(sum(sums, []), axis=0)
    lane = lanes_of(TILE)
    sub = lax.broadcasted_iota(jnp.int32, (TILE, channels), 0)
    quarters = []
    for quarter in range(4):
        turned = pltpu.roll(small, LANES - 32 * quarter, 1) if quarter else small
        piece = jnp.where(lane < 64, turned, pltpu.roll(turned, 64, 1))
        piece = jnp.where((lane & 32) == 0, piece, 0.0)
        quarters.append(split_terms(piece, lane))
    for shard in range(SHARDS):
        main = total[32 * shard : 32 * shard + 32, :]
        start = 8 * channels + 8 * (shard // 2)
        last = total[start : start + 8, :]
        if shard % 2:
            last = pltpu.roll(last, 4, 0)
        extra = quarters[shard % 4][shard // 4 : shard // 4 + 1, :]
        tail = jnp.where(sub < 4, last, jnp.where(sub == 4, extra, 0.0))
        payload_out[shard] = jnp.concatenate([main, tail], axis=0).astype(BF16)


def split_terms(values, lane):
    high = values.astype(BF16).astype(F32)
    return jnp.where(lane < 64, high, values - high)


def resplit(slots):
    main, tail = slots[:, 0:32, :], slots[:, 32:SLOT, :]
    flat = tail.reshape(-1, LANES)
    lane = lax.broadcasted_iota(jnp.int32, flat.shape, 1)
    row = lax.broadcasted_iota(jnp.int32, flat.shape, 0) & 7
    terms = split_terms(flat + pltpu.roll(flat, 64, 1), lane)
    tail = jnp.where(row == 4, terms, flat).reshape(tail.shape)
    return jnp.concatenate([main, tail], axis=1)


def core_body(gathered, slots_out, other_out):
    core, near_count = place(("c",)), slots_out.shape[0]
    mine = pl.ds(core * near_count, near_count)
    total = gathered[0, mine].astype(F32) + gathered[1, mine].astype(F32)
    other = gathered[1 - core, SHARDS]
    other_out[...] = other
    other = other.astype(F32)
    half = slots_out.shape[1] - SLOT
    passed = jnp.where(core == 0, other[half : 2 * half, :], other[0:half, :])
    passed = jnp.broadcast_to(passed[None], (near_count,) + passed.shape)
    slots_out[...] = jnp.concatenate([resplit(total), passed], axis=1).astype(BF16)


def near_body(slots, other, mixed, slots_out, wide_out, top_out, bottom_out):
    samples, rows, cols, _ = mixed.shape
    count, half = slots.shape[0], samples * rows
    core, near = place(("c",)), place(NEAR)
    total = jnp.sum(slots[:, 0:SLOT, :].astype(F32), axis=0)
    slots_out[...] = jnp.broadcast_to(resplit(total[None]).astype(BF16), slots_out.shape)
    apart = lax.rem(jnp.where(core == 0, near + count - 1, near + 1), count)
    passed = slots[apart].astype(F32)[SLOT : SLOT + half, :]
    mate = other[...].astype(F32)
    low = jnp.where(core == 0, passed, mate[half : 2 * half, :])
    high = jnp.where(core == 0, mate[0:half, :], passed)
    for sample in range(samples):
        here = slice(sample * rows, (sample + 1) * rows)
        wide_out[sample, :, 0, :] = low[here, :]
        wide_out[sample, :, 1 : 1 + cols, :] = mixed[sample].astype(F32)
        wide_out[sample, :, 1 + cols, :] = high[here, :]
        top_out[sample] = wide_out[sample, 0].astype(BF16)
        bottom_out[sample] = wide_out[sample, rows - 1].astype(BF16)


def lat_body(slots, slots_out):
    total = jnp.sum(slots[...].astype(F32), axis=0)
    slots_out[...] = jnp.broadcast_to(resplit(total[None]).astype(BF16), slots_out.shape)


def last_body(
    scale, cells, gathered, stats, norm, cotangent, grad_pre, gamma, style, column, demod,
    power, weight, emb_full, feats_out, weight_out, style_out, gamma_out, beta_out,
):
    samples, tile_rows, tile_cols, channels = cotangent.shape
    size = tile_rows * tile_cols
    lane = lanes_of()
    sub = lax.broadcasted_iota(jnp.int32, (TILE, channels), 0)
    main, tails, small = [], [], []
    for shard in range(SHARDS):
        slot = gathered[shard].astype(F32)
        main.append(slot[0:32, :])
        tails.append(slot[32:40, :])
    for row in range(TILE):
        whole = jnp.zeros((1, channels), F32)
        for quarter in range(4):
            piece = tails[4 * row + quarter][4:5, :]
            piece = piece + pltpu.roll(piece, 64, 1)
            if quarter:
                piece = pltpu.roll(piece, 32 * quarter, 1)
            whole = jnp.where((lane >> 5) == quarter, piece, whole)
        small.append(whole)
    demod_sums, style_sums, gamma_sums, beta_sums = small[0:2], small[2:4], small[4:6], small[6:8]
    gain = gamma[...]
    gamma_out[...] = scale * (gamma_sums[0] + gamma_sums[1])
    beta_out[...] = scale * (beta_sums[0] + beta_sums[1])
    shrink = jnp.zeros((channels, channels), F32)
    rows = []
    for sample in range(samples):
        demod_row = demod[sample : sample + 1, :]
        pulled = demod_sums[sample] * (demod_row * demod_row * demod_row)
        style_full = column[sample]
        shrink = shrink + style_full * style_full * pulled
        spent = jnp.sum((power[...] * pulled).T, axis=0, keepdims=True)
        rows.append(style_sums[sample] - style[sample : sample + 1, :] * spent)
    for tap in range(8):
        for part in range(4):
            here = slice(32 * part, 32 * part + 32)
            weight_out[tap, here, :] = scale * (
                main[4 * tap + part] - shrink[here, :] * weight[tap, here, :]
            )
    for pair in range(16):
        here = slice(8 * pair, 8 * pair + 8)
        block = jnp.where(sub < 4, tails[2 * pair], pltpu.roll(tails[2 * pair + 1], 4, 0))
        weight_out[8, here, :] = scale * (block - shrink[here, :] * weight[8, here, :])
    style_out[...] = scale * (emb_full[0] * rows[0] + emb_full[1] * rows[1])
    for sample in range(samples):
        inverse = stats[samples + sample : samples + sample + 1, :]
        product_mean = group_total(gain * beta_sums[sample]) * (1.0 / cells)
        squared_mean = group_total(gain * gamma_sums[sample]) * (1.0 / cells)
        change = inverse * (gain * grad_pre[sample] - product_mean - norm[sample] * squared_mean)
        out = cotangent[sample].reshape(size, channels).astype(F32) + change
        feats_out[sample] = out.astype(BF16).reshape(tile_rows, tile_cols, channels)


def on_device(
    feats, cond, null_field, drop_flags, emb, style_weight, conv_weight, gamma, beta, cotangent
):
    samples, tile_rows, tile_cols, channels = feats.shape
    group_size = channels // GROUPS
    lat_count, lon_count = lax.axis_size(LAT), lax.axis_size(LON)
    devices_all = lat_count * lon_count
    cells_local = tile_rows * tile_cols * group_size
    cells_per_group = cells_local * devices_all
    scale_gradient = 1.0 / math.sqrt(samples * tile_rows * tile_cols * devices_all)
    taps = conv_weight.reshape(9, channels, channels)

    lat_slot = -(-(8 + samples * (tile_cols + 2)) // 16) * 16
    lon_slot = 8 + samples * tile_rows
    mixed, slots, edges = call(
        mix_body,
        (
            array(feats.shape, BF16),
            array((lon_count, lon_slot, LANES), BF16),
            array((SLOT, LANES), BF16),
        ),
        (
            pltpu.VMEM(feats.shape, BF16),
            pltpu.VMEM(feats.shape, BF16),
            pltpu.VMEM(null_field.shape, BF16),
            pltpu.VMEM(feats.shape, BF16),
            pltpu.VMEM(drop_flags.shape, jnp.int32),
            pltpu.SemaphoreType.DMA((2 * samples + 3,)),
        ),
        room=60,
        in_specs=[pl.BlockSpec(memory_space=pl.ANY)] * 5,
    )(feats, cond, null_field, cotangent, drop_flags)
    slots = exchange(slots, LON)
    wide_cot, slots = call(
        functools.partial(merge_body, cells_local),
        (
            array((samples, tile_rows, tile_cols + 2, channels)),
            array((lat_count, lat_slot, LANES), BF16),
        ),
        (pltpu.VMEM((lat_slot, LANES), F32),),
    )(slots, cotangent)
    slots = exchange(slots, LAT)

    taps_shape = (samples, 3, 3 * channels, channels)
    gamma, beta, style, column, demod, power, emb_full, back_taps, fore_taps = call(
        weights_body,
        (
            array((1, channels)),
            array((1, channels)),
            array((samples, channels)),
            array((samples, channels, channels)),
            array((samples, channels)),
            array((channels, channels)),
            array((samples,) + style_weight.shape),
            array(taps_shape, BF16),
            array(taps_shape, BF16),
        ),
    )(emb, style_weight, gamma[None], beta[None], taps)
    spread = pltpu.VMEM((tile_rows + 2, tile_cols + 2, channels), F32)
    shifted = pltpu.VMEM(((tile_rows + 2) * tile_cols, 3 * channels), BF16)
    flat = (samples, tile_rows * tile_cols, channels)
    stats, norm, grad_pre, payload = call(
        functools.partial(sums_body, cells_local * lon_count, cells_per_group),
        (
            array((2 * samples, LANES)),
            array(flat),
            array(flat),
            array((SHARDS + 1, SLOT, LANES), BF16),
        ),
        (
            pltpu.VMEM((2, lat_slot, LANES), F32),
            spread,
            shifted,
            pltpu.VMEM((9 * channels, channels), F32),
        ),
    )(slots, mixed, edges, wide_cot, gamma, beta, back_taps, column, demod, taps)

    near_count = lax.axis_size(NEAR)
    half = samples * tile_rows
    slots, other = call(
        core_body,
        (array((near_count, SLOT + half, LANES), BF16), array((SLOT, LANES), BF16)),
    )(lax.all_gather(payload, "c"))
    border = array((samples, tile_cols + 2, channels), BF16)
    slots, wide_mixed, top, bottom = call(
        near_body,
        (
            array((lat_count, SLOT, LANES), BF16),
            array((samples, tile_rows, tile_cols + 2, channels)),
            border,
            border,
        ),
    )(exchange(slots, NEAR), other, mixed)
    low, high = shift(bottom, LAT, 1, False), shift(top, LAT, -1, False)
    slots = call(lat_body, array((near_count, SLOT, LANES), BF16))(exchange(slots, LAT))
    slots, low, high = lax.optimization_barrier((slots, low, high))
    payload = lax.all_gather(exchange(slots, NEAR), "c")
    block_out = call(forward_body, array(feats.shape, BF16), (spread, shifted))(
        wide_mixed, low, high, fore_taps, stats, gamma, beta
    )

    grad_feats, grad_weight, grad_style, grad_gamma, grad_beta = call(
        functools.partial(last_body, scale_gradient, cells_per_group),
        (
            array(feats.shape, BF16),
            array(taps.shape),
            array(style_weight.shape),
            array((1, LANES)),
            array((1, LANES)),
        ),
    )(
        payload.reshape(SHARDS, SLOT, LANES), stats, norm, cotangent, grad_pre, gamma, style,
        column, demod, power, taps, emb_full,
    )
    return (
        block_out,
        grad_feats,
        grad_weight.reshape(conv_weight.shape),
        grad_style,
        grad_gamma[0],
        grad_beta[0],
    )


def solution(mesh):
    parts = Mesh(mesh.devices.reshape(4, 4, 2, 8, 2), LAT + LON)
    tile = P(None, LAT, LON, None)
    placed = (tile, tile, P(LAT, LON, None), P(), P(), P(), P(), P(), P(), tile)
    return jax.shard_map(
        on_device,
        mesh=parts,
        in_specs=placed,
        out_specs=(tile, tile, P(), P(), P(), P()),
        check_vma=False,
    )
```

```python
import functools
import math

import jax
import jax.numpy as jnp
from jax import lax
from jax.experimental import pallas as pl
from jax.experimental.pallas import tpu as pltpu
from jax.sharding import Mesh, PartitionSpec as P

GROUPS = 32
LAT = ("zh", "x")
LON = ("zl", "y", "c")
NEAR = ("zl", "y")
F32 = jnp.float32
BF16 = jnp.bfloat16
TILE = 8
SHARDS = 32
SLOT = 40
LANES = 128


def shift(block, axes, step, periodic):
    count = lax.axis_size(axes)
    pairs = [(i, i + step) for i in range(count)]
    if periodic:
        pairs = [(source, target % count) for source, target in pairs]
    else:
        pairs = [(source, target) for source, target in pairs if 0 <= target < count]
    return lax.ppermute(block, axes, pairs)


def exchange(block, axes):
    return lax.all_to_all(block, axes, 0, 0)


def call(body, outputs, scratch=(), room=24, **more):
    return pl.pallas_call(
        body,
        out_shape=outputs,
        scratch_shapes=list(scratch),
        **more,
        compiler_params=pltpu.CompilerParams(vmem_limit_bytes=room * 1024 * 1024),
    )


def array(shape, dtype=F32):
    return jax.ShapeDtypeStruct(shape, dtype)


def lanes_of(rows=1):
    return lax.broadcasted_iota(jnp.int32, (rows, LANES), 1)


def group_total(row):
    lane = lanes_of()
    for step in (1, 2):
        after, before = pltpu.roll(row, LANES - step, 1), pltpu.roll(row, step, 1)
        row = row + jnp.where((lane & step) == 0, after, before)
    return row


def weave(first, second):
    return jnp.where((lanes_of() & 1) == 0, first, second)


def unweave(row, sample):
    if sample == 0:
        return weave(row, pltpu.roll(row, 1, 1))
    return weave(pltpu.roll(row, LANES - 1, 1), row)


def place(axes):
    index = 0
    for axis in axes:
        index = index * lax.axis_size(axis) + lax.axis_index(axis)
    return index


def three_terms(value):
    terms = []
    for _ in range(3):
        terms.append(value.astype(BF16).astype(F32))
        value = value - terms[-1]
    return terms


def merged(slots, count):
    rows = slots[:, 0:8, :].astype(F32)
    means = rows[:, 0:1, :] + rows[:, 1:2, :] + rows[:, 2:3, :]
    spreads = rows[:, 3:4, :] + rows[:, 4:5, :] + rows[:, 5:6, :]
    mean = jnp.mean(means, axis=0)
    away = means - mean[None]
    return mean, jnp.sum(spreads + count * away * away, axis=0)


def header(mean, spread):
    return three_terms(mean) + three_terms(spread) + [jnp.zeros((2, LANES), F32)]


def fetcher(arrivals):
    used = iter(range(arrivals.shape[0]))

    def fetch(source, target):
        copy = pltpu.make_async_copy(source, target, arrivals.at[next(used)])
        copy.start()
        return copy

    return fetch


def mix_body(
    feats_in, cond_in, null_in, cot_in, flags_in, mixed_out, slots_out, top_out, bottom_out,
    feats, cond, null, cot, flags, arrivals,
):
    fetch = fetcher(arrivals)
    flags_copy, null_copy = fetch(flags_in, flags), fetch(null_in, null)
    field_copies = [
        (fetch(feats_in.at[sample], feats.at[sample]), fetch(cond_in.at[sample], cond.at[sample]))
        for sample in range(feats.shape[0])
    ]
    cot_copy = fetch(cot_in, cot)
    flags_copy.wait()
    null_copy.wait()
    samples, tile_rows, tile_cols, channels = feats.shape
    cells = tile_rows * tile_cols
    size = cells * (channels // GROUPS)
    null32 = null[...].astype(F32)
    means, spreads = [], []
    for sample in range(samples):
        for copy in field_copies[sample]:
            copy.wait()
        dropped = flags[sample : sample + 1, :].astype(F32).reshape(1, 1, channels)
        mixed = (
            feats[sample].astype(F32) + dropped * null32 + (1.0 - dropped) * cond[sample].astype(F32)
        ).astype(BF16)
        mixed_out[sample] = mixed
        top_out[0, sample] = mixed[0]
        bottom_out[0, sample] = mixed[tile_rows - 1]
        wide = mixed.astype(F32).reshape(cells, channels)
        mean = group_total(jnp.sum(wide, axis=0, keepdims=True)) * (1.0 / size)
        away = wide - mean
        means.append(mean)
        spreads.append(group_total(jnp.sum(away * away, axis=0, keepdims=True)))
    rows = header(weave(*means), weave(*spreads))
    cot_copy.wait()
    firsts, lasts = [], []
    for sample in range(samples):
        top_out[1, sample] = cot[sample, 0]
        bottom_out[1, sample] = cot[sample, tile_rows - 1]
        wide = cot[sample].astype(F32)
        firsts.append(wide[:, 0, :])
        lasts.append(wide[:, tile_cols - 1, :])
    slots_out[...] = jnp.broadcast_to(
        jnp.concatenate(rows + firsts, axis=0).astype(BF16)[None], slots_out.shape
    )
    after = lax.rem(place(LON) + 1, slots_out.shape[0])
    slots_out[after] = jnp.concatenate(rows + lasts, axis=0).astype(BF16)


def merge_body(count, slots, cot, wide_out, slots_out):
    samples, tile_rows, tile_cols, channels = cot.shape
    lon_count, lat_count = slots.shape[0], slots_out.shape[0]
    mean, spread = merged(slots, count)
    me = place(LON)
    before = slots[lax.rem(me + lon_count - 1, lon_count)].astype(F32)
    after = slots[lax.rem(me + 1, lon_count)].astype(F32)
    for sample in range(samples):
        here = slice(8 + sample * tile_rows, 8 + (sample + 1) * tile_rows)
        wide_out[sample, :, 0, :] = before[here, :]
        wide_out[sample, :, 1 : 1 + tile_cols, :] = cot[sample].astype(F32)
        wide_out[sample, :, 1 + tile_cols, :] = after[here, :]
    rows = header(mean, spread)

    def slot(row):
        corners = [
            wide_out[sample, row, side : side + 1, :]
            for sample in range(samples)
            for side in (0, 1 + tile_cols)
        ]
        spare = jnp.zeros((slots_out.shape[1] - 8 - len(corners), channels), F32)
        return jnp.concatenate(rows + corners + [spare], axis=0).astype(BF16)

    slots_out[...] = jnp.broadcast_to(slot(0)[None], slots_out.shape)
    row = place(LAT)

    @pl.when(row < lat_count - 1)
    def _():
        slots_out[row + 1] = slot(tile_rows - 1)


def columns_body(mixed, low, high, edges_out, send_out):
    samples, _, tile_cols, channels = mixed.shape
    spare = [jnp.zeros((send_out.shape[0] - edges_out.shape[0] // 2, channels), F32)]

    def column(at):
        parts = []
        for sample in range(samples):
            parts.append(low[0, sample].astype(F32)[at : at + 1, :])
            parts.append(mixed[sample].astype(F32)[:, at, :])
            parts.append(high[0, sample].astype(F32)[at : at + 1, :])
        return parts

    first, last = column(0), column(tile_cols - 1)
    edges_out[...] = jnp.concatenate(first + last, axis=0).astype(BF16)
    first, last = jnp.concatenate(first + spare, axis=0), jnp.concatenate(last + spare, axis=0)
    send_out[...] = jnp.where(place(("c",)) == 0, first, last).astype(BF16)


def weights_body(
    emb, style_weight, gamma, beta, weight,
    gamma_out, beta_out, style_out, column_out, demod_out, power_out, emb_out, back_out, taps_out,
):
    gamma_out[...] = gamma[...]
    beta_out[...] = beta[...]
    power = jnp.zeros(weight.shape[1:], F32)
    for tap in range(9):
        power = power + weight[tap] * weight[tap]
    samples, channels = emb.shape[0], weight.shape[2]
    exact = lax.Precision.HIGHEST
    style = 1.0 + jnp.dot(
        emb[...], style_weight[...], precision=exact, preferred_element_type=F32
    )
    squares = jnp.dot(style * style, power, precision=exact, preferred_element_type=F32)
    demod = lax.rsqrt(squares + 1e-08)
    style_out[...] = style
    demod_out[...] = demod
    power_out[...] = power
    for sample in range(samples):
        here = slice(sample, sample + 1)
        column = jnp.broadcast_to(style[here, :], (channels, channels)).T
        column_out[sample] = column
        emb_out[sample] = jnp.broadcast_to(emb[here, :], (channels, emb.shape[1])).T
        for tap in range(9):
            row, col = tap // 3, tap % 3
            block = weight[tap] * column * demod[here, :]
            taps_out[sample, row, col * channels : (col + 1) * channels, :] = block.astype(BF16)
            row, col = 2 - row, 2 - col
            back_out[sample, row, col * channels : (col + 1) * channels, :] = block.T.astype(BF16)


def windows(spread, shifted, rows, cols):
    channels = spread.shape[-1]
    for tap in range(3):
        moved = spread[:, tap : tap + cols, :].reshape((rows + 2) * cols, channels)
        shifted[:, tap * channels : (tap + 1) * channels] = moved.astype(BF16)


def forward_body(
    mixed, low, high, other, passed, taps, stats, gamma, beta, block_out, spread, shifted
):
    samples, rows, cols, _ = mixed.shape
    size = rows * cols
    row = lax.broadcasted_iota(jnp.int32, spread.shape, 0) + place(LAT) * rows
    inside = (row > 0) & (row <= rows * lax.axis_size(LAT))
    core = place(("c",))
    mate, away = other[...].astype(F32), passed[...].astype(F32)
    half = samples * (rows + 2)
    left = jnp.where(core == 0, away[:half, :], mate[half : 2 * half, :])
    right = jnp.where(core == 0, mate[:half, :], away[:half, :])
    for sample in range(samples):
        here = slice(sample * (rows + 2), (sample + 1) * (rows + 2))
        spread[:, 0, :] = left[here, :]
        spread[:, 1 + cols, :] = right[here, :]
        spread[0, 1 : 1 + cols, :] = low[0, sample].astype(F32)
        spread[1 : 1 + rows, 1 : 1 + cols, :] = mixed[sample].astype(F32)
        spread[1 + rows, 1 : 1 + cols, :] = high[0, sample].astype(F32)
        mean = stats[sample : sample + 1, :][None]
        inverse = stats[samples + sample : samples + sample + 1, :][None]
        pre = (spread[...] - mean) * inverse * gamma[...][None] + beta[...][None]
        spread[...] = jnp.where(inside, pre / (1.0 + jnp.exp(-pre)), 0.0)
        windows(spread, shifted, rows, cols)
        total = mixed[sample].astype(F32).reshape(size, -1)
        for row_tap in range(3):
            window = shifted[row_tap * cols : row_tap * cols + size, :]
            total = total + jnp.dot(window, taps[sample, row_tap], preferred_element_type=F32)
        block_out[sample] = total.astype(BF16).reshape(rows, cols, -1)


def sums_body(
    count, cells, slots, mixed, edges, wide, low, high, gamma, beta, back_taps, column, demod,
    weight, stats_out, grad_far, payload_out, edge, spread, shifted, total, grad_out, arrivals,
):
    samples, rows, cols, channels = mixed.shape
    size = rows * cols
    fetch = fetcher(arrivals)
    copies = []
    mean_all, spread_all = merged(slots, count)
    inverse_all = lax.rsqrt(spread_all * (1.0 / cells) + 1e-05)
    lat_count, row = slots.shape[0], place(LAT)
    below = slots[lax.max(row - 1, 0)].astype(F32)
    above = slots[lax.min(row + 1, lat_count - 1)].astype(F32)
    edge[0] = jnp.where(row > 0, below, 0.0)
    edge[1] = jnp.where(row < lat_count - 1, above, 0.0)
    sums = [[], [], [], []]
    for sample in range(samples):
        mean, inverse = unweave(mean_all, sample), unweave(inverse_all, sample)
        stats_out[sample : sample + 1, :] = mean
        stats_out[samples + sample : samples + sample + 1, :] = inverse
        flat = mixed[sample].reshape(size, channels).astype(F32)
        norm = (flat - mean) * inverse
        pre = norm * gamma[...] + beta[...]
        sig = 1.0 / (1.0 + jnp.exp(-pre))
        act = (pre * sig).astype(BF16)
        slope = sig * (1.0 + pre * (1.0 - sig))
        spread[1 : 1 + rows] = wide[sample]
        for at, halo, corner in ((0, low, edge[0]), (1 + rows, high, edge[1])):
            spread[at, 1 : 1 + cols, :] = halo[1, sample].astype(F32)
            start = 8 + 2 * sample
            spread[at, 0:1, :] = corner[start : start + 1, :]
            spread[at, 1 + cols : 2 + cols, :] = corner[start + 1 : start + 2, :]
        windows(spread, shifted, rows, cols)
        style_full = column[sample]
        demod_row = demod[sample : sample + 1, :]
        both = style_full * demod_row
        product = jnp.zeros((channels, channels), F32)
        grad_act = jnp.zeros((size, channels), F32)
        for row_tap in range(3):
            window = shifted[row_tap * cols : row_tap * cols + size, :]
            grad_act = grad_act + jnp.dot(
                window, back_taps[sample, row_tap], preferred_element_type=F32
            )
            grad = lax.dot_general(
                act, window, (((0,), (0,)), ((), ())), preferred_element_type=F32
            )
            for col_tap in range(3):
                tap = (2 - row_tap) * 3 + 2 - col_tap
                block = grad[:, col_tap * channels : (col_tap + 1) * channels]
                product = product + block * weight[tap]
                here = slice(tap * channels, (tap + 1) * channels)
                part = block * both
                total[here, :] = part if sample == 0 else total[here, :] + part
        grad_pre = grad_act * slope
        grad_out[sample] = grad_pre
        copies.append(fetch(grad_out.at[sample], grad_far.at[sample]))
        sums[0].append(jnp.sum(product * style_full, axis=0, keepdims=True))
        sums[1].append(jnp.sum((product * demod_row).T, axis=0, keepdims=True))
        sums[2].append(jnp.sum(grad_pre * norm, axis=0, keepdims=True))
        sums[3].append(jnp.sum(grad_pre, axis=0, keepdims=True))
    payload_out[SHARDS] = edges[...]
    small = jnp.concatenate(sum(sums, []), axis=0)
    lane = lanes_of(TILE)
    sub = lax.broadcasted_iota(jnp.int32, (TILE, channels), 0)
    quarters = []
    for quarter in range(4):
        turned = pltpu.roll(small, LANES - 32 * quarter, 1) if quarter else small
        piece = jnp.where(lane < 64, turned, pltpu.roll(turned, 64, 1))
        piece = jnp.where((lane & 32) == 0, piece, 0.0)
        quarters.append(split_terms(piece, lane))
    for shard in range(SHARDS):
        main = total[32 * shard : 32 * shard + 32, :]
        start = 8 * channels + 8 * (shard // 2)
        last = total[start : start + 8, :]
        if shard % 2:
            last = pltpu.roll(last, 4, 0)
        extra = quarters[shard % 4][shard // 4 : shard // 4 + 1, :]
        tail = jnp.where(sub < 4, last, jnp.where(sub == 4, extra, 0.0))
        payload_out[shard] = jnp.concatenate([main, tail], axis=0).astype(BF16)
    for copy in copies:
        copy.wait()


def split_terms(values, lane):
    high = values.astype(BF16).astype(F32)
    return jnp.where(lane < 64, high, values - high)


def resplit(slots):
    main, tail = slots[:, 0:32, :], slots[:, 32:SLOT, :]
    flat = tail.reshape(-1, LANES)
    lane = lax.broadcasted_iota(jnp.int32, flat.shape, 1)
    row = lax.broadcasted_iota(jnp.int32, flat.shape, 0) & 7
    terms = split_terms(flat + pltpu.roll(flat, 64, 1), lane)
    tail = jnp.where(row == 4, terms, flat).reshape(tail.shape)
    return jnp.concatenate([main, tail], axis=1)


def core_body(gathered, slots_out, other_out):
    core, near_count = place(("c",)), slots_out.shape[0]
    mine = pl.ds(core * near_count, near_count)
    total = gathered[0, mine].astype(F32) + gathered[1, mine].astype(F32)
    other_out[...] = gathered[1 - core, SHARDS]
    slots_out[...] = resplit(total).astype(BF16)


def sum_body(slots, slots_out):
    total = jnp.sum(slots[...].astype(F32), axis=0)
    slots_out[...] = jnp.broadcast_to(resplit(total[None]).astype(BF16), slots_out.shape)


def last_body(
    scale, cells, gathered, stats, mixed, cotangent, grad_pre, gamma, style, column, demod,
    power, weight, emb_full, feats_out, weight_out, style_out, gamma_out, beta_out,
):
    samples, tile_rows, tile_cols, channels = cotangent.shape
    size = tile_rows * tile_cols
    lane = lanes_of()
    sub = lax.broadcasted_iota(jnp.int32, (TILE, channels), 0)
    main, tails, small = [], [], []
    for shard in range(SHARDS):
        slot = gathered[shard].astype(F32)
        main.append(slot[0:32, :])
        tails.append(slot[32:40, :])
    for row in range(TILE):
        whole = jnp.zeros((1, channels), F32)
        for quarter in range(4):
            piece = tails[4 * row + quarter][4:5, :]
            piece = piece + pltpu.roll(piece, 64, 1)
            if quarter:
                piece = pltpu.roll(piece, 32 * quarter, 1)
            whole = jnp.where((lane >> 5) == quarter, piece, whole)
        small.append(whole)
    demod_sums, style_sums, gamma_sums, beta_sums = small[0:2], small[2:4], small[4:6], small[6:8]
    gain = gamma[...]
    gamma_out[...] = scale * (gamma_sums[0] + gamma_sums[1])
    beta_out[...] = scale * (beta_sums[0] + beta_sums[1])
    shrink = jnp.zeros((channels, channels), F32)
    rows = []
    for sample in range(samples):
        demod_row = demod[sample : sample + 1, :]
        pulled = demod_sums[sample] * (demod_row * demod_row * demod_row)
        style_full = column[sample]
        shrink = shrink + style_full * style_full * pulled
        spent = jnp.sum((power[...] * pulled).T, axis=0, keepdims=True)
        rows.append(style_sums[sample] - style[sample : sample + 1, :] * spent)
    for tap in range(8):
        for part in range(4):
            here = slice(32 * part, 32 * part + 32)
            weight_out[tap, here, :] = scale * (
                main[4 * tap + part] - shrink[here, :] * weight[tap, here, :]
            )
    for pair in range(16):
        here = slice(8 * pair, 8 * pair + 8)
        block = jnp.where(sub < 4, tails[2 * pair], pltpu.roll(tails[2 * pair + 1], 4, 0))
        weight_out[8, here, :] = scale * (block - shrink[here, :] * weight[8, here, :])
    style_out[...] = scale * (emb_full[0] * rows[0] + emb_full[1] * rows[1])
    for sample in range(samples):
        inverse = stats[samples + sample : samples + sample + 1, :]
        product_mean = group_total(gain * beta_sums[sample]) * (1.0 / cells)
        squared_mean = group_total(gain * gamma_sums[sample]) * (1.0 / cells)
        flat = mixed[sample].astype(F32).reshape(size, channels)
        norm = (flat - stats[sample : sample + 1, :]) * inverse
        change = inverse * (gain * grad_pre[sample] - product_mean - norm * squared_mean)
        out = cotangent[sample].reshape(size, channels).astype(F32) + change
        feats_out[sample] = out.astype(BF16).reshape(tile_rows, tile_cols, channels)


def on_device(
    feats, cond, null_field, drop_flags, emb, style_weight, conv_weight, gamma, beta, cotangent
):
    samples, tile_rows, tile_cols, channels = feats.shape
    group_size = channels // GROUPS
    lat_count, lon_count = lax.axis_size(LAT), lax.axis_size(LON)
    devices_all = lat_count * lon_count
    cells_local = tile_rows * tile_cols * group_size
    cells_per_group = cells_local * devices_all
    scale_gradient = 1.0 / math.sqrt(samples * tile_rows * tile_cols * devices_all)
    taps = conv_weight.reshape(9, channels, channels)

    lon_slot, lat_slot = 8 + samples * tile_rows, 16
    rim = array((2, samples, tile_cols, channels), BF16)
    mixed, slots, top, bottom = call(
        mix_body,
        (array(feats.shape, BF16), array((lon_count, lon_slot, LANES), BF16), rim, rim),
        (
            pltpu.VMEM(feats.shape, BF16),
            pltpu.VMEM(feats.shape, BF16),
            pltpu.VMEM(null_field.shape, BF16),
            pltpu.VMEM(feats.shape, BF16),
            pltpu.VMEM(drop_flags.shape, jnp.int32),
            pltpu.SemaphoreType.DMA((2 * samples + 3,)),
        ),
        room=60,
        in_specs=[pl.BlockSpec(memory_space=pl.ANY)] * 5,
    )(feats, cond, null_field, cotangent, drop_flags)
    slots = exchange(slots, LON)
    low, high = shift(bottom, LAT, 1, False), shift(top, LAT, -1, False)
    wide_cot, slots = call(
        functools.partial(merge_body, cells_local),
        (
            array((samples, tile_rows, tile_cols + 2, channels)),
            array((lat_count, lat_slot, LANES), BF16),
        ),
    )(slots, cotangent)
    slots, low, high = lax.optimization_barrier((slots, low, high))
    slots = exchange(slots, LAT)
    half = samples * (tile_rows + 2)
    edges, passed = call(
        columns_body, (array((SLOT, LANES), BF16), array((-(-half // 8) * 8, LANES), BF16))
    )(mixed, low, high)
    pairs = [(i, (i + 1) % lon_count) for i in range(1, lon_count, 2)]
    passed = lax.ppermute(passed, LON, pairs + [(target, source) for source, target in pairs])

    taps_shape = (samples, 3, 3 * channels, channels)
    gamma, beta, style, column, demod, power, emb_full, back_taps, fore_taps = call(
        weights_body,
        (
            array((1, channels)),
            array((1, channels)),
            array((samples, channels)),
            array((samples, channels, channels)),
            array((samples, channels)),
            array((channels, channels)),
            array((samples,) + style_weight.shape),
            array(taps_shape, BF16),
            array(taps_shape, BF16),
        ),
    )(emb, style_weight, gamma[None], beta[None], taps)
    spread = pltpu.VMEM((tile_rows + 2, tile_cols + 2, channels), F32)
    shifted = pltpu.VMEM(((tile_rows + 2) * tile_cols, 3 * channels), BF16)
    flat = (samples, tile_rows * tile_cols, channels)
    near = pl.BlockSpec(memory_space=pltpu.VMEM)
    stats, grad_pre, payload = call(
        functools.partial(sums_body, cells_local * lon_count, cells_per_group),
        (
            array((2 * samples, LANES)),
            array(flat),
            array((SHARDS + 1, SLOT, LANES), BF16),
        ),
        (
            pltpu.VMEM((2, lat_slot, LANES), F32),
            spread,
            shifted,
            pltpu.VMEM((9 * channels, channels), F32),
            pltpu.VMEM(flat, F32),
            pltpu.SemaphoreType.DMA((samples,)),
        ),
        out_specs=(near, pl.BlockSpec(memory_space=pltpu.HBM), near),
    )(
        slots, mixed, edges, wide_cot, low, high, gamma, beta, back_taps, column, demod, taps
    )

    near_count = lax.axis_size(NEAR)
    shard = array((near_count, SLOT, LANES), BF16)
    slots, other = call(core_body, (shard, array((SLOT, LANES), BF16)))(
        lax.all_gather(payload, "c")
    )
    slots, passed = lax.optimization_barrier((slots, passed))
    summed = array((lat_count, SLOT, LANES), BF16)
    slots = call(sum_body, summed)(exchange(slots, NEAR))
    slots = call(sum_body, shard)(exchange(slots, LAT))
    payload = lax.all_gather(exchange(slots, NEAR), "c")
    block_out = call(forward_body, array(feats.shape, BF16), (spread, shifted))(
        mixed, low, high, other, passed, fore_taps, stats, gamma, beta
    )

    grad_feats, grad_weight, grad_style, grad_gamma, grad_beta = call(
        functools.partial(last_body, scale_gradient, cells_per_group),
        (
            array(feats.shape, BF16),
            array(taps.shape),
            array(style_weight.shape),
            array((1, LANES)),
            array((1, LANES)),
        ),
    )(
        payload.reshape(SHARDS, SLOT, LANES), stats, mixed, cotangent, grad_pre, gamma, style,
        column, demod, power, taps, emb_full,
    )
    return (
        block_out,
        grad_feats,
        grad_weight.reshape(conv_weight.shape),
        grad_style,
        grad_gamma[0],
        grad_beta[0],
    )


def solution(mesh):
    parts = Mesh(mesh.devices.reshape(4, 4, 2, 8, 2), LAT + LON)
    tile = P(None, LAT, LON, None)
    placed = (tile, tile, P(LAT, LON, None), P(), P(), P(), P(), P(), P(), tile)
    return jax.shard_map(
        on_device,
        mesh=parts,
        in_specs=placed,
        out_specs=(tile, tile, P(), P(), P(), P()),
        check_vma=False,
    )
```

```python
import functools
import math

import jax
import jax.numpy as jnp
from jax import lax
from jax.experimental import pallas as pl
from jax.experimental.pallas import tpu as pltpu
from jax.sharding import Mesh, PartitionSpec as P

GROUPS = 32
LAT = ("zh", "x")
LON = ("zl", "y", "c")
NEAR = ("zl", "y")
F32 = jnp.float32
BF16 = jnp.bfloat16
TILE = 8
SHARDS = 32
SLOT = 40
LANES = 128


def shift(block, axes, step, periodic):
    count = lax.axis_size(axes)
    pairs = [(i, i + step) for i in range(count)]
    if periodic:
        pairs = [(source, target % count) for source, target in pairs]
    else:
        pairs = [(source, target) for source, target in pairs if 0 <= target < count]
    return lax.ppermute(block, axes, pairs)


def exchange(block, axes):
    return lax.all_to_all(block, axes, 0, 0)


def call(body, outputs, scratch=(), room=24, **more):
    return pl.pallas_call(
        body,
        out_shape=outputs,
        scratch_shapes=list(scratch),
        **more,
        compiler_params=pltpu.CompilerParams(vmem_limit_bytes=room * 1024 * 1024),
    )


def array(shape, dtype=F32):
    return jax.ShapeDtypeStruct(shape, dtype)


def lanes_of(rows=1):
    return lax.broadcasted_iota(jnp.int32, (rows, LANES), 1)


def group_total(row):
    lane = lanes_of()
    for step in (1, 2):
        after, before = pltpu.roll(row, LANES - step, 1), pltpu.roll(row, step, 1)
        row = row + jnp.where((lane & step) == 0, after, before)
    return row


def weave(first, second):
    return jnp.where((lanes_of() & 1) == 0, first, second)


def unweave(row, sample):
    if sample == 0:
        return weave(row, pltpu.roll(row, 1, 1))
    return weave(pltpu.roll(row, LANES - 1, 1), row)


def place(axes):
    index = 0
    for axis in axes:
        index = index * lax.axis_size(axis) + lax.axis_index(axis)
    return index


def three_terms(value):
    terms = []
    for _ in range(3):
        terms.append(value.astype(BF16).astype(F32))
        value = value - terms[-1]
    return terms


def merged(slots, count):
    rows = slots[:, 0:8, :].astype(F32)
    means = rows[:, 0:1, :] + rows[:, 1:2, :] + rows[:, 2:3, :]
    spreads = rows[:, 3:4, :] + rows[:, 4:5, :] + rows[:, 5:6, :]
    mean = jnp.mean(means, axis=0)
    away = means - mean[None]
    return mean, jnp.sum(spreads + count * away * away, axis=0)


def header(mean, spread):
    return three_terms(mean) + three_terms(spread) + [jnp.zeros((2, LANES), F32)]


def fetcher(arrivals):
    used = iter(range(arrivals.shape[0]))

    def fetch(source, target):
        copy = pltpu.make_async_copy(source, target, arrivals.at[next(used)])
        copy.start()
        return copy

    return fetch


def mix_body(
    feats_in, cond_in, null_in, cot_in, flags_in, mixed_out, slots_out, edges_out, send_out,
    feats, cond, null, cot, flags, arrivals,
):
    fetch = fetcher(arrivals)
    flags_copy, null_copy = fetch(flags_in, flags), fetch(null_in, null)
    field_copies = [
        (fetch(feats_in.at[sample], feats.at[sample]), fetch(cond_in.at[sample], cond.at[sample]))
        for sample in range(feats.shape[0])
    ]
    cot_copy = fetch(cot_in, cot)
    flags_copy.wait()
    null_copy.wait()
    samples, tile_rows, tile_cols, channels = feats.shape
    cells = tile_rows * tile_cols
    size = cells * (channels // GROUPS)
    null32 = null[...].astype(F32)
    means, spreads, firsts, lasts = [], [], [], []
    for sample in range(samples):
        for copy in field_copies[sample]:
            copy.wait()
        dropped = flags[sample : sample + 1, :].astype(F32).reshape(1, 1, channels)
        mixed = (
            feats[sample].astype(F32) + dropped * null32 + (1.0 - dropped) * cond[sample].astype(F32)
        ).astype(BF16)
        mixed_out[sample] = mixed
        wide = mixed.astype(F32)
        firsts.append(wide[:, 0, :])
        lasts.append(wide[:, tile_cols - 1, :])
        wide = wide.reshape(cells, channels)
        mean = group_total(jnp.sum(wide, axis=0, keepdims=True)) * (1.0 / size)
        away = wide - mean
        means.append(mean)
        spreads.append(group_total(jnp.sum(away * away, axis=0, keepdims=True)))
    spare = jnp.zeros((SLOT - 2 * samples * tile_rows, channels), F32)
    edges_out[...] = jnp.concatenate(firsts + lasts + [spare], axis=0).astype(BF16)
    chosen = [
        jnp.where(place(("c",)) == 0, first, last) for first, last in zip(firsts, lasts, strict=True)
    ]
    send_out[...] = jnp.concatenate(chosen, axis=0).astype(BF16)
    rows = header(weave(*means), weave(*spreads))
    cot_copy.wait()
    firsts, lasts = [], []
    for sample in range(samples):
        wide = cot[sample].astype(F32)
        firsts.append(wide[:, 0, :])
        lasts.append(wide[:, tile_cols - 1, :])
    slots_out[...] = jnp.broadcast_to(
        jnp.concatenate(rows + firsts, axis=0).astype(BF16)[None], slots_out.shape
    )
    after = lax.rem(place(LON) + 1, slots_out.shape[0])
    slots_out[after] = jnp.concatenate(rows + lasts, axis=0).astype(BF16)


def merge_body(count, slots, cot, wide_out, slots_out, edge):
    samples, tile_rows, tile_cols, channels = cot.shape
    lon_count, lat_count = slots.shape[0], slots_out.shape[0]
    mean, spread = merged(slots, count)
    me = place(LON)
    before = slots[lax.rem(me + lon_count - 1, lon_count)].astype(F32)
    after = slots[lax.rem(me + 1, lon_count)].astype(F32)
    for sample in range(samples):
        here = slice(8 + sample * tile_rows, 8 + (sample + 1) * tile_rows)
        wide_out[sample, :, 0, :] = before[here, :]
        wide_out[sample, :, 1 : 1 + tile_cols, :] = cot[sample].astype(F32)
        wide_out[sample, :, 1 + tile_cols, :] = after[here, :]
    edge[...] = jnp.zeros(edge.shape, F32)
    edge[0:8, :] = jnp.concatenate(header(mean, spread), axis=0)
    span = tile_cols + 2
    for sample in range(samples):
        edge[8 + sample * span : 8 + (sample + 1) * span, :] = wide_out[sample, 0]
    slots_out[...] = jnp.broadcast_to(edge[...].astype(BF16)[None], slots_out.shape)
    for sample in range(samples):
        edge[8 + sample * span : 8 + (sample + 1) * span, :] = wide_out[sample, tile_rows - 1]
    row = place(LAT)

    @pl.when(row < lat_count - 1)
    def _():
        slots_out[row + 1] = edge[...].astype(BF16)


def weights_body(
    emb, style_weight, gamma, beta, weight,
    gamma_out, beta_out, style_out, column_out, demod_out, power_out, emb_out, back_out, taps_out,
):
    gamma_out[...] = gamma[...]
    beta_out[...] = beta[...]
    power = jnp.zeros(weight.shape[1:], F32)
    for tap in range(9):
        power = power + weight[tap] * weight[tap]
    samples, channels = emb.shape[0], weight.shape[2]
    exact = lax.Precision.HIGHEST
    style = 1.0 + jnp.dot(
        emb[...], style_weight[...], precision=exact, preferred_element_type=F32
    )
    squares = jnp.dot(style * style, power, precision=exact, preferred_element_type=F32)
    demod = lax.rsqrt(squares + 1e-08)
    style_out[...] = style
    demod_out[...] = demod
    power_out[...] = power
    for sample in range(samples):
        here = slice(sample, sample + 1)
        column = jnp.broadcast_to(style[here, :], (channels, channels)).T
        column_out[sample] = column
        emb_out[sample] = jnp.broadcast_to(emb[here, :], (channels, emb.shape[1])).T
        for tap in range(9):
            row, col = tap // 3, tap % 3
            block = weight[tap] * column * demod[here, :]
            taps_out[sample, row, col * channels : (col + 1) * channels, :] = block.astype(BF16)
            row, col = 2 - row, 2 - col
            back_out[sample, row, col * channels : (col + 1) * channels, :] = block.T.astype(BF16)


def windows(spread, shifted, rows, cols):
    channels = spread.shape[-1]
    for tap in range(3):
        moved = spread[:, tap : tap + cols, :].reshape((rows + 2) * cols, channels)
        shifted[:, tap * channels : (tap + 1) * channels] = moved.astype(BF16)


def forward_body(wide, low, high, taps, stats, gamma, beta, block_out, spread, shifted):
    samples, rows, cols = wide.shape[0], wide.shape[1], wide.shape[2] - 2
    size = rows * cols
    row = lax.broadcasted_iota(jnp.int32, spread.shape, 0) + place(LAT) * rows
    inside = (row > 0) & (row <= rows * lax.axis_size(LAT))
    for sample in range(samples):
        spread[0] = low[sample].astype(F32)
        spread[1 : 1 + rows] = wide[sample]
        spread[1 + rows] = high[sample].astype(F32)
        mean = stats[sample : sample + 1, :][None]
        inverse = stats[samples + sample : samples + sample + 1, :][None]
        pre = (spread[...] - mean) * inverse * gamma[...][None] + beta[...][None]
        spread[...] = jnp.where(inside, pre / (1.0 + jnp.exp(-pre)), 0.0)
        windows(spread, shifted, rows, cols)
        total = wide[sample, :, 1 : 1 + cols, :].reshape(size, -1)
        for row_tap in range(3):
            window = shifted[row_tap * cols : row_tap * cols + size, :]
            total = total + jnp.dot(window, taps[sample, row_tap], preferred_element_type=F32)
        block_out[sample] = total.astype(BF16).reshape(rows, cols, -1)


def sums_body(
    count, cells, slots, mixed, edges, wide, gamma, beta, back_taps, column, demod, weight,
    stats_out, grad_far, payload_out, edge, spread, shifted, total, grad_out, arrivals,
):
    samples, rows, cols, channels = mixed.shape
    size, span = rows * cols, cols + 2
    mean_all, spread_all = merged(slots, count)
    inverse_all = lax.rsqrt(spread_all * (1.0 / cells) + 1e-05)
    lat_count, row = slots.shape[0], place(LAT)
    below = slots[lax.max(row - 1, 0)].astype(F32)
    above = slots[lax.min(row + 1, lat_count - 1)].astype(F32)
    edge[0] = jnp.where(row > 0, below, 0.0)
    edge[1] = jnp.where(row < lat_count - 1, above, 0.0)
    fetch = fetcher(arrivals)
    sums = [[], [], [], []]
    acts, copies = [], []
    for sample in range(samples):
        mean, inverse = unweave(mean_all, sample), unweave(inverse_all, sample)
        stats_out[sample : sample + 1, :] = mean
        stats_out[samples + sample : samples + sample + 1, :] = inverse
        flat = mixed[sample].reshape(size, channels).astype(F32)
        norm = (flat - mean) * inverse
        pre = norm * gamma[...] + beta[...]
        sig = 1.0 / (1.0 + jnp.exp(-pre))
        acts.append((pre * sig).astype(BF16))
        here = slice(8 + sample * span, 8 + (sample + 1) * span)
        spread[0] = edge[0, here, :]
        spread[1 : 1 + rows] = wide[sample]
        spread[1 + rows] = edge[1, here, :]
        windows(spread, shifted.at[sample], rows, cols)
        grad_act = jnp.zeros((size, channels), F32)
        for row_tap in range(3):
            window = shifted[sample, row_tap * cols : row_tap * cols + size, :]
            grad_act = grad_act + jnp.dot(
                window, back_taps[sample, row_tap], preferred_element_type=F32
            )
        grad_pre = grad_act * (sig * (1.0 + pre * (1.0 - sig)))
        grad_out[sample] = grad_pre
        copies.append(fetch(grad_out.at[sample], grad_far.at[sample]))
        sums[2].append(jnp.sum(grad_pre * norm, axis=0, keepdims=True))
        sums[3].append(jnp.sum(grad_pre, axis=0, keepdims=True))
    for sample in range(samples):
        style_full = column[sample]
        demod_row = demod[sample : sample + 1, :]
        both = style_full * demod_row
        product = jnp.zeros((channels, channels), F32)
        for row_tap in range(3):
            window = shifted[sample, row_tap * cols : row_tap * cols + size, :]
            grad = lax.dot_general(
                acts[sample], window, (((0,), (0,)), ((), ())), preferred_element_type=F32
            )
            for col_tap in range(3):
                tap = (2 - row_tap) * 3 + 2 - col_tap
                block = grad[:, col_tap * channels : (col_tap + 1) * channels]
                product = product + block * weight[tap]
                here = slice(tap * channels, (tap + 1) * channels)
                part = block * both
                total[here, :] = part if sample == 0 else total[here, :] + part
        sums[0].append(jnp.sum(product * style_full, axis=0, keepdims=True))
        sums[1].append(jnp.sum((product * demod_row).T, axis=0, keepdims=True))
    payload_out[SHARDS] = edges[...]
    small = jnp.concatenate(sum(sums, []), axis=0)
    lane = lanes_of(TILE)
    sub = lax.broadcasted_iota(jnp.int32, (TILE, channels), 0)
    quarters = []
    for quarter in range(4):
        turned = pltpu.roll(small, LANES - 32 * quarter, 1) if quarter else small
        piece = jnp.where(lane < 64, turned, pltpu.roll(turned, 64, 1))
        piece = jnp.where((lane & 32) == 0, piece, 0.0)
        quarters.append(split_terms(piece, lane))
    for shard in range(SHARDS):
        main = total[32 * shard : 32 * shard + 32, :]
        start = 8 * channels + 8 * (shard // 2)
        last = total[start : start + 8, :]
        if shard % 2:
            last = pltpu.roll(last, 4, 0)
        extra = quarters[shard % 4][shard // 4 : shard // 4 + 1, :]
        tail = jnp.where(sub < 4, last, jnp.where(sub == 4, extra, 0.0))
        payload_out[shard] = jnp.concatenate([main, tail], axis=0).astype(BF16)
    for copy in copies:
        copy.wait()


def split_terms(values, lane):
    high = values.astype(BF16).astype(F32)
    return jnp.where(lane < 64, high, values - high)


def resplit(slots):
    main, tail = slots[:, 0:32, :], slots[:, 32:SLOT, :]
    flat = tail.reshape(-1, LANES)
    lane = lax.broadcasted_iota(jnp.int32, flat.shape, 1)
    row = lax.broadcasted_iota(jnp.int32, flat.shape, 0) & 7
    terms = split_terms(flat + pltpu.roll(flat, 64, 1), lane)
    tail = jnp.where(row == 4, terms, flat).reshape(tail.shape)
    return jnp.concatenate([main, tail], axis=1)


def core_body(gathered, slots_out, other_out):
    core, near_count = place(("c",)), slots_out.shape[0]
    mine = pl.ds(core * near_count, near_count)
    total = gathered[0, mine].astype(F32) + gathered[1, mine].astype(F32)
    other_out[...] = gathered[1 - core, SHARDS]
    slots_out[...] = resplit(total).astype(BF16)


def near_body(slots, other, passed, mixed, slots_out, wide_out, top_out, bottom_out):
    samples, rows, cols, _ = mixed.shape
    half, core = samples * rows, place(("c",))
    total = jnp.sum(slots[...].astype(F32), axis=0)
    slots_out[...] = jnp.broadcast_to(resplit(total[None]).astype(BF16), slots_out.shape)
    away = passed[...].astype(F32)
    mate = other[...].astype(F32)
    low = jnp.where(core == 0, away, mate[half : 2 * half, :])
    high = jnp.where(core == 0, mate[0:half, :], away)
    for sample in range(samples):
        here = slice(sample * rows, (sample + 1) * rows)
        wide_out[sample, :, 0, :] = low[here, :]
        wide_out[sample, :, 1 : 1 + cols, :] = mixed[sample].astype(F32)
        wide_out[sample, :, 1 + cols, :] = high[here, :]
        top_out[sample] = wide_out[sample, 0].astype(BF16)
        bottom_out[sample] = wide_out[sample, rows - 1].astype(BF16)


def lat_body(slots, slots_out):
    total = jnp.sum(slots[...].astype(F32), axis=0)
    slots_out[...] = jnp.broadcast_to(resplit(total[None]).astype(BF16), slots_out.shape)


def last_body(
    scale, cells, gathered, stats, mixed, cotangent, grad_pre, gamma, style, column, demod,
    power, weight, emb_full, feats_out, weight_out, style_out, gamma_out, beta_out,
):
    samples, tile_rows, tile_cols, channels = cotangent.shape
    size = tile_rows * tile_cols
    lane = lanes_of()
    sub = lax.broadcasted_iota(jnp.int32, (TILE, channels), 0)
    main, tails, small = [], [], []
    for shard in range(SHARDS):
        slot = gathered[shard].astype(F32)
        main.append(slot[0:32, :])
        tails.append(slot[32:40, :])
    for row in range(TILE):
        whole = jnp.zeros((1, channels), F32)
        for quarter in range(4):
            piece = tails[4 * row + quarter][4:5, :]
            piece = piece + pltpu.roll(piece, 64, 1)
            if quarter:
                piece = pltpu.roll(piece, 32 * quarter, 1)
            whole = jnp.where((lane >> 5) == quarter, piece, whole)
        small.append(whole)
    demod_sums, style_sums, gamma_sums, beta_sums = small[0:2], small[2:4], small[4:6], small[6:8]
    gain = gamma[...]
    gamma_out[...] = scale * (gamma_sums[0] + gamma_sums[1])
    beta_out[...] = scale * (beta_sums[0] + beta_sums[1])
    shrink = jnp.zeros((channels, channels), F32)
    rows = []
    for sample in range(samples):
        demod_row = demod[sample : sample + 1, :]
        pulled = demod_sums[sample] * (demod_row * demod_row * demod_row)
        style_full = column[sample]
        shrink = shrink + style_full * style_full * pulled
        spent = jnp.sum((power[...] * pulled).T, axis=0, keepdims=True)
        rows.append(style_sums[sample] - style[sample : sample + 1, :] * spent)
    for tap in range(8):
        for part in range(4):
            here = slice(32 * part, 32 * part + 32)
            weight_out[tap, here, :] = scale * (
                main[4 * tap + part] - shrink[here, :] * weight[tap, here, :]
            )
    for pair in range(16):
        here = slice(8 * pair, 8 * pair + 8)
        block = jnp.where(sub < 4, tails[2 * pair], pltpu.roll(tails[2 * pair + 1], 4, 0))
        weight_out[8, here, :] = scale * (block - shrink[here, :] * weight[8, here, :])
    style_out[...] = scale * (emb_full[0] * rows[0] + emb_full[1] * rows[1])
    for sample in range(samples):
        inverse = stats[samples + sample : samples + sample + 1, :]
        product_mean = group_total(gain * beta_sums[sample]) * (1.0 / cells)
        squared_mean = group_total(gain * gamma_sums[sample]) * (1.0 / cells)
        flat = mixed[sample].astype(F32).reshape(size, channels)
        norm = (flat - stats[sample : sample + 1, :]) * inverse
        change = inverse * (gain * grad_pre[sample] - product_mean - norm * squared_mean)
        out = cotangent[sample].reshape(size, channels).astype(F32) + change
        feats_out[sample] = out.astype(BF16).reshape(tile_rows, tile_cols, channels)


def on_device(
    feats, cond, null_field, drop_flags, emb, style_weight, conv_weight, gamma, beta, cotangent
):
    samples, tile_rows, tile_cols, channels = feats.shape
    group_size = channels // GROUPS
    lat_count, lon_count = lax.axis_size(LAT), lax.axis_size(LON)
    devices_all = lat_count * lon_count
    cells_local = tile_rows * tile_cols * group_size
    cells_per_group = cells_local * devices_all
    scale_gradient = 1.0 / math.sqrt(samples * tile_rows * tile_cols * devices_all)
    taps = conv_weight.reshape(9, channels, channels)

    lat_slot = -(-(8 + samples * (tile_cols + 2)) // 16) * 16
    half = samples * tile_rows
    lon_slot = 8 + half
    mixed, slots, edges, passed = call(
        mix_body,
        (
            array(feats.shape, BF16),
            array((lon_count, lon_slot, LANES), BF16),
            array((SLOT, LANES), BF16),
            array((half, LANES), BF16),
        ),
        (
            pltpu.VMEM(feats.shape, BF16),
            pltpu.VMEM(feats.shape, BF16),
            pltpu.VMEM(null_field.shape, BF16),
            pltpu.VMEM(feats.shape, BF16),
            pltpu.VMEM(drop_flags.shape, jnp.int32),
            pltpu.SemaphoreType.DMA((2 * samples + 3,)),
        ),
        room=60,
        in_specs=[pl.BlockSpec(memory_space=pl.ANY)] * 5,
    )(feats, cond, null_field, cotangent, drop_flags)
    slots = exchange(slots, LON)
    wide_cot, slots = call(
        functools.partial(merge_body, cells_local),
        (
            array((samples, tile_rows, tile_cols + 2, channels)),
            array((lat_count, lat_slot, LANES), BF16),
        ),
        (pltpu.VMEM((lat_slot, LANES), F32),),
    )(slots, cotangent)
    slots, passed = lax.optimization_barrier((slots, passed))
    slots = exchange(slots, LAT)
    pairs = [(i, (i + 1) % lon_count) for i in range(1, lon_count, 2)]
    passed = lax.ppermute(passed, LON, pairs + [(target, source) for source, target in pairs])

    taps_shape = (samples, 3, 3 * channels, channels)
    gamma, beta, style, column, demod, power, emb_full, back_taps, fore_taps = call(
        weights_body,
        (
            array((1, channels)),
            array((1, channels)),
            array((samples, channels)),
            array((samples, channels, channels)),
            array((samples, channels)),
            array((channels, channels)),
            array((samples,) + style_weight.shape),
            array(taps_shape, BF16),
            array(taps_shape, BF16),
        ),
    )(emb, style_weight, gamma[None], beta[None], taps)
    spread = pltpu.VMEM((tile_rows + 2, tile_cols + 2, channels), F32)
    shifted = pltpu.VMEM(((tile_rows + 2) * tile_cols, 3 * channels), BF16)
    flat = (samples, tile_rows * tile_cols, channels)
    near = pl.BlockSpec(memory_space=pltpu.VMEM)
    stats, grad_pre, payload = call(
        functools.partial(sums_body, cells_local * lon_count, cells_per_group),
        (
            array((2 * samples, LANES)),
            array(flat),
            array((SHARDS + 1, SLOT, LANES), BF16),
        ),
        (
            pltpu.VMEM((2, lat_slot, LANES), F32),
            spread,
            pltpu.VMEM((samples, (tile_rows + 2) * tile_cols, 3 * channels), BF16),
            pltpu.VMEM((9 * channels, channels), F32),
            pltpu.VMEM(flat, F32),
            pltpu.SemaphoreType.DMA((samples,)),
        ),
        out_specs=(near, pl.BlockSpec(memory_space=pltpu.HBM), near),
        room=52,
    )(slots, mixed, edges, wide_cot, gamma, beta, back_taps, column, demod, taps)

    near_count = lax.axis_size(NEAR)
    slots, other = call(
        core_body,
        (array((near_count, SLOT, LANES), BF16), array((SLOT, LANES), BF16)),
    )(lax.all_gather(payload, "c"))
    slots, passed = lax.optimization_barrier((slots, passed))
    border = array((samples, tile_cols + 2, channels), BF16)
    slots, wide_mixed, top, bottom = call(
        near_body,
        (
            array((lat_count, SLOT, LANES), BF16),
            array((samples, tile_rows, tile_cols + 2, channels)),
            border,
            border,
        ),
    )(exchange(slots, NEAR), other, passed, mixed)
    low, high = shift(bottom, LAT, 1, False), shift(top, LAT, -1, False)
    slots = call(lat_body, array((near_count, SLOT, LANES), BF16))(exchange(slots, LAT))
    slots, low, high = lax.optimization_barrier((slots, low, high))
    payload = lax.all_gather(exchange(slots, NEAR), "c")
    block_out = call(forward_body, array(feats.shape, BF16), (spread, shifted))(
        wide_mixed, low, high, fore_taps, stats, gamma, beta
    )

    grad_feats, grad_weight, grad_style, grad_gamma, grad_beta = call(
        functools.partial(last_body, scale_gradient, cells_per_group),
        (
            array(feats.shape, BF16),
            array(taps.shape),
            array(style_weight.shape),
            array((1, LANES)),
            array((1, LANES)),
        ),
    )(
        payload.reshape(SHARDS, SLOT, LANES), stats, mixed, cotangent, grad_pre, gamma, style,
        column, demod, power, taps, emb_full,
    )
    return (
        block_out,
        grad_feats,
        grad_weight.reshape(conv_weight.shape),
        grad_style,
        grad_gamma[0],
        grad_beta[0],
    )


def solution(mesh):
    parts = Mesh(mesh.devices.reshape(4, 4, 2, 8, 2), LAT + LON)
    tile = P(None, LAT, LON, None)
    placed = (tile, tile, P(LAT, LON, None), P(), P(), P(), P(), P(), P(), tile)
    return jax.shard_map(
        on_device,
        mesh=parts,
        in_specs=placed,
        out_specs=(tile, tile, P(), P(), P(), P()),
        check_vma=False,
    )
```

```python
import functools
import math

import jax
import jax.numpy as jnp
from jax import lax
from jax.experimental import pallas as pl
from jax.experimental.pallas import tpu as pltpu
from jax.sharding import Mesh, PartitionSpec as P

GROUPS = 32
LAT = ("zh", "x")
LON = ("zl", "y", "c")
NEAR = ("zl", "y")
F32 = jnp.float32
BF16 = jnp.bfloat16
TILE = 8
SHARDS = 32
SLOT = 40
LANES = 128


def swap(block, axes, first, periodic):
    count = lax.axis_size(axes)
    pairs = [(i, (i + 1) % count) for i in range(first, count, 2) if periodic or i + 1 < count]
    return lax.ppermute(block, axes, pairs + [(target, source) for source, target in pairs])


def halos(inner, outer, field, sample):
    near, far = inner[field, sample].astype(F32), outer[field, sample].astype(F32)
    even = lax.rem(place(LAT), 2) == 0
    return jnp.where(even, far, near), jnp.where(even, near, far)


def exchange(block, axes):
    return lax.all_to_all(block, axes, 0, 0)


def call(body, outputs, scratch=(), room=24, **more):
    return pl.pallas_call(
        body,
        out_shape=outputs,
        scratch_shapes=list(scratch),
        **more,
        compiler_params=pltpu.CompilerParams(vmem_limit_bytes=room * 1024 * 1024),
    )


def array(shape, dtype=F32):
    return jax.ShapeDtypeStruct(shape, dtype)


def lanes_of(rows=1):
    return lax.broadcasted_iota(jnp.int32, (rows, LANES), 1)


def group_total(row):
    lane = lanes_of()
    for step in (1, 2):
        after, before = pltpu.roll(row, LANES - step, 1), pltpu.roll(row, step, 1)
        row = row + jnp.where((lane & step) == 0, after, before)
    return row


def weave(first, second):
    return jnp.where((lanes_of() & 1) == 0, first, second)


def unweave(row, sample):
    if sample == 0:
        return weave(row, pltpu.roll(row, 1, 1))
    return weave(pltpu.roll(row, LANES - 1, 1), row)


def place(axes):
    index = 0
    for axis in axes:
        index = index * lax.axis_size(axis) + lax.axis_index(axis)
    return index


def three_terms(value):
    terms = []
    for _ in range(3):
        terms.append(value.astype(BF16).astype(F32))
        value = value - terms[-1]
    return terms


def merged(slots, count):
    rows = slots[:, 0:8, :].astype(F32)
    means = rows[:, 0:1, :] + rows[:, 1:2, :] + rows[:, 2:3, :]
    spreads = rows[:, 3:4, :] + rows[:, 4:5, :] + rows[:, 5:6, :]
    mean = jnp.mean(means, axis=0)
    away = means - mean[None]
    return mean, jnp.sum(spreads + count * away * away, axis=0)


def header(mean, spread):
    return three_terms(mean) + three_terms(spread) + [jnp.zeros((2, LANES), F32)]


def fetcher(arrivals):
    used = iter(range(arrivals.shape[0]))

    def fetch(source, target):
        copy = pltpu.make_async_copy(source, target, arrivals.at[next(used)])
        copy.start()
        return copy

    return fetch


def mix_body(
    feats_in, cond_in, null_in, cot_in, flags_in, mixed_out, slots_out, inner_out, outer_out,
    feats, cond, null, cot, flags, arrivals,
):
    fetch = fetcher(arrivals)
    flags_copy, null_copy = fetch(flags_in, flags), fetch(null_in, null)
    field_copies = [
        (fetch(feats_in.at[sample], feats.at[sample]), fetch(cond_in.at[sample], cond.at[sample]))
        for sample in range(feats.shape[0])
    ]
    cot_copy = fetch(cot_in, cot)
    flags_copy.wait()
    null_copy.wait()
    samples, tile_rows, tile_cols, channels = feats.shape
    cells = tile_rows * tile_cols
    size = cells * (channels // GROUPS)
    even = lax.rem(place(LAT), 2) == 0

    def put_rims(field, sample, top, bottom):
        top, bottom = top.astype(F32), bottom.astype(F32)
        inner_out[field, sample] = jnp.where(even, bottom, top).astype(BF16)
        outer_out[field, sample] = jnp.where(even, top, bottom).astype(BF16)

    null32 = null[...].astype(F32)
    means, spreads = [], []
    for sample in range(samples):
        for copy in field_copies[sample]:
            copy.wait()
        dropped = flags[sample : sample + 1, :].astype(F32).reshape(1, 1, channels)
        mixed = (
            feats[sample].astype(F32) + dropped * null32 + (1.0 - dropped) * cond[sample].astype(F32)
        ).astype(BF16)
        mixed_out[sample] = mixed
        put_rims(0, sample, mixed[0], mixed[tile_rows - 1])
        wide = mixed.astype(F32).reshape(cells, channels)
        mean = group_total(jnp.sum(wide, axis=0, keepdims=True)) * (1.0 / size)
        away = wide - mean
        means.append(mean)
        spreads.append(group_total(jnp.sum(away * away, axis=0, keepdims=True)))
    rows = header(weave(*means), weave(*spreads))
    cot_copy.wait()
    firsts, lasts = [], []
    for sample in range(samples):
        put_rims(1, sample, cot[sample, 0], cot[sample, tile_rows - 1])
        wide = cot[sample].astype(F32)
        firsts.append(wide[:, 0, :])
        lasts.append(wide[:, tile_cols - 1, :])
    slots_out[...] = jnp.broadcast_to(
        jnp.concatenate(rows + firsts, axis=0).astype(BF16)[None], slots_out.shape
    )
    after = lax.rem(place(LON) + 1, slots_out.shape[0])
    slots_out[after] = jnp.concatenate(rows + lasts, axis=0).astype(BF16)


def merge_body(count, slots, cot, wide_out, slots_out):
    samples, tile_rows, tile_cols, channels = cot.shape
    lon_count, lat_count = slots.shape[0], slots_out.shape[0]
    mean, spread = merged(slots, count)
    me = place(LON)
    before = slots[lax.rem(me + lon_count - 1, lon_count)].astype(F32)
    after = slots[lax.rem(me + 1, lon_count)].astype(F32)
    for sample in range(samples):
        here = slice(8 + sample * tile_rows, 8 + (sample + 1) * tile_rows)
        wide_out[sample, :, 0, :] = before[here, :]
        wide_out[sample, :, 1 : 1 + tile_cols, :] = cot[sample].astype(F32)
        wide_out[sample, :, 1 + tile_cols, :] = after[here, :]
    rows = header(mean, spread)

    def slot(row):
        corners = [
            wide_out[sample, row, side : side + 1, :]
            for sample in range(samples)
            for side in (0, 1 + tile_cols)
        ]
        spare = jnp.zeros((slots_out.shape[1] - 8 - len(corners), channels), F32)
        return jnp.concatenate(rows + corners + [spare], axis=0).astype(BF16)

    slots_out[...] = jnp.broadcast_to(slot(0)[None], slots_out.shape)
    row = place(LAT)

    @pl.when(row < lat_count - 1)
    def _():
        slots_out[row + 1] = slot(tile_rows - 1)


def columns_body(mixed, inner, outer, edges_out, send_out):
    samples, _, tile_cols, channels = mixed.shape
    spare = [jnp.zeros((send_out.shape[0] - edges_out.shape[0] // 2, channels), F32)]

    def column(at):
        parts = []
        for sample in range(samples):
            low, high = halos(inner, outer, 0, sample)
            parts.append(low[at : at + 1, :])
            parts.append(mixed[sample].astype(F32)[:, at, :])
            parts.append(high[at : at + 1, :])
        return parts

    first, last = column(0), column(tile_cols - 1)
    edges_out[...] = jnp.concatenate(first + last, axis=0).astype(BF16)
    first, last = jnp.concatenate(first + spare, axis=0), jnp.concatenate(last + spare, axis=0)
    send_out[...] = jnp.where(place(("c",)) == 0, first, last).astype(BF16)


def weights_body(
    emb, style_weight, gamma, beta, weight,
    gamma_out, beta_out, style_out, column_out, demod_out, power_out, emb_out, back_out, taps_out,
):
    gamma_out[...] = gamma[...]
    beta_out[...] = beta[...]
    power = jnp.zeros(weight.shape[1:], F32)
    for tap in range(9):
        power = power + weight[tap] * weight[tap]
    samples, channels = emb.shape[0], weight.shape[2]
    exact = lax.Precision.HIGHEST
    style = 1.0 + jnp.dot(
        emb[...], style_weight[...], precision=exact, preferred_element_type=F32
    )
    squares = jnp.dot(style * style, power, precision=exact, preferred_element_type=F32)
    demod = lax.rsqrt(squares + 1e-08)
    style_out[...] = style
    demod_out[...] = demod
    power_out[...] = power
    for sample in range(samples):
        here = slice(sample, sample + 1)
        column = jnp.broadcast_to(style[here, :], (channels, channels)).T
        column_out[sample] = column
        emb_out[sample] = jnp.broadcast_to(emb[here, :], (channels, emb.shape[1])).T
        for tap in range(9):
            row, col = tap // 3, tap % 3
            block = weight[tap] * column * demod[here, :]
            taps_out[sample, row, col * channels : (col + 1) * channels, :] = block.astype(BF16)
            row, col = 2 - row, 2 - col
            back_out[sample, row, col * channels : (col + 1) * channels, :] = block.T.astype(BF16)


def windows(spread, shifted, rows, cols):
    channels = spread.shape[-1]
    for tap in range(3):
        moved = spread[:, tap : tap + cols, :].reshape((rows + 2) * cols, channels)
        shifted[:, tap * channels : (tap + 1) * channels] = moved.astype(BF16)


def forward_body(
    mixed, inner, outer, other, passed, taps, stats, gamma, beta, block_out, spread, shifted
):
    samples, rows, cols, _ = mixed.shape
    size = rows * cols
    row = lax.broadcasted_iota(jnp.int32, spread.shape, 0) + place(LAT) * rows
    inside = (row > 0) & (row <= rows * lax.axis_size(LAT))
    core = place(("c",))
    mate, away = other[...].astype(F32), passed[...].astype(F32)
    half = samples * (rows + 2)
    left = jnp.where(core == 0, away[:half, :], mate[half : 2 * half, :])
    right = jnp.where(core == 0, mate[:half, :], away[:half, :])
    for sample in range(samples):
        here = slice(sample * (rows + 2), (sample + 1) * (rows + 2))
        spread[:, 0, :] = left[here, :]
        spread[:, 1 + cols, :] = right[here, :]
        low, high = halos(inner, outer, 0, sample)
        spread[0, 1 : 1 + cols, :] = low
        spread[1 : 1 + rows, 1 : 1 + cols, :] = mixed[sample].astype(F32)
        spread[1 + rows, 1 : 1 + cols, :] = high
        mean = stats[sample : sample + 1, :][None]
        inverse = stats[samples + sample : samples + sample + 1, :][None]
        pre = (spread[...] - mean) * inverse * gamma[...][None] + beta[...][None]
        spread[...] = jnp.where(inside, pre / (1.0 + jnp.exp(-pre)), 0.0)
        windows(spread, shifted, rows, cols)
        total = mixed[sample].astype(F32).reshape(size, -1)
        for row_tap in range(3):
            window = shifted[row_tap * cols : row_tap * cols + size, :]
            total = total + jnp.dot(window, taps[sample, row_tap], preferred_element_type=F32)
        block_out[sample] = total.astype(BF16).reshape(rows, cols, -1)


def sums_body(
    count, cells, slots, mixed, edges, wide, inner, outer, gamma, beta, back_taps, column, demod,
    weight, stats_out, grad_out, payload_out, edge, spread, shifted, total,
):
    samples, rows, cols, channels = mixed.shape
    size = rows * cols
    mean_all, spread_all = merged(slots, count)
    inverse_all = lax.rsqrt(spread_all * (1.0 / cells) + 1e-05)
    lat_count, row = slots.shape[0], place(LAT)
    below = slots[lax.max(row - 1, 0)].astype(F32)
    above = slots[lax.min(row + 1, lat_count - 1)].astype(F32)
    edge[0] = jnp.where(row > 0, below, 0.0)
    edge[1] = jnp.where(row < lat_count - 1, above, 0.0)
    sums = [[], [], [], []]
    for sample in range(samples):
        mean, inverse = unweave(mean_all, sample), unweave(inverse_all, sample)
        stats_out[sample : sample + 1, :] = mean
        stats_out[samples + sample : samples + sample + 1, :] = inverse
        flat = mixed[sample].reshape(size, channels).astype(F32)
        norm = (flat - mean) * inverse
        pre = norm * gamma[...] + beta[...]
        sig = 1.0 / (1.0 + jnp.exp(-pre))
        act = (pre * sig).astype(BF16)
        slope = sig * (1.0 + pre * (1.0 - sig))
        spread[1 : 1 + rows] = wide[sample]
        low, high = halos(inner, outer, 1, sample)
        for at, halo, corner in ((0, low, edge[0]), (1 + rows, high, edge[1])):
            spread[at, 1 : 1 + cols, :] = halo
            start = 8 + 2 * sample
            spread[at, 0:1, :] = corner[start : start + 1, :]
            spread[at, 1 + cols : 2 + cols, :] = corner[start + 1 : start + 2, :]
        windows(spread, shifted, rows, cols)
        style_full = column[sample]
        demod_row = demod[sample : sample + 1, :]
        both = style_full * demod_row
        product = jnp.zeros((channels, channels), F32)
        grad_act = jnp.zeros((size, channels), F32)
        for row_tap in range(3):
            window = shifted[row_tap * cols : row_tap * cols + size, :]
            grad_act = grad_act + jnp.dot(
                window, back_taps[sample, row_tap], preferred_element_type=F32
            )
            grad = lax.dot_general(
                act, window, (((0,), (0,)), ((), ())), preferred_element_type=F32
            )
            for col_tap in range(3):
                tap = (2 - row_tap) * 3 + 2 - col_tap
                block = grad[:, col_tap * channels : (col_tap + 1) * channels]
                product = product + block * weight[tap]
                here = slice(tap * channels, (tap + 1) * channels)
                part = block * both
                total[here, :] = part if sample == 0 else total[here, :] + part
        grad_pre = grad_act * slope
        grad_out[sample] = grad_pre
        sums[0].append(jnp.sum(product * style_full, axis=0, keepdims=True))
        sums[1].append(jnp.sum((product * demod_row).T, axis=0, keepdims=True))
        sums[2].append(jnp.sum(grad_pre * norm, axis=0, keepdims=True))
        sums[3].append(jnp.sum(grad_pre, axis=0, keepdims=True))
    payload_out[SHARDS] = edges[...]
    small = jnp.concatenate(sum(sums, []), axis=0)
    lane = lanes_of(TILE)
    sub = lax.broadcasted_iota(jnp.int32, (TILE, channels), 0)
    quarters = []
    for quarter in range(4):
        turned = pltpu.roll(small, LANES - 32 * quarter, 1) if quarter else small
        piece = jnp.where(lane < 64, turned, pltpu.roll(turned, 64, 1))
        piece = jnp.where((lane & 32) == 0, piece, 0.0)
        quarters.append(split_terms(piece, lane))
    for shard in range(SHARDS):
        main = total[32 * shard : 32 * shard + 32, :]
        start = 8 * channels + 8 * (shard // 2)
        last = total[start : start + 8, :]
        if shard % 2:
            last = pltpu.roll(last, 4, 0)
        extra = quarters[shard % 4][shard // 4 : shard // 4 + 1, :]
        tail = jnp.where(sub < 4, last, jnp.where(sub == 4, extra, 0.0))
        payload_out[shard] = jnp.concatenate([main, tail], axis=0).astype(BF16)


def split_terms(values, lane):
    high = values.astype(BF16).astype(F32)
    return jnp.where(lane < 64, high, values - high)


def resplit(slots):
    main, tail = slots[:, 0:32, :], slots[:, 32:SLOT, :]
    flat = tail.reshape(-1, LANES)
    lane = lax.broadcasted_iota(jnp.int32, flat.shape, 1)
    row = lax.broadcasted_iota(jnp.int32, flat.shape, 0) & 7
    terms = split_terms(flat + pltpu.roll(flat, 64, 1), lane)
    tail = jnp.where(row == 4, terms, flat).reshape(tail.shape)
    return jnp.concatenate([main, tail], axis=1)


def core_body(gathered, slots_out, other_out):
    core, near_count = place(("c",)), slots_out.shape[0]
    mine = pl.ds(core * near_count, near_count)
    total = gathered[0, mine].astype(F32) + gathered[1, mine].astype(F32)
    other_out[...] = gathered[1 - core, SHARDS]
    slots_out[...] = resplit(total).astype(BF16)


def sum_body(slots, slots_out):
    total = jnp.sum(slots[...].astype(F32), axis=0)
    slots_out[...] = jnp.broadcast_to(resplit(total[None]).astype(BF16), slots_out.shape)


def last_body(
    scale, cells, gathered, stats, mixed, cotangent, grad_pre, gamma, style, column, demod,
    power, weight, emb_full, feats_out, weight_out, style_out, gamma_out, beta_out,
):
    samples, tile_rows, tile_cols, channels = cotangent.shape
    size = tile_rows * tile_cols
    lane = lanes_of()
    sub = lax.broadcasted_iota(jnp.int32, (TILE, channels), 0)
    main, tails, small = [], [], []
    for shard in range(SHARDS):
        slot = gathered[shard].astype(F32)
        main.append(slot[0:32, :])
        tails.append(slot[32:40, :])
    for row in range(TILE):
        whole = jnp.zeros((1, channels), F32)
        for quarter in range(4):
            piece = tails[4 * row + quarter][4:5, :]
            piece = piece + pltpu.roll(piece, 64, 1)
            if quarter:
                piece = pltpu.roll(piece, 32 * quarter, 1)
            whole = jnp.where((lane >> 5) == quarter, piece, whole)
        small.append(whole)
    demod_sums, style_sums, gamma_sums, beta_sums = small[0:2], small[2:4], small[4:6], small[6:8]
    gain = gamma[...]
    gamma_out[...] = scale * (gamma_sums[0] + gamma_sums[1])
    beta_out[...] = scale * (beta_sums[0] + beta_sums[1])
    shrink = jnp.zeros((channels, channels), F32)
    rows = []
    for sample in range(samples):
        demod_row = demod[sample : sample + 1, :]
        pulled = demod_sums[sample] * (demod_row * demod_row * demod_row)
        style_full = column[sample]
        shrink = shrink + style_full * style_full * pulled
        spent = jnp.sum((power[...] * pulled).T, axis=0, keepdims=True)
        rows.append(style_sums[sample] - style[sample : sample + 1, :] * spent)
    for tap in range(8):
        for part in range(4):
            here = slice(32 * part, 32 * part + 32)
            weight_out[tap, here, :] = scale * (
                main[4 * tap + part] - shrink[here, :] * weight[tap, here, :]
            )
    for pair in range(16):
        here = slice(8 * pair, 8 * pair + 8)
        block = jnp.where(sub < 4, tails[2 * pair], pltpu.roll(tails[2 * pair + 1], 4, 0))
        weight_out[8, here, :] = scale * (block - shrink[here, :] * weight[8, here, :])
    style_out[...] = scale * (emb_full[0] * rows[0] + emb_full[1] * rows[1])
    for sample in range(samples):
        inverse = stats[samples + sample : samples + sample + 1, :]
        product_mean = group_total(gain * beta_sums[sample]) * (1.0 / cells)
        squared_mean = group_total(gain * gamma_sums[sample]) * (1.0 / cells)
        flat = mixed[sample].astype(F32).reshape(size, channels)
        norm = (flat - stats[sample : sample + 1, :]) * inverse
        change = inverse * (gain * grad_pre[sample] - product_mean - norm * squared_mean)
        out = cotangent[sample].reshape(size, channels).astype(F32) + change
        feats_out[sample] = out.astype(BF16).reshape(tile_rows, tile_cols, channels)


def on_device(
    feats, cond, null_field, drop_flags, emb, style_weight, conv_weight, gamma, beta, cotangent
):
    samples, tile_rows, tile_cols, channels = feats.shape
    group_size = channels // GROUPS
    lat_count, lon_count = lax.axis_size(LAT), lax.axis_size(LON)
    devices_all = lat_count * lon_count
    cells_local = tile_rows * tile_cols * group_size
    cells_per_group = cells_local * devices_all
    scale_gradient = 1.0 / math.sqrt(samples * tile_rows * tile_cols * devices_all)
    taps = conv_weight.reshape(9, channels, channels)

    lon_slot, lat_slot = 8 + samples * tile_rows, 16
    rim = array((2, samples, tile_cols, channels), BF16)
    mixed, slots, inner, outer = call(
        mix_body,
        (array(feats.shape, BF16), array((lon_count, lon_slot, LANES), BF16), rim, rim),
        (
            pltpu.VMEM(feats.shape, BF16),
            pltpu.VMEM(feats.shape, BF16),
            pltpu.VMEM(null_field.shape, BF16),
            pltpu.VMEM(feats.shape, BF16),
            pltpu.VMEM(drop_flags.shape, jnp.int32),
            pltpu.SemaphoreType.DMA((2 * samples + 3,)),
        ),
        room=60,
        in_specs=[pl.BlockSpec(memory_space=pl.ANY)] * 5,
    )(feats, cond, null_field, cotangent, drop_flags)
    slots = exchange(slots, LON)
    inner, outer = swap(inner, LAT, 0, False), swap(outer, LAT, 1, False)
    wide_cot, slots = call(
        functools.partial(merge_body, cells_local),
        (
            array((samples, tile_rows, tile_cols + 2, channels)),
            array((lat_count, lat_slot, LANES), BF16),
        ),
    )(slots, cotangent)
    slots, inner, outer = lax.optimization_barrier((slots, inner, outer))
    slots = exchange(slots, LAT)
    half = samples * (tile_rows + 2)
    edges, passed = call(
        columns_body, (array((SLOT, LANES), BF16), array((-(-half // 8) * 8, LANES), BF16))
    )(mixed, inner, outer)
    passed = swap(passed, LON, 1, True)

    taps_shape = (samples, 3, 3 * channels, channels)
    gamma, beta, style, column, demod, power, emb_full, back_taps, fore_taps = call(
        weights_body,
        (
            array((1, channels)),
            array((1, channels)),
            array((samples, channels)),
            array((samples, channels, channels)),
            array((samples, channels)),
            array((channels, channels)),
            array((samples,) + style_weight.shape),
            array(taps_shape, BF16),
            array(taps_shape, BF16),
        ),
    )(emb, style_weight, gamma[None], beta[None], taps)
    spread = pltpu.VMEM((tile_rows + 2, tile_cols + 2, channels), F32)
    shifted = pltpu.VMEM(((tile_rows + 2) * tile_cols, 3 * channels), BF16)
    flat = (samples, tile_rows * tile_cols, channels)
    stats, grad_pre, payload = call(
        functools.partial(sums_body, cells_local * lon_count, cells_per_group),
        (
            array((2 * samples, LANES)),
            array(flat),
            array((SHARDS + 1, SLOT, LANES), BF16),
        ),
        (
            pltpu.VMEM((2, lat_slot, LANES), F32),
            spread,
            shifted,
            pltpu.VMEM((9 * channels, channels), F32),
        ),
        room=52,
    )(
        slots, mixed, edges, wide_cot, inner, outer, gamma, beta, back_taps, column, demod, taps
    )

    near_count = lax.axis_size(NEAR)
    shard = array((near_count, SLOT, LANES), BF16)
    slots, other = call(core_body, (shard, array((SLOT, LANES), BF16)))(
        lax.all_gather(payload, "c")
    )
    slots, passed = lax.optimization_barrier((slots, passed))
    summed = array((lat_count, SLOT, LANES), BF16)
    slots = call(sum_body, summed)(exchange(slots, NEAR))
    slots = call(sum_body, shard)(exchange(slots, LAT))
    payload = lax.all_gather(exchange(slots, NEAR), "c")
    block_out = call(forward_body, array(feats.shape, BF16), (spread, shifted))(
        mixed, inner, outer, other, passed, fore_taps, stats, gamma, beta
    )

    grad_feats, grad_weight, grad_style, grad_gamma, grad_beta = call(
        functools.partial(last_body, scale_gradient, cells_per_group),
        (
            array(feats.shape, BF16),
            array(taps.shape),
            array(style_weight.shape),
            array((1, LANES)),
            array((1, LANES)),
        ),
    )(
        payload.reshape(SHARDS, SLOT, LANES), stats, mixed, cotangent, grad_pre, gamma, style,
        column, demod, power, taps, emb_full,
    )
    return (
        block_out,
        grad_feats,
        grad_weight.reshape(conv_weight.shape),
        grad_style,
        grad_gamma[0],
        grad_beta[0],
    )


def solution(mesh):
    parts = Mesh(mesh.devices.reshape(4, 4, 2, 8, 2), LAT + LON)
    tile = P(None, LAT, LON, None)
    placed = (tile, tile, P(LAT, LON, None), P(), P(), P(), P(), P(), P(), tile)
    return jax.shard_map(
        on_device,
        mesh=parts,
        in_specs=placed,
        out_specs=(tile, tile, P(), P(), P(), P()),
        check_vma=False,
    )
```

```python
import functools
import math

import jax
import jax.numpy as jnp
from jax import lax
from jax.experimental import pallas as pl
from jax.experimental.pallas import tpu as pltpu
from jax.sharding import Mesh, PartitionSpec as P

GROUPS = 32
LAT = ("zh", "x")
LON = ("zl", "y", "c")
NEAR = ("zl", "y")
F32 = jnp.float32
BF16 = jnp.bfloat16
TILE = 8
SHARDS = 32
SLOT = 40
LANES = 128


def swap(block, axes, first, periodic):
    count = lax.axis_size(axes)
    pairs = [(i, (i + 1) % count) for i in range(first, count, 2) if periodic or i + 1 < count]
    return lax.ppermute(block, axes, pairs + [(target, source) for source, target in pairs])


def halos(inner, outer, field, sample):
    near, far = inner[field, sample].astype(F32), outer[field, sample].astype(F32)
    even = lax.rem(place(LAT), 2) == 0
    return jnp.where(even, far, near), jnp.where(even, near, far)


def exchange(block, axes):
    return lax.all_to_all(block, axes, 0, 0)


def call(body, outputs, scratch=(), room=24, **more):
    return pl.pallas_call(
        body,
        out_shape=outputs,
        scratch_shapes=list(scratch),
        **more,
        compiler_params=pltpu.CompilerParams(vmem_limit_bytes=room * 1024 * 1024),
    )


def array(shape, dtype=F32):
    return jax.ShapeDtypeStruct(shape, dtype)


def lanes_of(rows=1):
    return lax.broadcasted_iota(jnp.int32, (rows, LANES), 1)


def group_total(row):
    lane = lanes_of()
    for step in (1, 2):
        after, before = pltpu.roll(row, LANES - step, 1), pltpu.roll(row, step, 1)
        row = row + jnp.where((lane & step) == 0, after, before)
    return row


def weave(first, second):
    return jnp.where((lanes_of() & 1) == 0, first, second)


def unweave(row, sample):
    if sample == 0:
        return weave(row, pltpu.roll(row, 1, 1))
    return weave(pltpu.roll(row, LANES - 1, 1), row)


def place(axes):
    index = 0
    for axis in axes:
        index = index * lax.axis_size(axis) + lax.axis_index(axis)
    return index


def three_terms(value):
    terms = []
    for _ in range(3):
        terms.append(value.astype(BF16).astype(F32))
        value = value - terms[-1]
    return terms


def merged(slots, count):
    rows = slots[:, 0:8, :].astype(F32)
    means = rows[:, 0:1, :] + rows[:, 1:2, :] + rows[:, 2:3, :]
    spreads = rows[:, 3:4, :] + rows[:, 4:5, :] + rows[:, 5:6, :]
    mean = jnp.mean(means, axis=0)
    away = means - mean[None]
    return mean, jnp.sum(spreads + count * away * away, axis=0)


def header(mean, spread):
    return three_terms(mean) + three_terms(spread) + [jnp.zeros((2, LANES), F32)]


def fetcher(arrivals):
    used = iter(range(arrivals.shape[0]))

    def fetch(source, target):
        copy = pltpu.make_async_copy(source, target, arrivals.at[next(used)])
        copy.start()
        return copy

    return fetch


def mix_body(
    feats_in, cond_in, null_in, cot_in, flags_in, mixed_out, slots_out, inner_out, outer_out,
    feats, cond, null, cot, flags, arrivals,
):
    fetch = fetcher(arrivals)
    flags_copy, null_copy = fetch(flags_in, flags), fetch(null_in, null)
    field_copies = [
        (fetch(feats_in.at[sample], feats.at[sample]), fetch(cond_in.at[sample], cond.at[sample]))
        for sample in range(feats.shape[0])
    ]
    cot_copy = fetch(cot_in, cot)
    flags_copy.wait()
    null_copy.wait()
    samples, tile_rows, tile_cols, channels = feats.shape
    cells = tile_rows * tile_cols
    size = cells * (channels // GROUPS)
    even = lax.rem(place(LAT), 2) == 0

    def put_rims(field, sample, top, bottom):
        top, bottom = top.astype(F32), bottom.astype(F32)
        inner_out[field, sample] = jnp.where(even, bottom, top).astype(BF16)
        outer_out[field, sample] = jnp.where(even, top, bottom).astype(BF16)

    null32 = null[...].astype(F32)
    means, spreads = [], []
    for sample in range(samples):
        for copy in field_copies[sample]:
            copy.wait()
        dropped = flags[sample : sample + 1, :].astype(F32).reshape(1, 1, channels)
        mixed = (
            feats[sample].astype(F32) + dropped * null32 + (1.0 - dropped) * cond[sample].astype(F32)
        ).astype(BF16)
        mixed_out[sample] = mixed
        put_rims(0, sample, mixed[0], mixed[tile_rows - 1])
        wide = mixed.astype(F32).reshape(cells, channels)
        mean = group_total(jnp.sum(wide, axis=0, keepdims=True)) * (1.0 / size)
        away = wide - mean
        means.append(mean)
        spreads.append(group_total(jnp.sum(away * away, axis=0, keepdims=True)))
    rows = header(weave(*means), weave(*spreads))
    cot_copy.wait()
    firsts, lasts = [], []
    for sample in range(samples):
        put_rims(1, sample, cot[sample, 0], cot[sample, tile_rows - 1])
        wide = cot[sample].astype(F32)
        firsts.append(wide[:, 0, :])
        lasts.append(wide[:, tile_cols - 1, :])
    slots_out[...] = jnp.broadcast_to(
        jnp.concatenate(rows + firsts, axis=0).astype(BF16)[None], slots_out.shape
    )
    after = lax.rem(place(LON) + 1, slots_out.shape[0])
    slots_out[after] = jnp.concatenate(rows + lasts, axis=0).astype(BF16)


def merge_body(count, slots, cot, wide_out, slots_out):
    samples, tile_rows, tile_cols, channels = cot.shape
    lon_count, lat_count = slots.shape[0], slots_out.shape[0]
    mean, spread = merged(slots, count)
    me = place(LON)
    before = slots[lax.rem(me + lon_count - 1, lon_count)].astype(F32)
    after = slots[lax.rem(me + 1, lon_count)].astype(F32)
    for sample in range(samples):
        here = slice(8 + sample * tile_rows, 8 + (sample + 1) * tile_rows)
        wide_out[sample, :, 0, :] = before[here, :]
        wide_out[sample, :, 1 : 1 + tile_cols, :] = cot[sample].astype(F32)
        wide_out[sample, :, 1 + tile_cols, :] = after[here, :]
    rows = header(mean, spread)

    def slot(row):
        corners = [
            wide_out[sample, row, side : side + 1, :]
            for sample in range(samples)
            for side in (0, 1 + tile_cols)
        ]
        spare = jnp.zeros((slots_out.shape[1] - 8 - len(corners), channels), F32)
        return jnp.concatenate(rows + corners + [spare], axis=0).astype(BF16)

    slots_out[...] = jnp.broadcast_to(slot(0)[None], slots_out.shape)
    row = place(LAT)

    @pl.when(row < lat_count - 1)
    def _():
        slots_out[row + 1] = slot(tile_rows - 1)


def columns_body(mixed, inner, outer, edges_out, send_out):
    samples, _, tile_cols, channels = mixed.shape
    spare = [jnp.zeros((send_out.shape[0] - edges_out.shape[0] // 2, channels), F32)]

    def column(at):
        parts = []
        for sample in range(samples):
            low, high = halos(inner, outer, 0, sample)
            parts.append(low[at : at + 1, :])
            parts.append(mixed[sample].astype(F32)[:, at, :])
            parts.append(high[at : at + 1, :])
        return parts

    first, last = column(0), column(tile_cols - 1)
    edges_out[...] = jnp.concatenate(first + last, axis=0).astype(BF16)
    first, last = jnp.concatenate(first + spare, axis=0), jnp.concatenate(last + spare, axis=0)
    send_out[...] = jnp.where(place(("c",)) == 0, first, last).astype(BF16)


def weights_body(
    emb, style_weight, gamma, beta, weight,
    gamma_out, beta_out, style_out, column_out, demod_out, power_out, emb_out, back_out, taps_out,
):
    gamma_out[...] = gamma[...]
    beta_out[...] = beta[...]
    power = jnp.zeros(weight.shape[1:], F32)
    for tap in range(9):
        power = power + weight[tap] * weight[tap]
    samples, channels = emb.shape[0], weight.shape[2]
    exact = lax.Precision.HIGHEST
    style = 1.0 + jnp.dot(
        emb[...], style_weight[...], precision=exact, preferred_element_type=F32
    )
    squares = jnp.dot(style * style, power, precision=exact, preferred_element_type=F32)
    demod = lax.rsqrt(squares + 1e-08)
    style_out[...] = style
    demod_out[...] = demod
    power_out[...] = power
    for sample in range(samples):
        here = slice(sample, sample + 1)
        column = jnp.broadcast_to(style[here, :], (channels, channels)).T
        column_out[sample] = column
        emb_out[sample] = jnp.broadcast_to(emb[here, :], (channels, emb.shape[1])).T
        for tap in range(9):
            row, col = tap // 3, tap % 3
            block = weight[tap] * column * demod[here, :]
            taps_out[sample, row, col * channels : (col + 1) * channels, :] = block.astype(BF16)
            row, col = 2 - row, 2 - col
            back_out[sample, row, col * channels : (col + 1) * channels, :] = block.T.astype(BF16)


def windows(spread, shifted, rows, cols):
    channels = spread.shape[-1]
    for tap in range(3):
        moved = spread[:, tap : tap + cols, :].reshape((rows + 2) * cols, channels)
        shifted[:, tap * channels : (tap + 1) * channels] = moved.astype(BF16)


def forward_body(
    mixed, inner, outer, other, passed, taps, stats, gamma, beta, block_out, spread, shifted
):
    samples, rows, cols, _ = mixed.shape
    size = rows * cols
    row = lax.broadcasted_iota(jnp.int32, spread.shape, 0) + place(LAT) * rows
    inside = (row > 0) & (row <= rows * lax.axis_size(LAT))
    core = place(("c",))
    mate, away = other[...].astype(F32), passed[...].astype(F32)
    half = samples * (rows + 2)
    left = jnp.where(core == 0, away[:half, :], mate[half : 2 * half, :])
    right = jnp.where(core == 0, mate[:half, :], away[:half, :])
    for sample in range(samples):
        here = slice(sample * (rows + 2), (sample + 1) * (rows + 2))
        spread[:, 0, :] = left[here, :]
        spread[:, 1 + cols, :] = right[here, :]
        low, high = halos(inner, outer, 0, sample)
        spread[0, 1 : 1 + cols, :] = low
        spread[1 : 1 + rows, 1 : 1 + cols, :] = mixed[sample].astype(F32)
        spread[1 + rows, 1 : 1 + cols, :] = high
        mean = stats[sample : sample + 1, :][None]
        inverse = stats[samples + sample : samples + sample + 1, :][None]
        pre = (spread[...] - mean) * inverse * gamma[...][None] + beta[...][None]
        spread[...] = jnp.where(inside, pre / (1.0 + jnp.exp(-pre)), 0.0)
        windows(spread, shifted, rows, cols)
        total = mixed[sample].astype(F32).reshape(size, -1)
        for row_tap in range(3):
            window = shifted[row_tap * cols : row_tap * cols + size, :]
            total = total + jnp.dot(window, taps[sample, row_tap], preferred_element_type=F32)
        block_out[sample] = total.astype(BF16).reshape(rows, cols, -1)


def sums_body(
    count, cells, slots, mixed, edges, wide, inner, outer, gamma, beta, back_taps, column, demod,
    weight, stats_out, grad_out, payload_out, edge, spread, shifted, total,
):
    samples, rows, cols, channels = mixed.shape
    size = rows * cols
    mean_all, spread_all = merged(slots, count)
    inverse_all = lax.rsqrt(spread_all * (1.0 / cells) + 1e-05)
    lat_count, row = slots.shape[0], place(LAT)
    below = slots[lax.max(row - 1, 0)].astype(F32)
    above = slots[lax.min(row + 1, lat_count - 1)].astype(F32)
    edge[0] = jnp.where(row > 0, below, 0.0)
    edge[1] = jnp.where(row < lat_count - 1, above, 0.0)
    sums = [[], [], [], []]
    for sample in range(samples):
        mean, inverse = unweave(mean_all, sample), unweave(inverse_all, sample)
        stats_out[sample : sample + 1, :] = mean
        stats_out[samples + sample : samples + sample + 1, :] = inverse
        flat = mixed[sample].reshape(size, channels).astype(F32)
        norm = (flat - mean) * inverse
        pre = norm * gamma[...] + beta[...]
        sig = 1.0 / (1.0 + jnp.exp(-pre))
        act = (pre * sig).astype(BF16)
        slope = sig * (1.0 + pre * (1.0 - sig))
        spread[1 : 1 + rows] = wide[sample]
        low, high = halos(inner, outer, 1, sample)
        for at, halo, corner in ((0, low, edge[0]), (1 + rows, high, edge[1])):
            spread[at, 1 : 1 + cols, :] = halo
            start = 8 + 2 * sample
            spread[at, 0:1, :] = corner[start : start + 1, :]
            spread[at, 1 + cols : 2 + cols, :] = corner[start + 1 : start + 2, :]
        windows(spread, shifted, rows, cols)
        style_full = column[sample]
        demod_row = demod[sample : sample + 1, :]
        both = style_full * demod_row
        product = jnp.zeros((channels, channels), F32)
        grad_act = jnp.zeros((size, channels), F32)
        for row_tap in range(3):
            window = shifted[row_tap * cols : row_tap * cols + size, :]
            grad_act = grad_act + jnp.dot(
                window, back_taps[sample, row_tap], preferred_element_type=F32
            )
            grad = lax.dot_general(
                act, window, (((0,), (0,)), ((), ())), preferred_element_type=F32
            )
            for col_tap in range(3):
                tap = (2 - row_tap) * 3 + 2 - col_tap
                block = grad[:, col_tap * channels : (col_tap + 1) * channels]
                product = product + block * weight[tap]
                here = slice(tap * channels, (tap + 1) * channels)
                part = block * both
                total[here, :] = part if sample == 0 else total[here, :] + part
        grad_pre = grad_act * slope
        grad_out[sample] = grad_pre
        sums[0].append(jnp.sum(product * style_full, axis=0, keepdims=True))
        sums[1].append(jnp.sum((product * demod_row).T, axis=0, keepdims=True))
        sums[2].append(jnp.sum(grad_pre * norm, axis=0, keepdims=True))
        sums[3].append(jnp.sum(grad_pre, axis=0, keepdims=True))
    payload_out[SHARDS] = edges[...]
    small = jnp.concatenate(sum(sums, []), axis=0)
    lane = lanes_of(TILE)
    sub = lax.broadcasted_iota(jnp.int32, (TILE, channels), 0)
    quarters = []
    for quarter in range(4):
        turned = pltpu.roll(small, LANES - 32 * quarter, 1) if quarter else small
        piece = jnp.where(lane < 64, turned, pltpu.roll(turned, 64, 1))
        piece = jnp.where((lane & 32) == 0, piece, 0.0)
        quarters.append(split_terms(piece, lane))
    for shard in range(SHARDS):
        main = total[32 * shard : 32 * shard + 32, :]
        start = 8 * channels + 8 * (shard // 2)
        last = total[start : start + 8, :]
        if shard % 2:
            last = pltpu.roll(last, 4, 0)
        extra = quarters[shard % 4][shard // 4 : shard // 4 + 1, :]
        tail = jnp.where(sub < 4, last, jnp.where(sub == 4, extra, 0.0))
        payload_out[shard] = jnp.concatenate([main, tail], axis=0).astype(BF16)


def split_terms(values, lane):
    high = values.astype(BF16).astype(F32)
    return jnp.where(lane < 64, high, values - high)


def resplit(slots):
    main, tail = slots[:, 0:32, :], slots[:, 32:SLOT, :]
    flat = tail.reshape(-1, LANES)
    lane = lax.broadcasted_iota(jnp.int32, flat.shape, 1)
    row = lax.broadcasted_iota(jnp.int32, flat.shape, 0) & 7
    terms = split_terms(flat + pltpu.roll(flat, 64, 1), lane)
    tail = jnp.where(row == 4, terms, flat).reshape(tail.shape)
    return jnp.concatenate([main, tail], axis=1)


def core_body(gathered, slots_out, other_out):
    core, near_count = place(("c",)), slots_out.shape[0]
    mine = pl.ds(core * near_count, near_count)
    total = gathered[0, mine].astype(F32) + gathered[1, mine].astype(F32)
    other_out[...] = gathered[1 - core, SHARDS]
    slots_out[...] = resplit(total).astype(BF16)


def sum_body(slots, slots_out):
    total = jnp.sum(slots[...].astype(F32), axis=0)
    slots_out[...] = jnp.broadcast_to(resplit(total[None]).astype(BF16), slots_out.shape)


def last_body(
    scale, cells, gathered, stats, mixed, cotangent, grad_pre, gamma, style, column, demod,
    power, weight, emb_full, feats_out, weight_out, style_out, gamma_out, beta_out,
):
    samples, tile_rows, tile_cols, channels = cotangent.shape
    size = tile_rows * tile_cols
    lane = lanes_of()
    sub = lax.broadcasted_iota(jnp.int32, (TILE, channels), 0)
    main, tails, small = [], [], []
    for shard in range(SHARDS):
        slot = gathered[shard].astype(F32)
        main.append(slot[0:32, :])
        tails.append(slot[32:40, :])
    for row in range(TILE):
        whole = jnp.zeros((1, channels), F32)
        for quarter in range(4):
            piece = tails[4 * row + quarter][4:5, :]
            piece = piece + pltpu.roll(piece, 64, 1)
            if quarter:
                piece = pltpu.roll(piece, 32 * quarter, 1)
            whole = jnp.where((lane >> 5) == quarter, piece, whole)
        small.append(whole)
    demod_sums, style_sums, gamma_sums, beta_sums = small[0:2], small[2:4], small[4:6], small[6:8]
    gain = gamma[...]
    gamma_out[...] = scale * (gamma_sums[0] + gamma_sums[1])
    beta_out[...] = scale * (beta_sums[0] + beta_sums[1])
    shrink = jnp.zeros((channels, channels), F32)
    rows = []
    for sample in range(samples):
        demod_row = demod[sample : sample + 1, :]
        pulled = demod_sums[sample] * (demod_row * demod_row * demod_row)
        style_full = column[sample]
        shrink = shrink + style_full * style_full * pulled
        spent = jnp.sum((power[...] * pulled).T, axis=0, keepdims=True)
        rows.append(style_sums[sample] - style[sample : sample + 1, :] * spent)
    for tap in range(8):
        for part in range(4):
            here = slice(32 * part, 32 * part + 32)
            weight_out[tap, here, :] = scale * (
                main[4 * tap + part] - shrink[here, :] * weight[tap, here, :]
            )
    for pair in range(16):
        here = slice(8 * pair, 8 * pair + 8)
        block = jnp.where(sub < 4, tails[2 * pair], pltpu.roll(tails[2 * pair + 1], 4, 0))
        weight_out[8, here, :] = scale * (block - shrink[here, :] * weight[8, here, :])
    style_out[...] = scale * (emb_full[0] * rows[0] + emb_full[1] * rows[1])
    for sample in range(samples):
        inverse = stats[samples + sample : samples + sample + 1, :]
        product_mean = group_total(gain * beta_sums[sample]) * (1.0 / cells)
        squared_mean = group_total(gain * gamma_sums[sample]) * (1.0 / cells)
        flat = mixed[sample].astype(F32).reshape(size, channels)
        norm = (flat - stats[sample : sample + 1, :]) * inverse
        change = inverse * (gain * grad_pre[sample] - product_mean - norm * squared_mean)
        out = cotangent[sample].reshape(size, channels).astype(F32) + change
        feats_out[sample] = out.astype(BF16).reshape(tile_rows, tile_cols, channels)


def on_device(
    feats, cond, null_field, drop_flags, emb, style_weight, conv_weight, gamma, beta, cotangent
):
    samples, tile_rows, tile_cols, channels = feats.shape
    group_size = channels // GROUPS
    lat_count, lon_count = lax.axis_size(LAT), lax.axis_size(LON)
    devices_all = lat_count * lon_count
    cells_local = tile_rows * tile_cols * group_size
    cells_per_group = cells_local * devices_all
    scale_gradient = 1.0 / math.sqrt(samples * tile_rows * tile_cols * devices_all)
    taps = conv_weight.reshape(9, channels, channels)

    lon_slot, lat_slot = 8 + samples * tile_rows, 16
    rim = array((2, samples, tile_cols, channels), BF16)
    mixed, slots, inner, outer = call(
        mix_body,
        (array(feats.shape, BF16), array((lon_count, lon_slot, LANES), BF16), rim, rim),
        (
            pltpu.VMEM(feats.shape, BF16),
            pltpu.VMEM(feats.shape, BF16),
            pltpu.VMEM(null_field.shape, BF16),
            pltpu.VMEM(feats.shape, BF16),
            pltpu.VMEM(drop_flags.shape, jnp.int32),
            pltpu.SemaphoreType.DMA((2 * samples + 3,)),
        ),
        room=60,
        in_specs=[pl.BlockSpec(memory_space=pl.ANY)] * 5,
    )(feats, cond, null_field, cotangent, drop_flags)
    slots = exchange(slots, LON)
    inner, outer = swap(inner, LAT, 0, False), swap(outer, LAT, 1, False)
    wide_cot, slots = call(
        functools.partial(merge_body, cells_local),
        (
            array((samples, tile_rows, tile_cols + 2, channels)),
            array((lat_count, lat_slot, LANES), BF16),
        ),
    )(slots, cotangent)
    slots, inner = lax.optimization_barrier((slots, inner))
    slots = exchange(slots, LAT)
    half = samples * (tile_rows + 2)
    edges, passed = call(
        columns_body, (array((SLOT, LANES), BF16), array((-(-half // 8) * 8, LANES), BF16))
    )(mixed, inner, outer)
    passed = swap(passed, LON, 1, True)

    taps_shape = (samples, 3, 3 * channels, channels)
    gamma, beta, style, column, demod, power, emb_full, back_taps, fore_taps = call(
        weights_body,
        (
            array((1, channels)),
            array((1, channels)),
            array((samples, channels)),
            array((samples, channels, channels)),
            array((samples, channels)),
            array((channels, channels)),
            array((samples,) + style_weight.shape),
            array(taps_shape, BF16),
            array(taps_shape, BF16),
        ),
    )(emb, style_weight, gamma[None], beta[None], taps)
    spread = pltpu.VMEM((tile_rows + 2, tile_cols + 2, channels), F32)
    shifted = pltpu.VMEM(((tile_rows + 2) * tile_cols, 3 * channels), BF16)
    flat = (samples, tile_rows * tile_cols, channels)
    stats, grad_pre, payload = call(
        functools.partial(sums_body, cells_local * lon_count, cells_per_group),
        (
            array((2 * samples, LANES)),
            array(flat),
            array((SHARDS + 1, SLOT, LANES), BF16),
        ),
        (
            pltpu.VMEM((2, lat_slot, LANES), F32),
            spread,
            shifted,
            pltpu.VMEM((9 * channels, channels), F32),
        ),
    )(
        slots, mixed, edges, wide_cot, inner, outer, gamma, beta, back_taps, column, demod, taps
    )

    near_count = lax.axis_size(NEAR)
    shard = array((near_count, SLOT, LANES), BF16)
    slots, other = call(core_body, (shard, array((SLOT, LANES), BF16)))(
        lax.all_gather(payload, "c")
    )
    slots, passed = lax.optimization_barrier((slots, passed))
    summed = array((lat_count, SLOT, LANES), BF16)
    slots = call(sum_body, summed)(exchange(slots, NEAR))
    slots = call(sum_body, shard)(exchange(slots, LAT))
    payload = lax.all_gather(exchange(slots, NEAR), "c")
    block_out = call(forward_body, array(feats.shape, BF16), (spread, shifted))(
        mixed, inner, outer, other, passed, fore_taps, stats, gamma, beta
    )

    grad_feats, grad_weight, grad_style, grad_gamma, grad_beta = call(
        functools.partial(last_body, scale_gradient, cells_per_group),
        (
            array(feats.shape, BF16),
            array(taps.shape),
            array(style_weight.shape),
            array((1, LANES)),
            array((1, LANES)),
        ),
    )(
        payload.reshape(SHARDS, SLOT, LANES), stats, mixed, cotangent, grad_pre, gamma, style,
        column, demod, power, taps, emb_full,
    )
    return (
        block_out,
        grad_feats,
        grad_weight.reshape(conv_weight.shape),
        grad_style,
        grad_gamma[0],
        grad_beta[0],
    )


def solution(mesh):
    parts = Mesh(mesh.devices.reshape(4, 4, 2, 8, 2), LAT + LON)
    tile = P(None, LAT, LON, None)
    placed = (tile, tile, P(LAT, LON, None), P(), P(), P(), P(), P(), P(), tile)
    return jax.shard_map(
        on_device,
        mesh=parts,
        in_specs=placed,
        out_specs=(tile, tile, P(), P(), P(), P()),
        check_vma=False,
    )
```

```python
import functools
import math

import jax
import jax.numpy as jnp
from jax import lax
from jax.experimental import pallas as pl
from jax.experimental.pallas import tpu as pltpu
from jax.sharding import Mesh, PartitionSpec as P

GROUPS = 32
LAT = ("zh", "x")
LON = ("zl", "y", "c")
NEAR = ("zl", "y")
F32 = jnp.float32
BF16 = jnp.bfloat16
TILE = 8
SHARDS = 32
SLOT = 40
LANES = 128


def swap(block, axes, first, periodic):
    count = lax.axis_size(axes)
    pairs = [(i, (i + 1) % count) for i in range(first, count, 2) if periodic or i + 1 < count]
    return lax.ppermute(block, axes, pairs + [(target, source) for source, target in pairs])


def halos(inner, outer, field, sample):
    near, far = inner[field, sample].astype(F32), outer[field, sample].astype(F32)
    even = lax.rem(place(LAT), 2) == 0
    return jnp.where(even, far, near), jnp.where(even, near, far)


def exchange(block, axes):
    return lax.all_to_all(block, axes, 0, 0)


def call(body, outputs, scratch=(), room=24, **more):
    return pl.pallas_call(
        body,
        out_shape=outputs,
        scratch_shapes=list(scratch),
        **more,
        compiler_params=pltpu.CompilerParams(vmem_limit_bytes=room * 1024 * 1024),
    )


def array(shape, dtype=F32):
    return jax.ShapeDtypeStruct(shape, dtype)


def lanes_of(rows=1):
    return lax.broadcasted_iota(jnp.int32, (rows, LANES), 1)


def group_total(row):
    lane = lanes_of()
    for step in (1, 2):
        after, before = pltpu.roll(row, LANES - step, 1), pltpu.roll(row, step, 1)
        row = row + jnp.where((lane & step) == 0, after, before)
    return row


def weave(first, second):
    return jnp.where((lanes_of() & 1) == 0, first, second)


def unweave(row, sample):
    if sample == 0:
        return weave(row, pltpu.roll(row, 1, 1))
    return weave(pltpu.roll(row, LANES - 1, 1), row)


def place(axes):
    index = 0
    for axis in axes:
        index = index * lax.axis_size(axis) + lax.axis_index(axis)
    return index


def three_terms(value):
    terms = []
    for _ in range(3):
        terms.append(value.astype(BF16).astype(F32))
        value = value - terms[-1]
    return terms


def merged(slots, count):
    rows = slots[:, 0:8, :].astype(F32)
    means = rows[:, 0:1, :] + rows[:, 1:2, :] + rows[:, 2:3, :]
    spreads = rows[:, 3:4, :] + rows[:, 4:5, :] + rows[:, 5:6, :]
    mean = jnp.mean(means, axis=0)
    away = means - mean[None]
    return mean, jnp.sum(spreads + count * away * away, axis=0)


def header(mean, spread):
    return three_terms(mean) + three_terms(spread) + [jnp.zeros((2, LANES), F32)]


def fetcher(arrivals):
    used = iter(range(arrivals.shape[0]))

    def fetch(source, target):
        copy = pltpu.make_async_copy(source, target, arrivals.at[next(used)])
        copy.start()
        return copy

    return fetch


def mix_body(
    feats_in, cond_in, null_in, cot_in, flags_in, mixed_out, slots_out, inner_out, outer_out,
    feats, cond, null, cot, flags, arrivals,
):
    fetch = fetcher(arrivals)
    flags_copy, null_copy = fetch(flags_in, flags), fetch(null_in, null)
    field_copies = [
        (fetch(feats_in.at[sample], feats.at[sample]), fetch(cond_in.at[sample], cond.at[sample]))
        for sample in range(feats.shape[0])
    ]
    cot_copy = fetch(cot_in, cot)
    flags_copy.wait()
    null_copy.wait()
    samples, tile_rows, tile_cols, channels = feats.shape
    cells = tile_rows * tile_cols
    size = cells * (channels // GROUPS)
    even = lax.rem(place(LAT), 2) == 0

    def put_rims(field, sample, top, bottom):
        top, bottom = top.astype(F32), bottom.astype(F32)
        inner_out[field, sample] = jnp.where(even, bottom, top).astype(BF16)
        outer_out[field, sample] = jnp.where(even, top, bottom).astype(BF16)

    null32 = null[...].astype(F32)
    means, spreads = [], []
    for sample in range(samples):
        for copy in field_copies[sample]:
            copy.wait()
        dropped = flags[sample : sample + 1, :].astype(F32).reshape(1, 1, channels)
        mixed = (
            feats[sample].astype(F32) + dropped * null32 + (1.0 - dropped) * cond[sample].astype(F32)
        ).astype(BF16)
        mixed_out[sample] = mixed
        put_rims(0, sample, mixed[0], mixed[tile_rows - 1])
        wide = mixed.astype(F32).reshape(cells, channels)
        mean = group_total(jnp.sum(wide, axis=0, keepdims=True)) * (1.0 / size)
        away = wide - mean
        means.append(mean)
        spreads.append(group_total(jnp.sum(away * away, axis=0, keepdims=True)))
    rows = header(weave(*means), weave(*spreads))
    cot_copy.wait()
    firsts, lasts = [], []
    for sample in range(samples):
        put_rims(1, sample, cot[sample, 0], cot[sample, tile_rows - 1])
        wide = cot[sample].astype(F32)
        firsts.append(wide[:, 0, :])
        lasts.append(wide[:, tile_cols - 1, :])
    slots_out[...] = jnp.broadcast_to(
        jnp.concatenate(rows + firsts, axis=0).astype(BF16)[None], slots_out.shape
    )
    after = lax.rem(place(LON) + 1, slots_out.shape[0])
    slots_out[after] = jnp.concatenate(rows + lasts, axis=0).astype(BF16)


def merge_body(count, slots, cot, wide_out, slots_out):
    samples, tile_rows, tile_cols, channels = cot.shape
    lon_count, lat_count = slots.shape[0], slots_out.shape[0]
    mean, spread = merged(slots, count)
    me = place(LON)
    before = slots[lax.rem(me + lon_count - 1, lon_count)].astype(F32)
    after = slots[lax.rem(me + 1, lon_count)].astype(F32)
    for sample in range(samples):
        here = slice(8 + sample * tile_rows, 8 + (sample + 1) * tile_rows)
        wide_out[sample, :, 0, :] = before[here, :]
        wide_out[sample, :, 1 : 1 + tile_cols, :] = cot[sample].astype(F32)
        wide_out[sample, :, 1 + tile_cols, :] = after[here, :]
    rows = header(mean, spread)

    def slot(row):
        corners = [
            wide_out[sample, row, side : side + 1, :]
            for sample in range(samples)
            for side in (0, 1 + tile_cols)
        ]
        spare = jnp.zeros((slots_out.shape[1] - 8 - len(corners), channels), F32)
        return jnp.concatenate(rows + corners + [spare], axis=0).astype(BF16)

    slots_out[...] = jnp.broadcast_to(slot(0)[None], slots_out.shape)
    row = place(LAT)

    @pl.when(row < lat_count - 1)
    def _():
        slots_out[row + 1] = slot(tile_rows - 1)


def columns_body(mixed, inner, outer, edges_out, send_out):
    samples, _, tile_cols, channels = mixed.shape
    spare = [jnp.zeros((send_out.shape[0] - edges_out.shape[0] // 2, channels), F32)]

    def column(at):
        parts = []
        for sample in range(samples):
            low, high = halos(inner, outer, 0, sample)
            parts.append(low[at : at + 1, :])
            parts.append(mixed[sample].astype(F32)[:, at, :])
            parts.append(high[at : at + 1, :])
        return parts

    first, last = column(0), column(tile_cols - 1)
    edges_out[...] = jnp.concatenate(first + last, axis=0).astype(BF16)
    first, last = jnp.concatenate(first + spare, axis=0), jnp.concatenate(last + spare, axis=0)
    send_out[...] = jnp.where(place(("c",)) == 0, first, last).astype(BF16)


def weights_body(
    emb, style_weight, gamma, beta, weight,
    gamma_out, beta_out, style_out, column_out, demod_out, power_out, emb_out, back_out, taps_out,
):
    gamma_out[...] = gamma[...]
    beta_out[...] = beta[...]
    power = jnp.zeros(weight.shape[1:], F32)
    for tap in range(9):
        power = power + weight[tap] * weight[tap]
    samples, channels = emb.shape[0], weight.shape[2]
    exact = lax.Precision.HIGHEST
    style = 1.0 + jnp.dot(
        emb[...], style_weight[...], precision=exact, preferred_element_type=F32
    )
    squares = jnp.dot(style * style, power, precision=exact, preferred_element_type=F32)
    demod = lax.rsqrt(squares + 1e-08)
    style_out[...] = style
    demod_out[...] = demod
    power_out[...] = power
    for sample in range(samples):
        here = slice(sample, sample + 1)
        column = jnp.broadcast_to(style[here, :], (channels, channels)).T
        column_out[sample] = column
        emb_out[sample] = jnp.broadcast_to(emb[here, :], (channels, emb.shape[1])).T
        for tap in range(9):
            row, col = tap // 3, tap % 3
            block = weight[tap] * column * demod[here, :]
            taps_out[sample, row, col * channels : (col + 1) * channels, :] = block.astype(BF16)
            row, col = 2 - row, 2 - col
            back_out[sample, row, col * channels : (col + 1) * channels, :] = block.T.astype(BF16)


def windows(spread, shifted, rows, cols):
    channels = spread.shape[-1]
    for tap in range(3):
        moved = spread[:, tap : tap + cols, :].reshape((rows + 2) * cols, channels)
        shifted[:, tap * channels : (tap + 1) * channels] = moved.astype(BF16)


def forward_body(
    mixed, inner, outer, other, passed, taps, stats, gamma, beta, block_out, spread, shifted
):
    samples, rows, cols, _ = mixed.shape
    size = rows * cols
    row = lax.broadcasted_iota(jnp.int32, spread.shape, 0) + place(LAT) * rows
    inside = (row > 0) & (row <= rows * lax.axis_size(LAT))
    core = place(("c",))
    mate, away = other[...].astype(F32), passed[...].astype(F32)
    half = samples * (rows + 2)
    left = jnp.where(core == 0, away[:half, :], mate[half : 2 * half, :])
    right = jnp.where(core == 0, mate[:half, :], away[:half, :])
    for sample in range(samples):
        here = slice(sample * (rows + 2), (sample + 1) * (rows + 2))
        spread[:, 0, :] = left[here, :]
        spread[:, 1 + cols, :] = right[here, :]
        low, high = halos(inner, outer, 0, sample)
        spread[0, 1 : 1 + cols, :] = low
        spread[1 : 1 + rows, 1 : 1 + cols, :] = mixed[sample].astype(F32)
        spread[1 + rows, 1 : 1 + cols, :] = high
        mean = stats[sample : sample + 1, :][None]
        inverse = stats[samples + sample : samples + sample + 1, :][None]
        pre = (spread[...] - mean) * inverse * gamma[...][None] + beta[...][None]
        spread[...] = jnp.where(inside, pre / (1.0 + jnp.exp(-pre)), 0.0)
        windows(spread, shifted, rows, cols)
        total = mixed[sample].astype(F32).reshape(size, -1)
        for row_tap in range(3):
            window = shifted[row_tap * cols : row_tap * cols + size, :]
            total = total + jnp.dot(window, taps[sample, row_tap], preferred_element_type=F32)
        block_out[sample] = total.astype(BF16).reshape(rows, cols, -1)


def sums_body(
    count, cells, slots, mixed, edges, wide, inner, outer, gamma, beta, back_taps, column, demod,
    weight, stats_out, grad_out, payload_out, edge, spread, shifted, total,
):
    samples, rows, cols, channels = mixed.shape
    size = rows * cols
    mean_all, spread_all = merged(slots, count)
    inverse_all = lax.rsqrt(spread_all * (1.0 / cells) + 1e-05)
    lat_count, row = slots.shape[0], place(LAT)
    below = slots[lax.max(row - 1, 0)].astype(F32)
    above = slots[lax.min(row + 1, lat_count - 1)].astype(F32)
    edge[0] = jnp.where(row > 0, below, 0.0)
    edge[1] = jnp.where(row < lat_count - 1, above, 0.0)
    sums = [[], [], [], []]
    for sample in range(samples):
        mean, inverse = unweave(mean_all, sample), unweave(inverse_all, sample)
        stats_out[sample : sample + 1, :] = mean
        stats_out[samples + sample : samples + sample + 1, :] = inverse
        flat = mixed[sample].reshape(size, channels).astype(F32)
        norm = (flat - mean) * inverse
        pre = norm * gamma[...] + beta[...]
        sig = 1.0 / (1.0 + jnp.exp(-pre))
        act = (pre * sig).astype(BF16)
        slope = sig * (1.0 + pre * (1.0 - sig))
        spread[1 : 1 + rows] = wide[sample]
        low, high = halos(inner, outer, 1, sample)
        for at, halo, corner in ((0, low, edge[0]), (1 + rows, high, edge[1])):
            spread[at, 1 : 1 + cols, :] = halo
            start = 8 + 2 * sample
            spread[at, 0:1, :] = corner[start : start + 1, :]
            spread[at, 1 + cols : 2 + cols, :] = corner[start + 1 : start + 2, :]
        windows(spread, shifted, rows, cols)
        style_full = column[sample]
        demod_row = demod[sample : sample + 1, :]
        both = style_full * demod_row
        product = jnp.zeros((channels, channels), F32)
        grad_act = jnp.zeros((size, channels), F32)
        for row_tap in range(3):
            window = shifted[row_tap * cols : row_tap * cols + size, :]
            grad_act = grad_act + jnp.dot(
                window, back_taps[sample, row_tap], preferred_element_type=F32
            )
            grad = lax.dot_general(
                act, window, (((0,), (0,)), ((), ())), preferred_element_type=F32
            )
            for col_tap in range(3):
                tap = (2 - row_tap) * 3 + 2 - col_tap
                block = grad[:, col_tap * channels : (col_tap + 1) * channels]
                product = product + block * weight[tap]
                here = slice(tap * channels, (tap + 1) * channels)
                part = block * both
                total[here, :] = part if sample == 0 else total[here, :] + part
        grad_pre = grad_act * slope
        grad_out[sample] = grad_pre
        sums[0].append(jnp.sum(product * style_full, axis=0, keepdims=True))
        sums[1].append(jnp.sum((product * demod_row).T, axis=0, keepdims=True))
        sums[2].append(jnp.sum(grad_pre * norm, axis=0, keepdims=True))
        sums[3].append(jnp.sum(grad_pre, axis=0, keepdims=True))
    payload_out[SHARDS] = edges[...]
    small = jnp.concatenate(sum(sums, []), axis=0)
    lane = lanes_of(TILE)
    sub = lax.broadcasted_iota(jnp.int32, (TILE, channels), 0)
    quarters = []
    for quarter in range(4):
        turned = pltpu.roll(small, LANES - 32 * quarter, 1) if quarter else small
        piece = jnp.where(lane < 64, turned, pltpu.roll(turned, 64, 1))
        piece = jnp.where((lane & 32) == 0, piece, 0.0)
        quarters.append(split_terms(piece, lane))
    for shard in range(SHARDS):
        main = total[32 * shard : 32 * shard + 32, :]
        start = 8 * channels + 8 * (shard // 2)
        last = total[start : start + 8, :]
        if shard % 2:
            last = pltpu.roll(last, 4, 0)
        extra = quarters[shard % 4][shard // 4 : shard // 4 + 1, :]
        tail = jnp.where(sub < 4, last, jnp.where(sub == 4, extra, 0.0))
        payload_out[shard] = jnp.concatenate([main, tail], axis=0).astype(BF16)


def split_terms(values, lane):
    high = values.astype(BF16).astype(F32)
    return jnp.where(lane < 64, high, values - high)


def resplit(slots):
    main, tail = slots[:, 0:32, :], slots[:, 32:SLOT, :]
    flat = tail.reshape(-1, LANES)
    lane = lax.broadcasted_iota(jnp.int32, flat.shape, 1)
    row = lax.broadcasted_iota(jnp.int32, flat.shape, 0) & 7
    terms = split_terms(flat + pltpu.roll(flat, 64, 1), lane)
    tail = jnp.where(row == 4, terms, flat).reshape(tail.shape)
    return jnp.concatenate([main, tail], axis=1)


def core_body(gathered, slots_out, other_out):
    core, near_count = place(("c",)), slots_out.shape[0]
    mine = pl.ds(core * near_count, near_count)
    total = gathered[0, mine].astype(F32) + gathered[1, mine].astype(F32)
    other_out[...] = gathered[1 - core, SHARDS]
    slots_out[...] = resplit(total).astype(BF16)


def sum_body(slots, slots_out):
    total = jnp.sum(slots[...].astype(F32), axis=0)
    slots_out[...] = jnp.broadcast_to(resplit(total[None]).astype(BF16), slots_out.shape)


def last_body(
    scale, cells, gathered, stats, mixed, cotangent, grad_pre, gamma, style, column, demod,
    power, weight, emb_full, feats_out, weight_out, style_out, gamma_out, beta_out,
):
    samples, tile_rows, tile_cols, channels = cotangent.shape
    size = tile_rows * tile_cols
    lane = lanes_of()
    sub = lax.broadcasted_iota(jnp.int32, (TILE, channels), 0)
    main, tails, small = [], [], []
    for shard in range(SHARDS):
        slot = gathered[shard].astype(F32)
        main.append(slot[0:32, :])
        tails.append(slot[32:40, :])
    for row in range(TILE):
        whole = jnp.zeros((1, channels), F32)
        for quarter in range(4):
            piece = tails[4 * row + quarter][4:5, :]
            piece = piece + pltpu.roll(piece, 64, 1)
            if quarter:
                piece = pltpu.roll(piece, 32 * quarter, 1)
            whole = jnp.where((lane >> 5) == quarter, piece, whole)
        small.append(whole)
    demod_sums, style_sums, gamma_sums, beta_sums = small[0:2], small[2:4], small[4:6], small[6:8]
    gain = gamma[...]
    gamma_out[...] = scale * (gamma_sums[0] + gamma_sums[1])
    beta_out[...] = scale * (beta_sums[0] + beta_sums[1])
    shrink = jnp.zeros((channels, channels), F32)
    rows = []
    for sample in range(samples):
        demod_row = demod[sample : sample + 1, :]
        pulled = demod_sums[sample] * (demod_row * demod_row * demod_row)
        style_full = column[sample]
        shrink = shrink + style_full * style_full * pulled
        spent = jnp.sum((power[...] * pulled).T, axis=0, keepdims=True)
        rows.append(style_sums[sample] - style[sample : sample + 1, :] * spent)
    for tap in range(8):
        for part in range(4):
            here = slice(32 * part, 32 * part + 32)
            weight_out[tap, here, :] = scale * (
                main[4 * tap + part] - shrink[here, :] * weight[tap, here, :]
            )
    for pair in range(16):
        here = slice(8 * pair, 8 * pair + 8)
        block = jnp.where(sub < 4, tails[2 * pair], pltpu.roll(tails[2 * pair + 1], 4, 0))
        weight_out[8, here, :] = scale * (block - shrink[here, :] * weight[8, here, :])
    style_out[...] = scale * (emb_full[0] * rows[0] + emb_full[1] * rows[1])
    for sample in range(samples):
        inverse = stats[samples + sample : samples + sample + 1, :]
        product_mean = group_total(gain * beta_sums[sample]) * (1.0 / cells)
        squared_mean = group_total(gain * gamma_sums[sample]) * (1.0 / cells)
        flat = mixed[sample].astype(F32).reshape(size, channels)
        norm = (flat - stats[sample : sample + 1, :]) * inverse
        change = inverse * (gain * grad_pre[sample] - product_mean - norm * squared_mean)
        out = cotangent[sample].reshape(size, channels).astype(F32) + change
        feats_out[sample] = out.astype(BF16).reshape(tile_rows, tile_cols, channels)


def on_device(
    feats, cond, null_field, drop_flags, emb, style_weight, conv_weight, gamma, beta, cotangent
):
    samples, tile_rows, tile_cols, channels = feats.shape
    group_size = channels // GROUPS
    lat_count, lon_count = lax.axis_size(LAT), lax.axis_size(LON)
    devices_all = lat_count * lon_count
    cells_local = tile_rows * tile_cols * group_size
    cells_per_group = cells_local * devices_all
    scale_gradient = 1.0 / math.sqrt(samples * tile_rows * tile_cols * devices_all)
    taps = conv_weight.reshape(9, channels, channels)

    lon_slot, lat_slot = 8 + samples * tile_rows, 16
    rim = array((2, samples, tile_cols, channels), BF16)
    mixed, slots, inner, outer = call(
        mix_body,
        (array(feats.shape, BF16), array((lon_count, lon_slot, LANES), BF16), rim, rim),
        (
            pltpu.VMEM(feats.shape, BF16),
            pltpu.VMEM(feats.shape, BF16),
            pltpu.VMEM(null_field.shape, BF16),
            pltpu.VMEM(feats.shape, BF16),
            pltpu.VMEM(drop_flags.shape, jnp.int32),
            pltpu.SemaphoreType.DMA((2 * samples + 3,)),
        ),
        room=60,
        in_specs=[pl.BlockSpec(memory_space=pl.ANY)] * 5,
    )(feats, cond, null_field, cotangent, drop_flags)
    slots = exchange(slots, LON)
    outer, inner = swap(outer, LAT, 1, False), swap(inner, LAT, 0, False)
    wide_cot, slots = call(
        functools.partial(merge_body, cells_local),
        (
            array((samples, tile_rows, tile_cols + 2, channels)),
            array((lat_count, lat_slot, LANES), BF16),
        ),
    )(slots, cotangent)
    slots, outer, inner = lax.optimization_barrier((slots, outer, inner))
    slots = exchange(slots, LAT)
    half = samples * (tile_rows + 2)
    edges, passed = call(
        columns_body, (array((SLOT, LANES), BF16), array((-(-half // 8) * 8, LANES), BF16))
    )(mixed, inner, outer)
    passed = swap(passed, LON, 1, True)

    taps_shape = (samples, 3, 3 * channels, channels)
    gamma, beta, style, column, demod, power, emb_full, back_taps, fore_taps = call(
        weights_body,
        (
            array((1, channels)),
            array((1, channels)),
            array((samples, channels)),
            array((samples, channels, channels)),
            array((samples, channels)),
            array((channels, channels)),
            array((samples,) + style_weight.shape),
            array(taps_shape, BF16),
            array(taps_shape, BF16),
        ),
    )(emb, style_weight, gamma[None], beta[None], taps)
    spread = pltpu.VMEM((tile_rows + 2, tile_cols + 2, channels), F32)
    shifted = pltpu.VMEM(((tile_rows + 2) * tile_cols, 3 * channels), BF16)
    flat = (samples, tile_rows * tile_cols, channels)
    stats, grad_pre, payload = call(
        functools.partial(sums_body, cells_local * lon_count, cells_per_group),
        (
            array((2 * samples, LANES)),
            array(flat),
            array((SHARDS + 1, SLOT, LANES), BF16),
        ),
        (
            pltpu.VMEM((2, lat_slot, LANES), F32),
            spread,
            shifted,
            pltpu.VMEM((9 * channels, channels), F32),
        ),
    )(
        slots, mixed, edges, wide_cot, inner, outer, gamma, beta, back_taps, column, demod, taps
    )

    near_count = lax.axis_size(NEAR)
    shard = array((near_count, SLOT, LANES), BF16)
    slots, other = call(core_body, (shard, array((SLOT, LANES), BF16)))(
        lax.all_gather(payload, "c")
    )
    slots, passed = lax.optimization_barrier((slots, passed))
    summed = array((lat_count, SLOT, LANES), BF16)
    slots = call(sum_body, summed)(exchange(slots, NEAR))
    slots = call(sum_body, shard)(exchange(slots, LAT))
    payload = lax.all_gather(exchange(slots, NEAR), "c")
    block_out = call(forward_body, array(feats.shape, BF16), (spread, shifted))(
        mixed, inner, outer, other, passed, fore_taps, stats, gamma, beta
    )

    grad_feats, grad_weight, grad_style, grad_gamma, grad_beta = call(
        functools.partial(last_body, scale_gradient, cells_per_group),
        (
            array(feats.shape, BF16),
            array(taps.shape),
            array(style_weight.shape),
            array((1, LANES)),
            array((1, LANES)),
        ),
    )(
        payload.reshape(SHARDS, SLOT, LANES), stats, mixed, cotangent, grad_pre, gamma, style,
        column, demod, power, taps, emb_full,
    )
    return (
        block_out,
        grad_feats,
        grad_weight.reshape(conv_weight.shape),
        grad_style,
        grad_gamma[0],
        grad_beta[0],
    )


def solution(mesh):
    parts = Mesh(mesh.devices.reshape(4, 4, 2, 8, 2), LAT + LON)
    tile = P(None, LAT, LON, None)
    placed = (tile, tile, P(LAT, LON, None), P(), P(), P(), P(), P(), P(), tile)
    return jax.shard_map(
        on_device,
        mesh=parts,
        in_specs=placed,
        out_specs=(tile, tile, P(), P(), P(), P()),
        check_vma=False,
    )
```

```python
import functools
import math

import jax
import jax.numpy as jnp
from jax import lax
from jax.experimental import pallas as pl
from jax.experimental.pallas import tpu as pltpu
from jax.sharding import Mesh, PartitionSpec as P

GROUPS = 32
LAT = ("zh", "x")
LON = ("zl", "y", "c")
NEAR = ("zl", "y")
F32 = jnp.float32
BF16 = jnp.bfloat16
TILE = 8
SHARDS = 32
SLOT = 40
LANES = 128


def swap(block, axes, first, periodic):
    count = lax.axis_size(axes)
    pairs = [(i, (i + 1) % count) for i in range(first, count, 2) if periodic or i + 1 < count]
    return lax.ppermute(block, axes, pairs + [(target, source) for source, target in pairs])


def halos(inner, outer, field, sample):
    near, far = inner[field, sample].astype(F32), outer[field, sample].astype(F32)
    even = lax.rem(place(LAT), 2) == 0
    return jnp.where(even, far, near), jnp.where(even, near, far)


def exchange(block, axes):
    return lax.all_to_all(block, axes, 0, 0)


def call(body, outputs, scratch=(), room=24, **more):
    return pl.pallas_call(
        body,
        out_shape=outputs,
        scratch_shapes=list(scratch),
        **more,
        compiler_params=pltpu.CompilerParams(vmem_limit_bytes=room * 1024 * 1024),
    )


def array(shape, dtype=F32):
    return jax.ShapeDtypeStruct(shape, dtype)


def lanes_of(rows=1):
    return lax.broadcasted_iota(jnp.int32, (rows, LANES), 1)


def group_total(row):
    lane = lanes_of()
    for step in (1, 2):
        after, before = pltpu.roll(row, LANES - step, 1), pltpu.roll(row, step, 1)
        row = row + jnp.where((lane & step) == 0, after, before)
    return row


def weave(first, second):
    return jnp.where((lanes_of() & 1) == 0, first, second)


def unweave(row, sample):
    if sample == 0:
        return weave(row, pltpu.roll(row, 1, 1))
    return weave(pltpu.roll(row, LANES - 1, 1), row)


def place(axes):
    index = 0
    for axis in axes:
        index = index * lax.axis_size(axis) + lax.axis_index(axis)
    return index


def three_terms(value):
    terms = []
    for _ in range(3):
        terms.append(value.astype(BF16).astype(F32))
        value = value - terms[-1]
    return terms


def merged(slots, count):
    rows = slots[:, 0:8, :].astype(F32)
    means = rows[:, 0:1, :] + rows[:, 1:2, :] + rows[:, 2:3, :]
    spreads = rows[:, 3:4, :] + rows[:, 4:5, :] + rows[:, 5:6, :]
    mean = jnp.mean(means, axis=0)
    away = means - mean[None]
    return mean, jnp.sum(spreads + count * away * away, axis=0)


def header(mean, spread):
    return three_terms(mean) + three_terms(spread) + [jnp.zeros((2, LANES), F32)]


def fetcher(arrivals):
    used = iter(range(arrivals.shape[0]))

    def fetch(source, target):
        copy = pltpu.make_async_copy(source, target, arrivals.at[next(used)])
        copy.start()
        return copy

    return fetch


def mix_body(
    feats_in, cond_in, null_in, cot_in, flags_in, mixed_out, slots_out, inner_out, outer_out,
    feats, cond, null, cot, flags, arrivals,
):
    fetch = fetcher(arrivals)
    flags_copy, null_copy = fetch(flags_in, flags), fetch(null_in, null)
    field_copies = [
        (fetch(feats_in.at[sample], feats.at[sample]), fetch(cond_in.at[sample], cond.at[sample]))
        for sample in range(feats.shape[0])
    ]
    cot_copy = fetch(cot_in, cot)
    flags_copy.wait()
    null_copy.wait()
    samples, tile_rows, tile_cols, channels = feats.shape
    cells = tile_rows * tile_cols
    size = cells * (channels // GROUPS)
    even = lax.rem(place(LAT), 2) == 0

    def put_rims(field, sample, top, bottom):
        top, bottom = top.astype(F32), bottom.astype(F32)
        inner_out[field, sample] = jnp.where(even, bottom, top).astype(BF16)
        outer_out[field, sample] = jnp.where(even, top, bottom).astype(BF16)

    null32 = null[...].astype(F32)
    fields, sums = [], []
    for sample in range(samples):
        for copy in field_copies[sample]:
            copy.wait()
        dropped = flags[sample : sample + 1, :].astype(F32).reshape(1, 1, channels)
        mixed = (
            feats[sample].astype(F32) + dropped * null32 + (1.0 - dropped) * cond[sample].astype(F32)
        ).astype(BF16)
        mixed_out[sample] = mixed
        put_rims(0, sample, mixed[0], mixed[tile_rows - 1])
        fields.append(mixed.astype(F32).reshape(cells, channels))
        sums.append(jnp.sum(fields[-1], axis=0, keepdims=True))
    means = group_total(jnp.concatenate(sums, axis=0)) * (1.0 / size)
    sums = []
    for sample in range(samples):
        away = fields[sample] - means[sample : sample + 1, :]
        sums.append(jnp.sum(away * away, axis=0, keepdims=True))
    spreads = group_total(jnp.concatenate(sums, axis=0))
    means, spreads = (means[0:1, :], means[1:2, :]), (spreads[0:1, :], spreads[1:2, :])
    rows = header(weave(*means), weave(*spreads))
    cot_copy.wait()
    firsts, lasts = [], []
    for sample in range(samples):
        put_rims(1, sample, cot[sample, 0], cot[sample, tile_rows - 1])
        wide = cot[sample].astype(F32)
        firsts.append(wide[:, 0, :])
        lasts.append(wide[:, tile_cols - 1, :])
    slots_out[...] = jnp.broadcast_to(
        jnp.concatenate(rows + firsts, axis=0).astype(BF16)[None], slots_out.shape
    )
    after = lax.rem(place(LON) + 1, slots_out.shape[0])
    slots_out[after] = jnp.concatenate(rows + lasts, axis=0).astype(BF16)


def merge_body(count, slots, cot, wide_out, slots_out):
    samples, tile_rows, tile_cols, channels = cot.shape
    lon_count, lat_count = slots.shape[0], slots_out.shape[0]
    mean, spread = merged(slots, count)
    me = place(LON)
    before = slots[lax.rem(me + lon_count - 1, lon_count)].astype(F32)
    after = slots[lax.rem(me + 1, lon_count)].astype(F32)
    for sample in range(samples):
        here = slice(8 + sample * tile_rows, 8 + (sample + 1) * tile_rows)
        wide_out[sample, :, 0, :] = before[here, :]
        wide_out[sample, :, 1 : 1 + tile_cols, :] = cot[sample].astype(F32)
        wide_out[sample, :, 1 + tile_cols, :] = after[here, :]
    rows = header(mean, spread)

    def slot(row):
        corners = [
            wide_out[sample, row, side : side + 1, :]
            for sample in range(samples)
            for side in (0, 1 + tile_cols)
        ]
        spare = jnp.zeros((slots_out.shape[1] - 8 - len(corners), channels), F32)
        return jnp.concatenate(rows + corners + [spare], axis=0).astype(BF16)

    slots_out[...] = jnp.broadcast_to(slot(0)[None], slots_out.shape)
    row = place(LAT)

    @pl.when(row < lat_count - 1)
    def _():
        slots_out[row + 1] = slot(tile_rows - 1)


def columns_body(mixed, inner, outer, edges_out, send_out):
    samples, _, tile_cols, channels = mixed.shape
    spare = [jnp.zeros((send_out.shape[0] - edges_out.shape[0] // 2, channels), F32)]

    def column(at):
        parts = []
        for sample in range(samples):
            low, high = halos(inner, outer, 0, sample)
            parts.append(low[at : at + 1, :])
            parts.append(mixed[sample].astype(F32)[:, at, :])
            parts.append(high[at : at + 1, :])
        return parts

    first, last = column(0), column(tile_cols - 1)
    edges_out[...] = jnp.concatenate(first + last, axis=0).astype(BF16)
    first, last = jnp.concatenate(first + spare, axis=0), jnp.concatenate(last + spare, axis=0)
    send_out[...] = jnp.where(place(("c",)) == 0, first, last).astype(BF16)


def weights_body(
    emb, style_weight, gamma, beta, weight,
    gamma_out, beta_out, style_out, column_out, demod_out, power_out, emb_out, back_out, taps_out,
):
    gamma_out[...] = gamma[...]
    beta_out[...] = beta[...]
    power = jnp.zeros(weight.shape[1:], F32)
    for tap in range(9):
        power = power + weight[tap] * weight[tap]
    samples, channels = emb.shape[0], weight.shape[2]
    exact = lax.Precision.HIGHEST
    style = 1.0 + jnp.dot(
        emb[...], style_weight[...], precision=exact, preferred_element_type=F32
    )
    squares = jnp.dot(style * style, power, precision=exact, preferred_element_type=F32)
    demod = lax.rsqrt(squares + 1e-08)
    style_out[...] = style
    demod_out[...] = demod
    power_out[...] = power
    for sample in range(samples):
        here = slice(sample, sample + 1)
        column = jnp.broadcast_to(style[here, :], (channels, channels)).T
        column_out[sample] = column
        emb_out[sample] = jnp.broadcast_to(emb[here, :], (channels, emb.shape[1])).T
        for tap in range(9):
            row, col = tap // 3, tap % 3
            block = weight[tap] * column * demod[here, :]
            taps_out[sample, row, col * channels : (col + 1) * channels, :] = block.astype(BF16)
            row, col = 2 - row, 2 - col
            back_out[sample, row, col * channels : (col + 1) * channels, :] = block.T.astype(BF16)


def windows(spread, shifted, rows, cols):
    channels = spread.shape[-1]
    for tap in range(3):
        moved = spread[:, tap : tap + cols, :].reshape((rows + 2) * cols, channels)
        shifted[:, tap * channels : (tap + 1) * channels] = moved.astype(BF16)


def forward_body(
    mixed, inner, outer, other, passed, taps, stats, gamma, beta, block_out, spread, shifted
):
    samples, rows, cols, _ = mixed.shape
    size = rows * cols
    row = lax.broadcasted_iota(jnp.int32, spread.shape, 0) + place(LAT) * rows
    inside = (row > 0) & (row <= rows * lax.axis_size(LAT))
    core = place(("c",))
    mate, away = other[...].astype(F32), passed[...].astype(F32)
    half = samples * (rows + 2)
    left = jnp.where(core == 0, away[:half, :], mate[half : 2 * half, :])
    right = jnp.where(core == 0, mate[:half, :], away[:half, :])
    for sample in range(samples):
        here = slice(sample * (rows + 2), (sample + 1) * (rows + 2))
        spread[:, 0, :] = left[here, :]
        spread[:, 1 + cols, :] = right[here, :]
        low, high = halos(inner, outer, 0, sample)
        spread[0, 1 : 1 + cols, :] = low
        spread[1 : 1 + rows, 1 : 1 + cols, :] = mixed[sample].astype(F32)
        spread[1 + rows, 1 : 1 + cols, :] = high
        mean = stats[sample : sample + 1, :][None]
        inverse = stats[samples + sample : samples + sample + 1, :][None]
        pre = (spread[...] - mean) * inverse * gamma[...][None] + beta[...][None]
        spread[...] = jnp.where(inside, pre / (1.0 + jnp.exp(-pre)), 0.0)
        windows(spread, shifted, rows, cols)
        total = mixed[sample].astype(F32).reshape(size, -1)
        for row_tap in range(3):
            window = shifted[row_tap * cols : row_tap * cols + size, :]
            total = total + jnp.dot(window, taps[sample, row_tap], preferred_element_type=F32)
        block_out[sample] = total.astype(BF16).reshape(rows, cols, -1)


def sums_body(
    count, cells, slots, mixed, edges, wide, inner, outer, gamma, beta, back_taps, column, demod,
    weight, stats_out, grad_out, payload_out, edge, spread, shifted, total,
):
    samples, rows, cols, channels = mixed.shape
    size = rows * cols
    mean_all, spread_all = merged(slots, count)
    inverse_all = lax.rsqrt(spread_all * (1.0 / cells) + 1e-05)
    lat_count, row = slots.shape[0], place(LAT)
    below = slots[lax.max(row - 1, 0)].astype(F32)
    above = slots[lax.min(row + 1, lat_count - 1)].astype(F32)
    edge[0] = jnp.where(row > 0, below, 0.0)
    edge[1] = jnp.where(row < lat_count - 1, above, 0.0)
    sums = [[], [], [], []]
    for sample in range(samples):
        mean, inverse = unweave(mean_all, sample), unweave(inverse_all, sample)
        stats_out[sample : sample + 1, :] = mean
        stats_out[samples + sample : samples + sample + 1, :] = inverse
        flat = mixed[sample].reshape(size, channels).astype(F32)
        norm = (flat - mean) * inverse
        pre = norm * gamma[...] + beta[...]
        sig = 1.0 / (1.0 + jnp.exp(-pre))
        act = (pre * sig).astype(BF16)
        slope = sig * (1.0 + pre * (1.0 - sig))
        spread[1 : 1 + rows] = wide[sample]
        low, high = halos(inner, outer, 1, sample)
        for at, halo, corner in ((0, low, edge[0]), (1 + rows, high, edge[1])):
            spread[at, 1 : 1 + cols, :] = halo
            start = 8 + 2 * sample
            spread[at, 0:1, :] = corner[start : start + 1, :]
            spread[at, 1 + cols : 2 + cols, :] = corner[start + 1 : start + 2, :]
        windows(spread, shifted, rows, cols)
        style_full = column[sample]
        demod_row = demod[sample : sample + 1, :]
        both = style_full * demod_row
        product = jnp.zeros((channels, channels), F32)
        grad_act = jnp.zeros((size, channels), F32)
        for row_tap in range(3):
            window = shifted[row_tap * cols : row_tap * cols + size, :]
            grad_act = grad_act + jnp.dot(
                window, back_taps[sample, row_tap], preferred_element_type=F32
            )
            grad = lax.dot_general(
                act, window, (((0,), (0,)), ((), ())), preferred_element_type=F32
            )
            for col_tap in range(3):
                tap = (2 - row_tap) * 3 + 2 - col_tap
                block = grad[:, col_tap * channels : (col_tap + 1) * channels]
                product = product + block * weight[tap]
                here = slice(tap * channels, (tap + 1) * channels)
                part = block * both
                total[here, :] = part if sample == 0 else total[here, :] + part
        grad_pre = grad_act * slope
        grad_out[sample] = grad_pre
        sums[0].append(jnp.sum(product * style_full, axis=0, keepdims=True))
        sums[1].append(jnp.sum((product * demod_row).T, axis=0, keepdims=True))
        sums[2].append(jnp.sum(grad_pre * norm, axis=0, keepdims=True))
        sums[3].append(jnp.sum(grad_pre, axis=0, keepdims=True))
    payload_out[SHARDS] = edges[...]
    small = jnp.concatenate(sum(sums, []), axis=0)
    lane = lanes_of(TILE)
    sub = lax.broadcasted_iota(jnp.int32, (TILE, channels), 0)
    quarters = []
    for quarter in range(4):
        turned = pltpu.roll(small, LANES - 32 * quarter, 1) if quarter else small
        piece = jnp.where(lane < 64, turned, pltpu.roll(turned, 64, 1))
        piece = jnp.where((lane & 32) == 0, piece, 0.0)
        quarters.append(split_terms(piece, lane))
    for shard in range(SHARDS):
        main = total[32 * shard : 32 * shard + 32, :]
        start = 8 * channels + 8 * (shard // 2)
        last = total[start : start + 8, :]
        if shard % 2:
            last = pltpu.roll(last, 4, 0)
        extra = quarters[shard % 4][shard // 4 : shard // 4 + 1, :]
        tail = jnp.where(sub < 4, last, jnp.where(sub == 4, extra, 0.0))
        payload_out[shard] = jnp.concatenate([main, tail], axis=0).astype(BF16)


def split_terms(values, lane):
    high = values.astype(BF16).astype(F32)
    return jnp.where(lane < 64, high, values - high)


def resplit(slots):
    main, tail = slots[:, 0:32, :], slots[:, 32:SLOT, :]
    flat = tail.reshape(-1, LANES)
    lane = lax.broadcasted_iota(jnp.int32, flat.shape, 1)
    row = lax.broadcasted_iota(jnp.int32, flat.shape, 0) & 7
    terms = split_terms(flat + pltpu.roll(flat, 64, 1), lane)
    tail = jnp.where(row == 4, terms, flat).reshape(tail.shape)
    return jnp.concatenate([main, tail], axis=1)


def core_body(gathered, slots_out, other_out):
    core, near_count = place(("c",)), slots_out.shape[0]
    mine = pl.ds(core * near_count, near_count)
    total = gathered[0, mine].astype(F32) + gathered[1, mine].astype(F32)
    other_out[...] = gathered[1 - core, SHARDS]
    slots_out[...] = resplit(total).astype(BF16)


def sum_body(slots, slots_out):
    total = jnp.sum(slots[...].astype(F32), axis=0)
    slots_out[...] = jnp.broadcast_to(resplit(total[None]).astype(BF16), slots_out.shape)


def last_body(
    scale, cells, gathered, stats, mixed, cotangent, grad_pre, gamma, style, column, demod,
    power, weight, emb_full, feats_out, weight_out, style_out, gamma_out, beta_out,
):
    samples, tile_rows, tile_cols, channels = cotangent.shape
    size = tile_rows * tile_cols
    lane = lanes_of()
    sub = lax.broadcasted_iota(jnp.int32, (TILE, channels), 0)
    main, tails, small = [], [], []
    for shard in range(SHARDS):
        slot = gathered[shard].astype(F32)
        main.append(slot[0:32, :])
        tails.append(slot[32:40, :])
    for row in range(TILE):
        whole = jnp.zeros((1, channels), F32)
        for quarter in range(4):
            piece = tails[4 * row + quarter][4:5, :]
            piece = piece + pltpu.roll(piece, 64, 1)
            if quarter:
                piece = pltpu.roll(piece, 32 * quarter, 1)
            whole = jnp.where((lane >> 5) == quarter, piece, whole)
        small.append(whole)
    demod_sums, style_sums, gamma_sums, beta_sums = small[0:2], small[2:4], small[4:6], small[6:8]
    gain = gamma[...]
    group_means = group_total(gain * jnp.concatenate(beta_sums + gamma_sums, axis=0)) * (1.0 / cells)
    gamma_out[...] = scale * (gamma_sums[0] + gamma_sums[1])
    beta_out[...] = scale * (beta_sums[0] + beta_sums[1])
    shrink = jnp.zeros((channels, channels), F32)
    rows = []
    for sample in range(samples):
        demod_row = demod[sample : sample + 1, :]
        pulled = demod_sums[sample] * (demod_row * demod_row * demod_row)
        style_full = column[sample]
        shrink = shrink + style_full * style_full * pulled
        spent = jnp.sum((power[...] * pulled).T, axis=0, keepdims=True)
        rows.append(style_sums[sample] - style[sample : sample + 1, :] * spent)
    for tap in range(8):
        for part in range(4):
            here = slice(32 * part, 32 * part + 32)
            weight_out[tap, here, :] = scale * (
                main[4 * tap + part] - shrink[here, :] * weight[tap, here, :]
            )
    for pair in range(16):
        here = slice(8 * pair, 8 * pair + 8)
        block = jnp.where(sub < 4, tails[2 * pair], pltpu.roll(tails[2 * pair + 1], 4, 0))
        weight_out[8, here, :] = scale * (block - shrink[here, :] * weight[8, here, :])
    style_out[...] = scale * (emb_full[0] * rows[0] + emb_full[1] * rows[1])
    for sample in range(samples):
        inverse = stats[samples + sample : samples + sample + 1, :]
        product_mean = group_means[sample : sample + 1, :]
        squared_mean = group_means[samples + sample : samples + sample + 1, :]
        flat = mixed[sample].astype(F32).reshape(size, channels)
        norm = (flat - stats[sample : sample + 1, :]) * inverse
        change = inverse * (gain * grad_pre[sample] - product_mean - norm * squared_mean)
        out = cotangent[sample].reshape(size, channels).astype(F32) + change
        feats_out[sample] = out.astype(BF16).reshape(tile_rows, tile_cols, channels)


def on_device(
    feats, cond, null_field, drop_flags, emb, style_weight, conv_weight, gamma, beta, cotangent
):
    samples, tile_rows, tile_cols, channels = feats.shape
    group_size = channels // GROUPS
    lat_count, lon_count = lax.axis_size(LAT), lax.axis_size(LON)
    devices_all = lat_count * lon_count
    cells_local = tile_rows * tile_cols * group_size
    cells_per_group = cells_local * devices_all
    scale_gradient = 1.0 / math.sqrt(samples * tile_rows * tile_cols * devices_all)
    taps = conv_weight.reshape(9, channels, channels)

    lon_slot, lat_slot = 8 + samples * tile_rows, 16
    rim = array((2, samples, tile_cols, channels), BF16)
    mixed, slots, inner, outer = call(
        mix_body,
        (array(feats.shape, BF16), array((lon_count, lon_slot, LANES), BF16), rim, rim),
        (
            pltpu.VMEM(feats.shape, BF16),
            pltpu.VMEM(feats.shape, BF16),
            pltpu.VMEM(null_field.shape, BF16),
            pltpu.VMEM(feats.shape, BF16),
            pltpu.VMEM(drop_flags.shape, jnp.int32),
            pltpu.SemaphoreType.DMA((2 * samples + 3,)),
        ),
        room=60,
        in_specs=[pl.BlockSpec(memory_space=pl.ANY)] * 5,
    )(feats, cond, null_field, cotangent, drop_flags)
    slots = exchange(slots, LON)
    outer, inner = swap(outer, LAT, 1, False), swap(inner, LAT, 0, False)
    wide_cot, slots = call(
        functools.partial(merge_body, cells_local),
        (
            array((samples, tile_rows, tile_cols + 2, channels)),
            array((lat_count, lat_slot, LANES), BF16),
        ),
    )(slots, cotangent)
    slots, outer, inner = lax.optimization_barrier((slots, outer, inner))
    slots = exchange(slots, LAT)
    half = samples * (tile_rows + 2)
    edges, passed = call(
        columns_body, (array((SLOT, LANES), BF16), array((-(-half // 8) * 8, LANES), BF16))
    )(mixed, inner, outer)
    passed = swap(passed, LON, 1, True)

    taps_shape = (samples, 3, 3 * channels, channels)
    gamma, beta, style, column, demod, power, emb_full, back_taps, fore_taps = call(
        weights_body,
        (
            array((1, channels)),
            array((1, channels)),
            array((samples, channels)),
            array((samples, channels, channels)),
            array((samples, channels)),
            array((channels, channels)),
            array((samples,) + style_weight.shape),
            array(taps_shape, BF16),
            array(taps_shape, BF16),
        ),
    )(emb, style_weight, gamma[None], beta[None], taps)
    spread = pltpu.VMEM((tile_rows + 2, tile_cols + 2, channels), F32)
    shifted = pltpu.VMEM(((tile_rows + 2) * tile_cols, 3 * channels), BF16)
    flat = (samples, tile_rows * tile_cols, channels)
    stats, grad_pre, payload = call(
        functools.partial(sums_body, cells_local * lon_count, cells_per_group),
        (
            array((2 * samples, LANES)),
            array(flat),
            array((SHARDS + 1, SLOT, LANES), BF16),
        ),
        (
            pltpu.VMEM((2, lat_slot, LANES), F32),
            spread,
            shifted,
            pltpu.VMEM((9 * channels, channels), F32),
        ),
    )(
        slots, mixed, edges, wide_cot, inner, outer, gamma, beta, back_taps, column, demod, taps
    )

    near_count = lax.axis_size(NEAR)
    shard = array((near_count, SLOT, LANES), BF16)
    slots, other = call(core_body, (shard, array((SLOT, LANES), BF16)))(
        lax.all_gather(payload, "c")
    )
    slots, passed = lax.optimization_barrier((slots, passed))
    summed = array((lat_count, SLOT, LANES), BF16)
    slots = call(sum_body, summed)(exchange(slots, NEAR))
    slots = call(sum_body, shard)(exchange(slots, LAT))
    payload = lax.all_gather(exchange(slots, NEAR), "c")
    block_out = call(forward_body, array(feats.shape, BF16), (spread, shifted))(
        mixed, inner, outer, other, passed, fore_taps, stats, gamma, beta
    )

    grad_feats, grad_weight, grad_style, grad_gamma, grad_beta = call(
        functools.partial(last_body, scale_gradient, cells_per_group),
        (
            array(feats.shape, BF16),
            array(taps.shape),
            array(style_weight.shape),
            array((1, LANES)),
            array((1, LANES)),
        ),
    )(
        payload.reshape(SHARDS, SLOT, LANES), stats, mixed, cotangent, grad_pre, gamma, style,
        column, demod, power, taps, emb_full,
    )
    return (
        block_out,
        grad_feats,
        grad_weight.reshape(conv_weight.shape),
        grad_style,
        grad_gamma[0],
        grad_beta[0],
    )


def solution(mesh):
    parts = Mesh(mesh.devices.reshape(4, 4, 2, 8, 2), LAT + LON)
    tile = P(None, LAT, LON, None)
    placed = (tile, tile, P(LAT, LON, None), P(), P(), P(), P(), P(), P(), tile)
    return jax.shard_map(
        on_device,
        mesh=parts,
        in_specs=placed,
        out_specs=(tile, tile, P(), P(), P(), P()),
        check_vma=False,
    )
```

```python
import functools
import math

import jax
import jax.numpy as jnp
from jax import lax
from jax.experimental import pallas as pl
from jax.experimental.pallas import tpu as pltpu
from jax.sharding import Mesh, PartitionSpec as P

GROUPS = 32
LAT = ("zh", "x")
LON = ("zl", "y", "c")
NEAR = ("zl", "y")
F32 = jnp.float32
BF16 = jnp.bfloat16
TILE = 8
SHARDS = 32
SLOT = 40
LANES = 128


def swap(block, axes, first, periodic):
    count = lax.axis_size(axes)
    pairs = [(i, (i + 1) % count) for i in range(first, count, 2) if periodic or i + 1 < count]
    return lax.ppermute(block, axes, pairs + [(target, source) for source, target in pairs])


def halos(inner, outer, field, sample):
    near, far = inner[field, sample].astype(F32), outer[field, sample].astype(F32)
    even = lax.rem(place(LAT), 2) == 0
    return jnp.where(even, far, near), jnp.where(even, near, far)


def exchange(block, axes):
    return lax.all_to_all(block, axes, 0, 0)


def call(body, outputs, scratch=(), room=24, **more):
    return pl.pallas_call(
        body,
        out_shape=outputs,
        scratch_shapes=list(scratch),
        **more,
        compiler_params=pltpu.CompilerParams(vmem_limit_bytes=room * 1024 * 1024),
    )


def array(shape, dtype=F32):
    return jax.ShapeDtypeStruct(shape, dtype)


def lanes_of(rows=1):
    return lax.broadcasted_iota(jnp.int32, (rows, LANES), 1)


def group_total(row):
    lane = lanes_of()
    for step in (1, 2):
        after, before = pltpu.roll(row, LANES - step, 1), pltpu.roll(row, step, 1)
        row = row + jnp.where((lane & step) == 0, after, before)
    return row


def weave(first, second):
    return jnp.where((lanes_of() & 1) == 0, first, second)


def unweave(row, sample):
    if sample == 0:
        return weave(row, pltpu.roll(row, 1, 1))
    return weave(pltpu.roll(row, LANES - 1, 1), row)


def place(axes):
    index = 0
    for axis in axes:
        index = index * lax.axis_size(axis) + lax.axis_index(axis)
    return index


def three_terms(value):
    terms = []
    for _ in range(3):
        terms.append(value.astype(BF16).astype(F32))
        value = value - terms[-1]
    return terms


def merged(slots, count):
    rows = slots[:, 0:8, :].astype(F32)
    means = rows[:, 0:1, :] + rows[:, 1:2, :] + rows[:, 2:3, :]
    spreads = rows[:, 3:4, :] + rows[:, 4:5, :] + rows[:, 5:6, :]
    mean = jnp.mean(means, axis=0)
    away = means - mean[None]
    return mean, jnp.sum(spreads + count * away * away, axis=0)


def header(mean, spread):
    return three_terms(mean) + three_terms(spread) + [jnp.zeros((2, LANES), F32)]


def fetcher(arrivals):
    used = iter(range(arrivals.shape[0]))

    def fetch(source, target):
        copy = pltpu.make_async_copy(source, target, arrivals.at[next(used)])
        copy.start()
        return copy

    return fetch


def mix_body(
    feats_in, cond_in, null_in, cot_in, flags_in, mixed_out, slots_out, inner_out, outer_out,
    feats, cond, null, cot, flags, arrivals,
):
    fetch = fetcher(arrivals)
    flags_copy, null_copy = fetch(flags_in, flags), fetch(null_in, null)
    field_copies = [
        (fetch(feats_in.at[sample], feats.at[sample]), fetch(cond_in.at[sample], cond.at[sample]))
        for sample in range(feats.shape[0])
    ]
    cot_copy = fetch(cot_in, cot)
    flags_copy.wait()
    null_copy.wait()
    samples, tile_rows, tile_cols, channels = feats.shape
    cells = tile_rows * tile_cols
    size = cells * (channels // GROUPS)
    even = lax.rem(place(LAT), 2) == 0

    def put_rims(field, sample, top, bottom):
        top, bottom = top.astype(F32), bottom.astype(F32)
        inner_out[field, sample] = jnp.where(even, bottom, top).astype(BF16)
        outer_out[field, sample] = jnp.where(even, top, bottom).astype(BF16)

    null32 = null[...].astype(F32)
    fields, sums = [], []
    for sample in range(samples):
        for copy in field_copies[sample]:
            copy.wait()
        dropped = flags[sample : sample + 1, :].astype(F32).reshape(1, 1, channels)
        mixed = (
            feats[sample].astype(F32) + dropped * null32 + (1.0 - dropped) * cond[sample].astype(F32)
        ).astype(BF16)
        mixed_out[sample] = mixed
        put_rims(0, sample, mixed[0], mixed[tile_rows - 1])
        fields.append(mixed.astype(F32).reshape(cells, channels))
        sums.append(jnp.sum(fields[-1], axis=0, keepdims=True))
    means = group_total(jnp.concatenate(sums, axis=0)) * (1.0 / size)
    sums = []
    for sample in range(samples):
        away = fields[sample] - means[sample : sample + 1, :]
        sums.append(jnp.sum(away * away, axis=0, keepdims=True))
    spreads = group_total(jnp.concatenate(sums, axis=0))
    means, spreads = (means[0:1, :], means[1:2, :]), (spreads[0:1, :], spreads[1:2, :])
    rows = header(weave(*means), weave(*spreads))
    cot_copy.wait()
    firsts, lasts = [], []
    for sample in range(samples):
        put_rims(1, sample, cot[sample, 0], cot[sample, tile_rows - 1])
        wide = cot[sample].astype(F32)
        firsts.append(wide[:, 0, :])
        lasts.append(wide[:, tile_cols - 1, :])
    slots_out[...] = jnp.broadcast_to(
        jnp.concatenate(rows + firsts, axis=0).astype(BF16)[None], slots_out.shape
    )
    after = lax.rem(place(LON) + 1, slots_out.shape[0])
    slots_out[after] = jnp.concatenate(rows + lasts, axis=0).astype(BF16)


def merge_body(count, slots, cot, wide_out, slots_out):
    samples, tile_rows, tile_cols, channels = cot.shape
    lon_count, lat_count = slots.shape[0], slots_out.shape[0]
    mean, spread = merged(slots, count)
    me = place(LON)
    before = slots[lax.rem(me + lon_count - 1, lon_count)].astype(F32)
    after = slots[lax.rem(me + 1, lon_count)].astype(F32)
    for sample in range(samples):
        here = slice(8 + sample * tile_rows, 8 + (sample + 1) * tile_rows)
        wide_out[sample, :, 0, :] = before[here, :]
        wide_out[sample, :, 1 : 1 + tile_cols, :] = cot[sample].astype(F32)
        wide_out[sample, :, 1 + tile_cols, :] = after[here, :]
    rows = header(mean, spread)

    def slot(row):
        corners = [
            wide_out[sample, row, side : side + 1, :]
            for sample in range(samples)
            for side in (0, 1 + tile_cols)
        ]
        spare = jnp.zeros((slots_out.shape[1] - 8 - len(corners), channels), F32)
        return jnp.concatenate(rows + corners + [spare], axis=0).astype(BF16)

    slots_out[...] = jnp.broadcast_to(slot(0)[None], slots_out.shape)
    row = place(LAT)

    @pl.when(row < lat_count - 1)
    def _():
        slots_out[row + 1] = slot(tile_rows - 1)


def columns_body(mixed, inner, outer, edges_out, send_out):
    samples, _, tile_cols, channels = mixed.shape
    spare = [jnp.zeros((send_out.shape[0] - edges_out.shape[0] // 2, channels), F32)]

    def column(at):
        parts = []
        for sample in range(samples):
            low, high = halos(inner, outer, 0, sample)
            parts.append(low[at : at + 1, :])
            parts.append(mixed[sample].astype(F32)[:, at, :])
            parts.append(high[at : at + 1, :])
        return parts

    first, last = column(0), column(tile_cols - 1)
    edges_out[...] = jnp.concatenate(first + last, axis=0).astype(BF16)
    first, last = jnp.concatenate(first + spare, axis=0), jnp.concatenate(last + spare, axis=0)
    send_out[...] = jnp.where(place(("c",)) == 0, first, last).astype(BF16)


def weights_body(
    emb, style_weight, gamma, beta, weight,
    gamma_out, beta_out, style_out, column_out, demod_out, power_out, emb_out, back_out, taps_out,
):
    gamma_out[...] = gamma[...]
    beta_out[...] = beta[...]
    power = jnp.zeros(weight.shape[1:], F32)
    for tap in range(9):
        power = power + weight[tap] * weight[tap]
    samples, channels = emb.shape[0], weight.shape[2]
    exact = lax.Precision.HIGHEST
    style = 1.0 + jnp.dot(
        emb[...], style_weight[...], precision=exact, preferred_element_type=F32
    )
    squares = jnp.dot(style * style, power, precision=exact, preferred_element_type=F32)
    demod = lax.rsqrt(squares + 1e-08)
    style_out[...] = style
    demod_out[...] = demod
    power_out[...] = power
    for sample in range(samples):
        here = slice(sample, sample + 1)
        column = jnp.broadcast_to(style[here, :], (channels, channels)).T
        column_out[sample] = column
        emb_out[sample] = jnp.broadcast_to(emb[here, :], (channels, emb.shape[1])).T
        for tap in range(9):
            row, col = tap // 3, tap % 3
            block = weight[tap] * column * demod[here, :]
            taps_out[sample, row, col * channels : (col + 1) * channels, :] = block.astype(BF16)
            row, col = 2 - row, 2 - col
            back_out[sample, row, col * channels : (col + 1) * channels, :] = block.T.astype(BF16)


def windows(spread, shifted, rows, cols):
    channels = spread.shape[-1]
    for tap in range(3):
        moved = spread[:, tap : tap + cols, :].reshape((rows + 2) * cols, channels)
        shifted[:, tap * channels : (tap + 1) * channels] = moved.astype(BF16)


def forward_body(
    mixed, inner, outer, other, passed, taps, stats, gamma, beta, block_out, spread, shifted
):
    samples, rows, cols, _ = mixed.shape
    size = rows * cols
    row = lax.broadcasted_iota(jnp.int32, spread.shape, 0) + place(LAT) * rows
    inside = (row > 0) & (row <= rows * lax.axis_size(LAT))
    core = place(("c",))
    mate, away = other[...].astype(F32), passed[...].astype(F32)
    half = samples * (rows + 2)
    left = jnp.where(core == 0, away[:half, :], mate[half : 2 * half, :])
    right = jnp.where(core == 0, mate[:half, :], away[:half, :])
    for sample in range(samples):
        here = slice(sample * (rows + 2), (sample + 1) * (rows + 2))
        spread[:, 0, :] = left[here, :]
        spread[:, 1 + cols, :] = right[here, :]
        low, high = halos(inner, outer, 0, sample)
        spread[0, 1 : 1 + cols, :] = low
        spread[1 : 1 + rows, 1 : 1 + cols, :] = mixed[sample].astype(F32)
        spread[1 + rows, 1 : 1 + cols, :] = high
        mean = stats[sample : sample + 1, :][None]
        inverse = stats[samples + sample : samples + sample + 1, :][None]
        pre = (spread[...] - mean) * inverse * gamma[...][None] + beta[...][None]
        spread[...] = jnp.where(inside, pre / (1.0 + jnp.exp(-pre)), 0.0)
        windows(spread, shifted, rows, cols)
        total = mixed[sample].astype(F32).reshape(size, -1)
        for row_tap in range(3):
            window = shifted[row_tap * cols : row_tap * cols + size, :]
            total = total + jnp.dot(window, taps[sample, row_tap], preferred_element_type=F32)
        block_out[sample] = total.astype(BF16).reshape(rows, cols, -1)


def sums_body(
    count, cells, slots, mixed, edges, wide, inner, outer, gamma, beta, back_taps, column, demod,
    weight, stats_out, grad_out, payload_out, edge, spread, shifted, total,
):
    samples, rows, cols, channels = mixed.shape
    size = rows * cols
    mean_all, spread_all = merged(slots, count)
    inverse_all = lax.rsqrt(spread_all * (1.0 / cells) + 1e-05)
    lat_count, row = slots.shape[0], place(LAT)
    below = slots[lax.max(row - 1, 0)].astype(F32)
    above = slots[lax.min(row + 1, lat_count - 1)].astype(F32)
    edge[0] = jnp.where(row > 0, below, 0.0)
    edge[1] = jnp.where(row < lat_count - 1, above, 0.0)
    sums = [[], [], [], []]
    for sample in range(samples):
        mean, inverse = unweave(mean_all, sample), unweave(inverse_all, sample)
        stats_out[sample : sample + 1, :] = mean
        stats_out[samples + sample : samples + sample + 1, :] = inverse
        flat = mixed[sample].reshape(size, channels).astype(F32)
        norm = (flat - mean) * inverse
        pre = norm * gamma[...] + beta[...]
        sig = 1.0 / (1.0 + jnp.exp(-pre))
        act = (pre * sig).astype(BF16)
        slope = sig * (1.0 + pre * (1.0 - sig))
        spread[1 : 1 + rows] = wide[sample]
        low, high = halos(inner, outer, 1, sample)
        for at, halo, corner in ((0, low, edge[0]), (1 + rows, high, edge[1])):
            spread[at, 1 : 1 + cols, :] = halo
            start = 8 + 2 * sample
            spread[at, 0:1, :] = corner[start : start + 1, :]
            spread[at, 1 + cols : 2 + cols, :] = corner[start + 1 : start + 2, :]
        windows(spread, shifted, rows, cols)
        style_full = column[sample]
        demod_row = demod[sample : sample + 1, :]
        both = style_full * demod_row
        product = jnp.zeros((channels, channels), F32)
        grad_act = jnp.zeros((size, channels), F32)
        for row_tap in range(3):
            window = shifted[row_tap * cols : row_tap * cols + size, :]
            grad_act = grad_act + jnp.dot(
                window, back_taps[sample, row_tap], preferred_element_type=F32
            )
            grad = lax.dot_general(
                act, window, (((0,), (0,)), ((), ())), preferred_element_type=F32
            )
            for col_tap in range(3):
                tap = (2 - row_tap) * 3 + 2 - col_tap
                block = grad[:, col_tap * channels : (col_tap + 1) * channels]
                product = product + block * weight[tap]
                here = slice(tap * channels, (tap + 1) * channels)
                part = block * both
                total[here, :] = part if sample == 0 else total[here, :] + part
        grad_pre = grad_act * slope
        grad_out[sample] = grad_pre
        sums[0].append(jnp.sum(product * style_full, axis=0, keepdims=True))
        sums[1].append(jnp.sum((product * demod_row).T, axis=0, keepdims=True))
        sums[2].append(jnp.sum(grad_pre * norm, axis=0, keepdims=True))
        sums[3].append(jnp.sum(grad_pre, axis=0, keepdims=True))
    payload_out[SHARDS] = edges[...]
    small = jnp.concatenate(sum(sums, []), axis=0)
    lane = lanes_of(TILE)
    sub = lax.broadcasted_iota(jnp.int32, (TILE, channels), 0)
    quarters = []
    for quarter in range(4):
        turned = pltpu.roll(small, LANES - 32 * quarter, 1) if quarter else small
        piece = jnp.where(lane < 64, turned, pltpu.roll(turned, 64, 1))
        piece = jnp.where((lane & 32) == 0, piece, 0.0)
        quarters.append(split_terms(piece, lane))
    for shard in range(SHARDS):
        main = total[32 * shard : 32 * shard + 32, :]
        start = 8 * channels + 8 * (shard // 2)
        last = total[start : start + 8, :]
        if shard % 2:
            last = pltpu.roll(last, 4, 0)
        extra = quarters[shard % 4][shard // 4 : shard // 4 + 1, :]
        tail = jnp.where(sub < 4, last, jnp.where(sub == 4, extra, 0.0))
        payload_out[shard] = jnp.concatenate([main, tail], axis=0).astype(BF16)


def split_terms(values, lane):
    high = values.astype(BF16).astype(F32)
    return jnp.where(lane < 64, high, values - high)


def resplit(slots):
    main, tail = slots[:, 0:32, :], slots[:, 32:SLOT, :]
    flat = tail.reshape(-1, LANES)
    lane = lax.broadcasted_iota(jnp.int32, flat.shape, 1)
    row = lax.broadcasted_iota(jnp.int32, flat.shape, 0) & 7
    terms = split_terms(flat + pltpu.roll(flat, 64, 1), lane)
    tail = jnp.where(row == 4, terms, flat).reshape(tail.shape)
    return jnp.concatenate([main, tail], axis=1)


def core_body(gathered, slots_out, other_out):
    core, near_count = place(("c",)), slots_out.shape[0]
    mine = pl.ds(core * near_count, near_count)
    total = gathered[0, mine].astype(F32) + gathered[1, mine].astype(F32)
    other_out[...] = gathered[1 - core, SHARDS]
    slots_out[...] = resplit(total).astype(BF16)


def sum_body(slots, slots_out):
    total = jnp.sum(slots[...].astype(F32), axis=0)
    slots_out[...] = jnp.broadcast_to(resplit(total[None]).astype(BF16), slots_out.shape)


def last_body(
    scale, cells, gathered, stats, mixed, cotangent, grad_pre, gamma, beta, style, column, demod,
    power, weight, emb_full, inner, outer, other, passed, fore_taps,
    feats_out, weight_out, style_out, gamma_out, beta_out, block_out, spread, shifted,
):
    samples, tile_rows, tile_cols, channels = cotangent.shape
    size = tile_rows * tile_cols
    lane = lanes_of()
    sub = lax.broadcasted_iota(jnp.int32, (TILE, channels), 0)
    main, tails, small = [], [], []
    for shard in range(SHARDS):
        slot = gathered[shard].astype(F32)
        main.append(slot[0:32, :])
        tails.append(slot[32:40, :])
    for row in range(TILE):
        whole = jnp.zeros((1, channels), F32)
        for quarter in range(4):
            piece = tails[4 * row + quarter][4:5, :]
            piece = piece + pltpu.roll(piece, 64, 1)
            if quarter:
                piece = pltpu.roll(piece, 32 * quarter, 1)
            whole = jnp.where((lane >> 5) == quarter, piece, whole)
        small.append(whole)
    demod_sums, style_sums, gamma_sums, beta_sums = small[0:2], small[2:4], small[4:6], small[6:8]
    gain = gamma[...]
    group_means = group_total(gain * jnp.concatenate(beta_sums + gamma_sums, axis=0)) * (1.0 / cells)
    gamma_out[...] = scale * (gamma_sums[0] + gamma_sums[1])
    beta_out[...] = scale * (beta_sums[0] + beta_sums[1])
    shrink = jnp.zeros((channels, channels), F32)
    rows = []
    for sample in range(samples):
        demod_row = demod[sample : sample + 1, :]
        pulled = demod_sums[sample] * (demod_row * demod_row * demod_row)
        style_full = column[sample]
        shrink = shrink + style_full * style_full * pulled
        spent = jnp.sum((power[...] * pulled).T, axis=0, keepdims=True)
        rows.append(style_sums[sample] - style[sample : sample + 1, :] * spent)
    for tap in range(8):
        for part in range(4):
            here = slice(32 * part, 32 * part + 32)
            weight_out[tap, here, :] = scale * (
                main[4 * tap + part] - shrink[here, :] * weight[tap, here, :]
            )
    for pair in range(16):
        here = slice(8 * pair, 8 * pair + 8)
        block = jnp.where(sub < 4, tails[2 * pair], pltpu.roll(tails[2 * pair + 1], 4, 0))
        weight_out[8, here, :] = scale * (block - shrink[here, :] * weight[8, here, :])
    style_out[...] = scale * (emb_full[0] * rows[0] + emb_full[1] * rows[1])
    for sample in range(samples):
        inverse = stats[samples + sample : samples + sample + 1, :]
        product_mean = group_means[sample : sample + 1, :]
        squared_mean = group_means[samples + sample : samples + sample + 1, :]
        flat = mixed[sample].astype(F32).reshape(size, channels)
        norm = (flat - stats[sample : sample + 1, :]) * inverse
        change = inverse * (gain * grad_pre[sample] - product_mean - norm * squared_mean)
        out = cotangent[sample].reshape(size, channels).astype(F32) + change
        feats_out[sample] = out.astype(BF16).reshape(tile_rows, tile_cols, channels)
    forward_body(
        mixed, inner, outer, other, passed, fore_taps, stats, gamma, beta, block_out, spread, shifted
    )


def on_device(
    feats, cond, null_field, drop_flags, emb, style_weight, conv_weight, gamma, beta, cotangent
):
    samples, tile_rows, tile_cols, channels = feats.shape
    group_size = channels // GROUPS
    lat_count, lon_count = lax.axis_size(LAT), lax.axis_size(LON)
    devices_all = lat_count * lon_count
    cells_local = tile_rows * tile_cols * group_size
    cells_per_group = cells_local * devices_all
    scale_gradient = 1.0 / math.sqrt(samples * tile_rows * tile_cols * devices_all)
    taps = conv_weight.reshape(9, channels, channels)

    lon_slot, lat_slot = 8 + samples * tile_rows, 16
    rim = array((2, samples, tile_cols, channels), BF16)
    mixed, slots, inner, outer = call(
        mix_body,
        (array(feats.shape, BF16), array((lon_count, lon_slot, LANES), BF16), rim, rim),
        (
            pltpu.VMEM(feats.shape, BF16),
            pltpu.VMEM(feats.shape, BF16),
            pltpu.VMEM(null_field.shape, BF16),
            pltpu.VMEM(feats.shape, BF16),
            pltpu.VMEM(drop_flags.shape, jnp.int32),
            pltpu.SemaphoreType.DMA((2 * samples + 3,)),
        ),
        room=60,
        in_specs=[pl.BlockSpec(memory_space=pl.ANY)] * 5,
    )(feats, cond, null_field, cotangent, drop_flags)
    slots = exchange(slots, LON)
    outer, inner = swap(outer, LAT, 1, False), swap(inner, LAT, 0, False)
    wide_cot, slots = call(
        functools.partial(merge_body, cells_local),
        (
            array((samples, tile_rows, tile_cols + 2, channels)),
            array((lat_count, lat_slot, LANES), BF16),
        ),
    )(slots, cotangent)
    slots, outer, inner = lax.optimization_barrier((slots, outer, inner))
    slots = exchange(slots, LAT)
    half = samples * (tile_rows + 2)
    edges, passed = call(
        columns_body, (array((SLOT, LANES), BF16), array((-(-half // 8) * 8, LANES), BF16))
    )(mixed, inner, outer)
    passed = swap(passed, LON, 1, True)

    taps_shape = (samples, 3, 3 * channels, channels)
    gamma, beta, style, column, demod, power, emb_full, back_taps, fore_taps = call(
        weights_body,
        (
            array((1, channels)),
            array((1, channels)),
            array((samples, channels)),
            array((samples, channels, channels)),
            array((samples, channels)),
            array((channels, channels)),
            array((samples,) + style_weight.shape),
            array(taps_shape, BF16),
            array(taps_shape, BF16),
        ),
    )(emb, style_weight, gamma[None], beta[None], taps)
    spread = pltpu.VMEM((tile_rows + 2, tile_cols + 2, channels), F32)
    shifted = pltpu.VMEM(((tile_rows + 2) * tile_cols, 3 * channels), BF16)
    flat = (samples, tile_rows * tile_cols, channels)
    stats, grad_pre, payload = call(
        functools.partial(sums_body, cells_local * lon_count, cells_per_group),
        (
            array((2 * samples, LANES)),
            array(flat),
            array((SHARDS + 1, SLOT, LANES), BF16),
        ),
        (
            pltpu.VMEM((2, lat_slot, LANES), F32),
            spread,
            shifted,
            pltpu.VMEM((9 * channels, channels), F32),
        ),
    )(
        slots, mixed, edges, wide_cot, inner, outer, gamma, beta, back_taps, column, demod, taps
    )

    near_count = lax.axis_size(NEAR)
    shard = array((near_count, SLOT, LANES), BF16)
    slots, other = call(core_body, (shard, array((SLOT, LANES), BF16)))(
        lax.all_gather(payload, "c")
    )
    slots, passed = lax.optimization_barrier((slots, passed))
    summed = array((lat_count, SLOT, LANES), BF16)
    slots = call(sum_body, summed)(exchange(slots, NEAR))
    slots = call(sum_body, shard)(exchange(slots, LAT))
    payload = lax.all_gather(exchange(slots, NEAR), "c")
    grad_feats, grad_weight, grad_style, grad_gamma, grad_beta, block_out = call(
        functools.partial(last_body, scale_gradient, cells_per_group),
        (
            array(feats.shape, BF16),
            array(taps.shape),
            array(style_weight.shape),
            array((1, LANES)),
            array((1, LANES)),
            array(feats.shape, BF16),
        ),
        (spread, shifted),
    )(
        payload.reshape(SHARDS, SLOT, LANES), stats, mixed, cotangent, grad_pre, gamma, beta, style,
        column, demod, power, taps, emb_full, inner, outer, other, passed, fore_taps,
    )
    return (
        block_out,
        grad_feats,
        grad_weight.reshape(conv_weight.shape),
        grad_style,
        grad_gamma[0],
        grad_beta[0],
    )


def solution(mesh):
    parts = Mesh(mesh.devices.reshape(4, 4, 2, 8, 2), LAT + LON)
    tile = P(None, LAT, LON, None)
    placed = (tile, tile, P(LAT, LON, None), P(), P(), P(), P(), P(), P(), tile)
    return jax.shard_map(
        on_device,
        mesh=parts,
        in_specs=placed,
        out_specs=(tile, tile, P(), P(), P(), P()),
        check_vma=False,
    )
```

```python
import functools
import math

import jax
import jax.numpy as jnp
from jax import lax
from jax.experimental import pallas as pl
from jax.experimental.pallas import tpu as pltpu
from jax.sharding import Mesh, PartitionSpec as P

GROUPS = 32
LAT = ("zh", "x")
LON = ("zl", "y", "c")
NEAR = ("zl", "y")
F32 = jnp.float32
BF16 = jnp.bfloat16
TILE = 8
SHARDS = 32
SLOT = 40
LANES = 128


def swap(block, axes, first, periodic):
    count = lax.axis_size(axes)
    pairs = [(i, (i + 1) % count) for i in range(first, count, 2) if periodic or i + 1 < count]
    return lax.ppermute(block, axes, pairs + [(target, source) for source, target in pairs])


def halos(inner, outer, field, sample):
    near, far = inner[field, sample].astype(F32), outer[field, sample].astype(F32)
    even = lax.rem(place(LAT), 2) == 0
    return jnp.where(even, far, near), jnp.where(even, near, far)


def exchange(block, axes):
    return lax.all_to_all(block, axes, 0, 0)


def call(body, outputs, scratch=(), room=24, **more):
    return pl.pallas_call(
        body,
        out_shape=outputs,
        scratch_shapes=list(scratch),
        **more,
        compiler_params=pltpu.CompilerParams(vmem_limit_bytes=room * 1024 * 1024),
    )


def array(shape, dtype=F32):
    return jax.ShapeDtypeStruct(shape, dtype)


def lanes_of(rows=1):
    return lax.broadcasted_iota(jnp.int32, (rows, LANES), 1)


def group_total(row):
    lane = lanes_of()
    for step in (1, 2):
        after, before = pltpu.roll(row, LANES - step, 1), pltpu.roll(row, step, 1)
        row = row + jnp.where((lane & step) == 0, after, before)
    return row


def weave(first, second):
    return jnp.where((lanes_of() & 1) == 0, first, second)


def unweave(row, sample):
    if sample == 0:
        return weave(row, pltpu.roll(row, 1, 1))
    return weave(pltpu.roll(row, LANES - 1, 1), row)


def place(axes):
    index = 0
    for axis in axes:
        index = index * lax.axis_size(axis) + lax.axis_index(axis)
    return index


def three_terms(value):
    terms = []
    for _ in range(3):
        terms.append(value.astype(BF16).astype(F32))
        value = value - terms[-1]
    return terms


def merged(slots, count):
    rows = slots[:, 0:8, :].astype(F32)
    means = rows[:, 0:1, :] + rows[:, 1:2, :] + rows[:, 2:3, :]
    spreads = rows[:, 3:4, :] + rows[:, 4:5, :] + rows[:, 5:6, :]
    mean = jnp.mean(means, axis=0)
    away = means - mean[None]
    return mean, jnp.sum(spreads + count * away * away, axis=0)


def header(mean, spread):
    return three_terms(mean) + three_terms(spread) + [jnp.zeros((2, LANES), F32)]


def fetcher(arrivals):
    used = iter(range(arrivals.shape[0]))

    def fetch(source, target):
        copy = pltpu.make_async_copy(source, target, arrivals.at[next(used)])
        copy.start()
        return copy

    return fetch


def mix_body(
    feats_in, cond_in, null_in, cot_in, flags_in, mixed_out, slots_out, inner_out, outer_out,
    feats, cond, null, cot, flags, arrivals,
):
    fetch = fetcher(arrivals)
    flags_copy, null_copy = fetch(flags_in, flags), fetch(null_in, null)
    field_copies = [
        (fetch(feats_in.at[sample], feats.at[sample]), fetch(cond_in.at[sample], cond.at[sample]))
        for sample in range(feats.shape[0])
    ]
    cot_copy = fetch(cot_in, cot)
    flags_copy.wait()
    null_copy.wait()
    samples, tile_rows, tile_cols, channels = feats.shape
    cells = tile_rows * tile_cols
    size = cells * (channels // GROUPS)
    even = lax.rem(place(LAT), 2) == 0

    def put_rims(field, sample, top, bottom):
        top, bottom = top.astype(F32), bottom.astype(F32)
        inner_out[field, sample] = jnp.where(even, bottom, top).astype(BF16)
        outer_out[field, sample] = jnp.where(even, top, bottom).astype(BF16)

    null32 = null[...].astype(F32)
    fields, sums = [], []
    for sample in range(samples):
        for copy in field_copies[sample]:
            copy.wait()
        dropped = flags[sample : sample + 1, :].astype(F32).reshape(1, 1, channels)
        mixed = (
            feats[sample].astype(F32) + dropped * null32 + (1.0 - dropped) * cond[sample].astype(F32)
        ).astype(BF16)
        mixed_out[sample] = mixed
        put_rims(0, sample, mixed[0], mixed[tile_rows - 1])
        fields.append(mixed.astype(F32).reshape(cells, channels))
        sums.append(jnp.sum(fields[-1], axis=0, keepdims=True))
    means = group_total(jnp.concatenate(sums, axis=0)) * (1.0 / size)
    sums = []
    for sample in range(samples):
        away = fields[sample] - means[sample : sample + 1, :]
        sums.append(jnp.sum(away * away, axis=0, keepdims=True))
    spreads = group_total(jnp.concatenate(sums, axis=0))
    means, spreads = (means[0:1, :], means[1:2, :]), (spreads[0:1, :], spreads[1:2, :])
    rows = header(weave(*means), weave(*spreads))
    cot_copy.wait()
    firsts, lasts = [], []
    for sample in range(samples):
        put_rims(1, sample, cot[sample, 0], cot[sample, tile_rows - 1])
        wide = cot[sample].astype(F32)
        firsts.append(wide[:, 0, :])
        lasts.append(wide[:, tile_cols - 1, :])
    slots_out[...] = jnp.broadcast_to(
        jnp.concatenate(rows + firsts, axis=0).astype(BF16)[None], slots_out.shape
    )
    after = lax.rem(place(LON) + 1, slots_out.shape[0])
    slots_out[after] = jnp.concatenate(rows + lasts, axis=0).astype(BF16)


def merge_body(count, slots, cot, wide_out, slots_out):
    samples, tile_rows, tile_cols, channels = cot.shape
    lon_count, lat_count = slots.shape[0], slots_out.shape[0]
    mean, spread = merged(slots, count)
    me = place(LON)
    before = slots[lax.rem(me + lon_count - 1, lon_count)].astype(F32)
    after = slots[lax.rem(me + 1, lon_count)].astype(F32)
    for sample in range(samples):
        here = slice(8 + sample * tile_rows, 8 + (sample + 1) * tile_rows)
        wide_out[sample, :, 0, :] = before[here, :]
        wide_out[sample, :, 1 : 1 + tile_cols, :] = cot[sample].astype(F32)
        wide_out[sample, :, 1 + tile_cols, :] = after[here, :]
    rows = header(mean, spread)

    def slot(row):
        corners = [
            wide_out[sample, row, side : side + 1, :]
            for sample in range(samples)
            for side in (0, 1 + tile_cols)
        ]
        spare = jnp.zeros((slots_out.shape[1] - 8 - len(corners), channels), F32)
        return jnp.concatenate(rows + corners + [spare], axis=0).astype(BF16)

    slots_out[...] = jnp.broadcast_to(slot(0)[None], slots_out.shape)
    row = place(LAT)

    @pl.when(row < lat_count - 1)
    def _():
        slots_out[row + 1] = slot(tile_rows - 1)


def columns_body(mixed, inner, outer, edges_out, send_out):
    samples, _, tile_cols, channels = mixed.shape
    spare = [jnp.zeros((send_out.shape[0] - edges_out.shape[0] // 2, channels), F32)]

    def column(at):
        parts = []
        for sample in range(samples):
            low, high = halos(inner, outer, 0, sample)
            parts.append(low[at : at + 1, :])
            parts.append(mixed[sample].astype(F32)[:, at, :])
            parts.append(high[at : at + 1, :])
        return parts

    first, last = column(0), column(tile_cols - 1)
    edges_out[...] = jnp.concatenate(first + last, axis=0).astype(BF16)
    first, last = jnp.concatenate(first + spare, axis=0), jnp.concatenate(last + spare, axis=0)
    send_out[...] = jnp.where(place(("c",)) == 0, first, last).astype(BF16)


def weights_body(
    emb, style_weight, gamma, beta, weight,
    gamma_out, beta_out, style_out, column_out, demod_out, power_out, emb_out, back_out, taps_out,
):
    gamma_out[...] = gamma[...]
    beta_out[...] = beta[...]
    power = jnp.zeros(weight.shape[1:], F32)
    for tap in range(9):
        power = power + weight[tap] * weight[tap]
    samples, channels = emb.shape[0], weight.shape[2]
    exact = lax.Precision.HIGHEST
    style = 1.0 + jnp.dot(
        emb[...], style_weight[...], precision=exact, preferred_element_type=F32
    )
    squares = jnp.dot(style * style, power, precision=exact, preferred_element_type=F32)
    demod = lax.rsqrt(squares + 1e-08)
    style_out[...] = style
    demod_out[...] = demod
    power_out[...] = power
    for sample in range(samples):
        here = slice(sample, sample + 1)
        column = jnp.broadcast_to(style[here, :], (channels, channels)).T
        column_out[sample] = column
        emb_out[sample] = jnp.broadcast_to(emb[here, :], (channels, emb.shape[1])).T
        for tap in range(9):
            row, col = tap // 3, tap % 3
            block = weight[tap] * column * demod[here, :]
            taps_out[sample, row, col * channels : (col + 1) * channels, :] = block.astype(BF16)
            row, col = 2 - row, 2 - col
            back_out[sample, row, col * channels : (col + 1) * channels, :] = block.T.astype(BF16)


def windows(spread, shifted, rows, cols):
    channels = spread.shape[-1]
    for tap in range(3):
        moved = spread[:, tap : tap + cols, :].reshape((rows + 2) * cols, channels)
        shifted[:, tap * channels : (tap + 1) * channels] = moved.astype(BF16)


def forward_body(
    mixed, inner, outer, other, passed, taps, stats, gamma, beta, block_out, spread, shifted
):
    samples, rows, cols, _ = mixed.shape
    size = rows * cols
    row = lax.broadcasted_iota(jnp.int32, spread.shape, 0) + place(LAT) * rows
    inside = (row > 0) & (row <= rows * lax.axis_size(LAT))
    core = place(("c",))
    mate, away = other[...].astype(F32), passed[...].astype(F32)
    half = samples * (rows + 2)
    left = jnp.where(core == 0, away[:half, :], mate[half : 2 * half, :])
    right = jnp.where(core == 0, mate[:half, :], away[:half, :])
    for sample in range(samples):
        here = slice(sample * (rows + 2), (sample + 1) * (rows + 2))
        spread[:, 0, :] = left[here, :]
        spread[:, 1 + cols, :] = right[here, :]
        low, high = halos(inner, outer, 0, sample)
        spread[0, 1 : 1 + cols, :] = low
        spread[1 : 1 + rows, 1 : 1 + cols, :] = mixed[sample].astype(F32)
        spread[1 + rows, 1 : 1 + cols, :] = high
        mean = stats[sample : sample + 1, :][None]
        inverse = stats[samples + sample : samples + sample + 1, :][None]
        pre = (spread[...] - mean) * inverse * gamma[...][None] + beta[...][None]
        spread[...] = jnp.where(inside, pre / (1.0 + jnp.exp(-pre)), 0.0)
        windows(spread, shifted, rows, cols)
        total = mixed[sample].astype(F32).reshape(size, -1)
        for row_tap in range(3):
            window = shifted[row_tap * cols : row_tap * cols + size, :]
            total = total + jnp.dot(window, taps[sample, row_tap], preferred_element_type=F32)
        block_out[sample] = total.astype(BF16).reshape(rows, cols, -1)


def sums_body(
    count, cells, slots, mixed, edges, wide, inner, outer, gamma, beta, back_taps, column, demod,
    weight, stats_out, grad_out, payload_out, edge, spread, shifted, total,
):
    samples, rows, cols, channels = mixed.shape
    size = rows * cols
    mean_all, spread_all = merged(slots, count)
    inverse_all = lax.rsqrt(spread_all * (1.0 / cells) + 1e-05)
    lat_count, row = slots.shape[0], place(LAT)
    below = slots[lax.max(row - 1, 0)].astype(F32)
    above = slots[lax.min(row + 1, lat_count - 1)].astype(F32)
    edge[0] = jnp.where(row > 0, below, 0.0)
    edge[1] = jnp.where(row < lat_count - 1, above, 0.0)
    sums = [[], [], [], []]
    for sample in range(samples):
        mean, inverse = unweave(mean_all, sample), unweave(inverse_all, sample)
        stats_out[sample : sample + 1, :] = mean
        stats_out[samples + sample : samples + sample + 1, :] = inverse
        flat = mixed[sample].reshape(size, channels).astype(F32)
        norm = (flat - mean) * inverse
        pre = norm * gamma[...] + beta[...]
        sig = 1.0 / (1.0 + jnp.exp(-pre))
        act = (pre * sig).astype(BF16)
        slope = sig * (1.0 + pre * (1.0 - sig))
        spread[1 : 1 + rows] = wide[sample]
        low, high = halos(inner, outer, 1, sample)
        for at, halo, corner in ((0, low, edge[0]), (1 + rows, high, edge[1])):
            spread[at, 1 : 1 + cols, :] = halo
            start = 8 + 2 * sample
            spread[at, 0:1, :] = corner[start : start + 1, :]
            spread[at, 1 + cols : 2 + cols, :] = corner[start + 1 : start + 2, :]
        windows(spread, shifted, rows, cols)
        style_full = column[sample]
        demod_row = demod[sample : sample + 1, :]
        both = style_full * demod_row
        product = jnp.zeros((channels, channels), F32)
        grad_act = jnp.zeros((size, channels), F32)
        for row_tap in range(3):
            window = shifted[row_tap * cols : row_tap * cols + size, :]
            grad_act = grad_act + jnp.dot(
                window, back_taps[sample, row_tap], preferred_element_type=F32
            )
            grad = lax.dot_general(
                act, window, (((0,), (0,)), ((), ())), preferred_element_type=F32
            )
            for col_tap in range(3):
                tap = (2 - row_tap) * 3 + 2 - col_tap
                block = grad[:, col_tap * channels : (col_tap + 1) * channels]
                product = product + block * weight[tap]
                here = slice(tap * channels, (tap + 1) * channels)
                part = block * both
                total[here, :] = part if sample == 0 else total[here, :] + part
        grad_pre = grad_act * slope
        grad_out[sample] = grad_pre
        sums[0].append(jnp.sum(product * style_full, axis=0, keepdims=True))
        sums[1].append(jnp.sum((product * demod_row).T, axis=0, keepdims=True))
        sums[2].append(jnp.sum(grad_pre * norm, axis=0, keepdims=True))
        sums[3].append(jnp.sum(grad_pre, axis=0, keepdims=True))
    payload_out[SHARDS] = edges[...]
    small = jnp.concatenate(sum(sums, []), axis=0)
    lane = lanes_of(TILE)
    sub = lax.broadcasted_iota(jnp.int32, (TILE, channels), 0)
    quarters = []
    for quarter in range(4):
        turned = pltpu.roll(small, LANES - 32 * quarter, 1) if quarter else small
        piece = jnp.where(lane < 64, turned, pltpu.roll(turned, 64, 1))
        piece = jnp.where((lane & 32) == 0, piece, 0.0)
        quarters.append(split_terms(piece, lane))
    for shard in range(SHARDS):
        main = total[32 * shard : 32 * shard + 32, :]
        start = 8 * channels + 8 * (shard // 2)
        last = total[start : start + 8, :]
        if shard % 2:
            last = pltpu.roll(last, 4, 0)
        extra = quarters[shard % 4][shard // 4 : shard // 4 + 1, :]
        tail = jnp.where(sub < 4, last, jnp.where(sub == 4, extra, 0.0))
        payload_out[shard] = jnp.concatenate([main, tail], axis=0).astype(BF16)


def split_terms(values, lane):
    high = values.astype(BF16).astype(F32)
    return jnp.where(lane < 64, high, values - high)


def resplit(slots):
    main, tail = slots[:, 0:32, :], slots[:, 32:SLOT, :]
    flat = tail.reshape(-1, LANES)
    lane = lax.broadcasted_iota(jnp.int32, flat.shape, 1)
    row = lax.broadcasted_iota(jnp.int32, flat.shape, 0) & 7
    terms = split_terms(flat + pltpu.roll(flat, 64, 1), lane)
    tail = jnp.where(row == 4, terms, flat).reshape(tail.shape)
    return jnp.concatenate([main, tail], axis=1)


def core_body(gathered, slots_out, other_out):
    core, near_count = place(("c",)), slots_out.shape[0]
    mine = pl.ds(core * near_count, near_count)
    total = gathered[0, mine].astype(F32) + gathered[1, mine].astype(F32)
    other_out[...] = gathered[1 - core, SHARDS]
    slots_out[...] = resplit(total).astype(BF16)


def sum_body(slots, slots_out):
    total = jnp.sum(slots[...].astype(F32), axis=0)
    slots_out[...] = jnp.broadcast_to(resplit(total[None]).astype(BF16), slots_out.shape)


def last_body(
    scale, cells, gathered, stats, mixed, cotangent, grad_pre, gamma, beta, style, column, demod,
    power, weight, emb_full, inner, outer, other, passed, fore_taps,
    feats_far, weight_far, style_far, gamma_out, beta_out, block_out,
    spread, shifted, feats_out, weight_out, style_out, arrivals,
):
    samples, tile_rows, tile_cols, channels = cotangent.shape
    size = tile_rows * tile_cols
    lane = lanes_of()
    sub = lax.broadcasted_iota(jnp.int32, (TILE, channels), 0)
    main, tails, small = [], [], []
    for shard in range(SHARDS):
        slot = gathered[shard].astype(F32)
        main.append(slot[0:32, :])
        tails.append(slot[32:40, :])
    for row in range(TILE):
        whole = jnp.zeros((1, channels), F32)
        for quarter in range(4):
            piece = tails[4 * row + quarter][4:5, :]
            piece = piece + pltpu.roll(piece, 64, 1)
            if quarter:
                piece = pltpu.roll(piece, 32 * quarter, 1)
            whole = jnp.where((lane >> 5) == quarter, piece, whole)
        small.append(whole)
    demod_sums, style_sums, gamma_sums, beta_sums = small[0:2], small[2:4], small[4:6], small[6:8]
    gain = gamma[...]
    group_means = group_total(gain * jnp.concatenate(beta_sums + gamma_sums, axis=0)) * (1.0 / cells)
    gamma_out[...] = scale * (gamma_sums[0] + gamma_sums[1])
    beta_out[...] = scale * (beta_sums[0] + beta_sums[1])
    shrink = jnp.zeros((channels, channels), F32)
    rows = []
    for sample in range(samples):
        demod_row = demod[sample : sample + 1, :]
        pulled = demod_sums[sample] * (demod_row * demod_row * demod_row)
        style_full = column[sample]
        shrink = shrink + style_full * style_full * pulled
        spent = jnp.sum((power[...] * pulled).T, axis=0, keepdims=True)
        rows.append(style_sums[sample] - style[sample : sample + 1, :] * spent)
    for tap in range(8):
        for part in range(4):
            here = slice(32 * part, 32 * part + 32)
            weight_out[tap, here, :] = scale * (
                main[4 * tap + part] - shrink[here, :] * weight[tap, here, :]
            )
    for pair in range(16):
        here = slice(8 * pair, 8 * pair + 8)
        block = jnp.where(sub < 4, tails[2 * pair], pltpu.roll(tails[2 * pair + 1], 4, 0))
        weight_out[8, here, :] = scale * (block - shrink[here, :] * weight[8, here, :])
    fetch = fetcher(arrivals)
    copies = [fetch(weight_out, weight_far)]
    style_out[...] = scale * (emb_full[0] * rows[0] + emb_full[1] * rows[1])
    copies.append(fetch(style_out, style_far))
    for sample in range(samples):
        inverse = stats[samples + sample : samples + sample + 1, :]
        product_mean = group_means[sample : sample + 1, :]
        squared_mean = group_means[samples + sample : samples + sample + 1, :]
        flat = mixed[sample].astype(F32).reshape(size, channels)
        norm = (flat - stats[sample : sample + 1, :]) * inverse
        change = inverse * (gain * grad_pre[sample] - product_mean - norm * squared_mean)
        out = cotangent[sample].reshape(size, channels).astype(F32) + change
        feats_out[sample] = out.astype(BF16).reshape(tile_rows, tile_cols, channels)
    copies.append(fetch(feats_out, feats_far))
    forward_body(
        mixed, inner, outer, other, passed, fore_taps, stats, gamma, beta, block_out, spread, shifted
    )
    for copy in copies:
        copy.wait()


def on_device(
    feats, cond, null_field, drop_flags, emb, style_weight, conv_weight, gamma, beta, cotangent
):
    samples, tile_rows, tile_cols, channels = feats.shape
    group_size = channels // GROUPS
    lat_count, lon_count = lax.axis_size(LAT), lax.axis_size(LON)
    devices_all = lat_count * lon_count
    cells_local = tile_rows * tile_cols * group_size
    cells_per_group = cells_local * devices_all
    scale_gradient = 1.0 / math.sqrt(samples * tile_rows * tile_cols * devices_all)
    taps = conv_weight.reshape(9, channels, channels)

    lon_slot, lat_slot = 8 + samples * tile_rows, 16
    rim = array((2, samples, tile_cols, channels), BF16)
    mixed, slots, inner, outer = call(
        mix_body,
        (array(feats.shape, BF16), array((lon_count, lon_slot, LANES), BF16), rim, rim),
        (
            pltpu.VMEM(feats.shape, BF16),
            pltpu.VMEM(feats.shape, BF16),
            pltpu.VMEM(null_field.shape, BF16),
            pltpu.VMEM(feats.shape, BF16),
            pltpu.VMEM(drop_flags.shape, jnp.int32),
            pltpu.SemaphoreType.DMA((2 * samples + 3,)),
        ),
        room=60,
        in_specs=[pl.BlockSpec(memory_space=pl.ANY)] * 5,
    )(feats, cond, null_field, cotangent, drop_flags)
    slots = exchange(slots, LON)
    outer, inner = swap(outer, LAT, 1, False), swap(inner, LAT, 0, False)
    wide_cot, slots = call(
        functools.partial(merge_body, cells_local),
        (
            array((samples, tile_rows, tile_cols + 2, channels)),
            array((lat_count, lat_slot, LANES), BF16),
        ),
    )(slots, cotangent)
    slots, outer, inner = lax.optimization_barrier((slots, outer, inner))
    slots = exchange(slots, LAT)
    half = samples * (tile_rows + 2)
    edges, passed = call(
        columns_body, (array((SLOT, LANES), BF16), array((-(-half // 8) * 8, LANES), BF16))
    )(mixed, inner, outer)
    passed = swap(passed, LON, 1, True)

    taps_shape = (samples, 3, 3 * channels, channels)
    gamma, beta, style, column, demod, power, emb_full, back_taps, fore_taps = call(
        weights_body,
        (
            array((1, channels)),
            array((1, channels)),
            array((samples, channels)),
            array((samples, channels, channels)),
            array((samples, channels)),
            array((channels, channels)),
            array((samples,) + style_weight.shape),
            array(taps_shape, BF16),
            array(taps_shape, BF16),
        ),
    )(emb, style_weight, gamma[None], beta[None], taps)
    spread = pltpu.VMEM((tile_rows + 2, tile_cols + 2, channels), F32)
    shifted = pltpu.VMEM(((tile_rows + 2) * tile_cols, 3 * channels), BF16)
    flat = (samples, tile_rows * tile_cols, channels)
    stats, grad_pre, payload = call(
        functools.partial(sums_body, cells_local * lon_count, cells_per_group),
        (
            array((2 * samples, LANES)),
            array(flat),
            array((SHARDS + 1, SLOT, LANES), BF16),
        ),
        (
            pltpu.VMEM((2, lat_slot, LANES), F32),
            spread,
            shifted,
            pltpu.VMEM((9 * channels, channels), F32),
        ),
    )(
        slots, mixed, edges, wide_cot, inner, outer, gamma, beta, back_taps, column, demod, taps
    )

    near_count = lax.axis_size(NEAR)
    shard = array((near_count, SLOT, LANES), BF16)
    slots, other = call(core_body, (shard, array((SLOT, LANES), BF16)))(
        lax.all_gather(payload, "c")
    )
    slots, passed = lax.optimization_barrier((slots, passed))
    summed = array((lat_count, SLOT, LANES), BF16)
    slots = call(sum_body, summed)(exchange(slots, NEAR))
    slots = call(sum_body, shard)(exchange(slots, LAT))
    payload = lax.all_gather(exchange(slots, NEAR), "c")
    grad_feats, grad_weight, grad_style, grad_gamma, grad_beta, block_out = call(
        functools.partial(last_body, scale_gradient, cells_per_group),
        (
            array(feats.shape, BF16),
            array(taps.shape),
            array(style_weight.shape),
            array((1, LANES)),
            array((1, LANES)),
            array(feats.shape, BF16),
        ),
        (
            spread,
            shifted,
            pltpu.VMEM(feats.shape, BF16),
            pltpu.VMEM(taps.shape, F32),
            pltpu.VMEM(style_weight.shape, F32),
            pltpu.SemaphoreType.DMA((3,)),
        ),
        out_specs=[pl.BlockSpec(memory_space=pl.ANY)] * 3
        + [pl.BlockSpec(memory_space=pltpu.VMEM)] * 3,
    )(
        payload.reshape(SHARDS, SLOT, LANES), stats, mixed, cotangent, grad_pre, gamma, beta, style,
        column, demod, power, taps, emb_full, inner, outer, other, passed, fore_taps,
    )
    return (
        block_out,
        grad_feats,
        grad_weight.reshape(conv_weight.shape),
        grad_style,
        grad_gamma[0],
        grad_beta[0],
    )


def solution(mesh):
    parts = Mesh(mesh.devices.reshape(4, 4, 2, 8, 2), LAT + LON)
    tile = P(None, LAT, LON, None)
    placed = (tile, tile, P(LAT, LON, None), P(), P(), P(), P(), P(), P(), tile)
    return jax.shard_map(
        on_device,
        mesh=parts,
        in_specs=placed,
        out_specs=(tile, tile, P(), P(), P(), P()),
        check_vma=False,
    )
```
